32 devices in a mesh: comp: 4 (over z), tile: 8 (over y, x, core).
Axes of the slice: x: 2, y: 2, z: 4, core: 2. Of those that a mesh axis runs over, the one named last changes fastest.
Arguments:
- state: float32 [4, 16, 32, 3072], P('comp', None, 'tile'), may hold values from -6 to 6
- coupling: float32 [4, 32, 3072], P('comp', 'tile'), may hold values from -6 to 6
- land_mask: int32 [4, 32, 3072], P('comp', 'tile'), may hold values 0 or 1
- codes: int32 [4, 32, 3072], P('comp', 'tile'), may hold values from 0 to 3
- mixing: float32 [4, 16], P('comp'), may hold values from 0.1 to 0.19
- courant: float32 [4, 16], P('comp'), may hold values from 0.05 to 0.24
- matrices: float32 [4, 4, 16, 16], P('comp'), may hold values from -1.5 to 1.5
- weights: bfloat16 [4, 2304, 8, 128], P('comp', 'tile'), may hold values from 0 to 0.25
- sources: int32 [4, 2304], P('comp', 'tile'), may hold values from 0 to 95, as said below
- targets: int32 [4, 2304], P('comp', 'tile'), may hold values from 0 to 383, as said below
Outputs:
- new_state: float32 [4, 16, 32, 3072], P('comp', None, 'tile')
- new_coupling: float32 [4, 32, 3072], P('comp', 'tile')
The draws below stay inside these ranges and needn't reach their ends.
Inputs may be any that keep to these rules, and one draw needn't show every extreme that they name: `sources`: on every tile each of its 96 blocks is the source of exactly 3 of its margin blocks. An atmosphere tile of group a targets only blocks of group 3 * 4 / 4 + a // 3, each of them exactly 3 times; an ocean tile of group o targets every block of the groups 3 (o - 3 * 4 / 4) + j, j < 3, exactly once.
All inputs are finite; a program needn't handle non-finite values. No bound on the sum of `land_mask` on one device may be relied on, other than what follows from the above.
Results may differ from the reference program's by a relative error of at most 0.0011.
Values sent between devices are 32-bit elements; how exact they have to be, the bound alone decides.
No kernel may reach another device: no remote copies, remote signals or barrier semaphores. Data moves between devices by JAX's collectives and lax.ppermute only.
A program may use at most 64 MiB of HBM per device.

```python
import jax
import jax.numpy as jnp
from jax import lax

RA = 4
W = 3072
BLOCK = 128
BAND = 8
SUBSTEPS = 2
INTERVALS = 2
BRANCHES = 4
NV = 16
MARGINS = 288
ROWS = 32
N_COMP = 4
N_TILE = 8


def margin_pairs(key):
    blocks_dev = RA * W // BLOCK
    span = 3 * blocks_dev
    air_count = 3 * N_COMP // 4
    keys = jax.random.split(key, N_COMP * N_TILE)
    owners = jnp.arange(N_COMP * N_TILE, dtype=jnp.int32) // N_TILE

    def one_tile(tile_key, group):
        first_key, second_key = jax.random.split(tile_key)
        base = jnp.arange(span, dtype=jnp.int32) % blocks_dev
        source_list = jax.random.permutation(first_key, base).astype(jnp.int32)
        shuffled = jax.random.permutation(second_key, span).astype(jnp.int32)
        air_target = (air_count + group // 3) * blocks_dev + shuffled % blocks_dev
        sea_target = (3 * (group - air_count) + shuffled // blocks_dev) * blocks_dev + shuffled % blocks_dev
        target_list = jnp.where(group < air_count, air_target, sea_target).astype(jnp.int32)
        return (source_list, target_list)
    source_all, target_all = jax.vmap(one_tile)(keys, owners)
    return (source_all.reshape(N_COMP, N_TILE * span), target_all.reshape(N_COMP, N_TILE * span))


def draw_sources(key, part):
    return margin_pairs(jax.random.fold_in(key, 7))[0]


def draw_targets(key, part):
    return margin_pairs(jax.random.fold_in(key, 7))[1]


def touch_ends(entries, key, least, top_value):
    extent = entries.shape
    place = [jax.random.randint(jax.random.fold_in(key, axis), (), 0, extent[axis]) for axis in range(len(extent))]
    entries = entries.at[tuple(place)].set(least)
    longest = extent.index(max(extent))
    place[longest] = (place[longest] + 1) % extent[longest]
    return entries.at[tuple(place)].set(top_value)


def level_of(rng, shape, shards, low, high):
    gain, own = 1.0, jax.random.fold_in(rng, 6)
    for position, shards_of in shards:
        heights = jnp.exp(jax.random.uniform(jax.random.fold_in(own, position), (shards_of,), jnp.float32, low / len(shards), high / len(shards)))
        gain = gain * jnp.repeat(heights, shape[position] // shards_of).reshape([-1 if axis == position else 1 for axis in range(len(shape))])
    return gain


def noise(rng, extent, spread, limit, cuts=(), held_as=jnp.bfloat16):
    factor_of = level_of(rng, extent, cuts, -0.22, 0.18) if cuts else 1.0
    values = jax.random.normal(rng, extent, jnp.float32) * spread * factor_of
    return jnp.minimum(jnp.maximum(values, -limit), limit).astype(held_as)


def setup_inputs(seed: int = 0) -> dict:
    seeds = jax.random.split(jax.random.key(seed), 11)
    state = noise(seeds[0], (N_COMP, NV, ROWS, W), 1.0, 6.0, ((0, 4), (2, 8)), jnp.float32)
    coupling = noise(seeds[1], (N_COMP, ROWS, W), 1.0, 6.0, ((0, 4), (1, 8)), jnp.float32)
    land_mask = touch_ends((jax.random.randint(seeds[2], (N_COMP, ROWS, W), 0, 4) < 3).astype(jnp.int32), jax.random.fold_in(seeds[2], 1), 0, 1)
    codes = touch_ends(jax.random.randint(seeds[3], (N_COMP, ROWS, W), 0, BRANCHES), jax.random.fold_in(seeds[3], 1), 0, BRANCHES - 1).astype(jnp.int32)
    mixing = jnp.clip(0.1 + 0.089999996 * jax.random.uniform(seeds[4], (N_COMP, NV), jnp.float32) ** level_of(seeds[4], (N_COMP, NV), ((0, 4),), -0.2, 0.2), 0.1, 0.19)
    courant = jnp.clip(0.05 + 0.19 * jax.random.uniform(seeds[5], (N_COMP, NV), jnp.float32) ** level_of(seeds[5], (N_COMP, NV), ((0, 4),), -0.2, 0.2), 0.05, 0.24)
    matrices = noise(seeds[6], (N_COMP, BRANCHES, NV, NV), 0.3, 1.5, ((0, 4),), jnp.float32)
    weights = jnp.clip(0.25 * jax.random.uniform(seeds[7], (N_COMP, N_TILE * MARGINS, BAND, BLOCK), jnp.float32) ** level_of(seeds[7], (N_COMP, N_TILE * MARGINS, BAND, BLOCK), ((0, 4), (1, 8)), -0.2, 0.2), 0.0, 0.25).astype(jnp.bfloat16)
    sources = draw_sources(jax.random.fold_in(seeds[10], 71), 0)
    targets = draw_targets(jax.random.fold_in(seeds[10], 71), 0)
    return dict(state=state, coupling=coupling, land_mask=land_mask, codes=codes, mixing=mixing, courant=courant, matrices=matrices, weights=weights, sources=sources, targets=targets)


EXCHANGE = 0.5
OCEAN_SHARE = 0.3


def remap_all(handed, weights, sources, targets):
    blocks_dev = RA * W // BLOCK
    slot_count = N_COMP * blocks_dev
    blocks = handed.reshape(N_COMP, N_TILE, blocks_dev, BLOCK).astype(jnp.bfloat16)
    group_weights = weights.reshape(N_COMP, N_TILE, MARGINS, BAND, BLOCK)
    group_sources = sources.reshape(N_COMP, N_TILE, MARGINS)
    group_targets = targets.reshape(N_COMP, N_TILE, MARGINS)

    def one_group(pieces):
        tile_blocks, tile_weights, tile_sources, tile_targets = pieces
        rows_index = jnp.arange(N_TILE, dtype=jnp.int32)[:, None]
        picked = tile_blocks[rows_index, tile_sources].astype(jnp.float32)
        shifted = jnp.stack([jnp.roll(picked, -offset, axis=2) for offset in range(BAND)], axis=2)
        contrib = jnp.sum(tile_weights.astype(jnp.float32) * shifted, axis=2)
        selector = (tile_targets[:, :, None] == jnp.arange(slot_count, dtype=jnp.int32)[None, None, :]).astype(jnp.float32)
        return jnp.einsum("pks,pki->psi", selector, contrib, precision=lax.Precision.HIGHEST)

    payload = lax.map(one_group, (blocks, group_weights, group_sources, group_targets))
    payload = payload.reshape(N_COMP, N_TILE, N_COMP, blocks_dev * BLOCK)
    received = jnp.sum(payload, axis=0)
    return jnp.transpose(received, (1, 0, 2)).reshape(N_COMP, N_TILE * RA, W)


def reference(state, coupling, land_mask, codes, mixing, courant, matrices, weights, sources, targets):
    air_group = jnp.arange(N_COMP, dtype=jnp.int32) < 3 * N_COMP // 4
    wet_cells = land_mask.astype(jnp.float32)
    mixing_rate = mixing[:, :, None, None]
    courant_rate = courant[:, :, None, None]
    evolved = state
    handed = coupling
    for interval in range(INTERVALS):
        received = remap_all(handed, weights, sources, targets)
        surface = evolved[:, 0]
        surface_flux = wet_cells * EXCHANGE * (received - surface)
        new_surface = jnp.where(air_group[:, None, None], surface + surface_flux, surface - OCEAN_SHARE * received)
        diffused = evolved.at[:, 0].set(new_surface)
        for substep in range(SUBSTEPS):
            row_above = jnp.roll(diffused, 1, axis=2)
            row_below = jnp.roll(diffused, -1, axis=2)
            col_left = jnp.roll(diffused, 1, axis=3)
            col_right = jnp.roll(diffused, -1, axis=3)
            diffused = diffused + mixing_rate * (row_above + row_below + col_left + col_right - 4.0 * diffused) + courant_rate * (row_above - diffused)
        squashed = jnp.tanh(diffused)
        tendency = jnp.zeros_like(diffused)
        for branch in range(BRANCHES):
            branch_term = jnp.einsum("cij,cjrw->cirw", matrices[:, branch], squashed, precision=lax.Precision.HIGHEST)
            tendency = tendency + jnp.where(codes[:, None] == branch, branch_term, jnp.float32(0.0))
        evolved = diffused + tendency
        evolved = jnp.where(air_group[:, None, None, None], evolved, evolved * wet_cells[:, None])
        handed = jnp.where(air_group[:, None, None], surface_flux, evolved[:, 0])
    return evolved, handed
```

```python
import functools

import jax
import jax.numpy as jnp
from jax import lax
from jax.experimental import pallas as pl
from jax.experimental.pallas import tpu as pltpu
from jax.sharding import PartitionSpec as P

SUBSTEPS = 2
INTERVALS = 2
EXCHANGE = 0.5
OCEAN_SHARE = 0.3

F32 = jnp.float32
BF16 = jnp.bfloat16
VMEM = pl.BlockSpec(memory_space=pltpu.VMEM)
PARAMS = pltpu.CompilerParams(vmem_limit_bytes=40 * 1024 * 1024)


def partner_offsets(groups):
    air_count = 3 * groups // 4
    upward = [(air_count + member // 3 - member) % groups for member in range(air_count)]
    downward = [
        (3 * member + offset - air_count - member) % groups
        for member in range(groups - air_count)
        for offset in range(3)
    ]
    return sorted(set(upward + downward))


def ring_pairs(count, steps):
    return [(source, (source + steps) % count) for source in range(count)]


def inner_pairs(count):
    return [(tile, tile ^ 1) for tile in range(count)]


def outer_pairs(count):
    return [(tile, (tile + 1) % count if tile % 2 else (tile - 1) % count) for tile in range(count)]


def split_high_low(value):
    high = value.astype(BF16)
    low = (value - high.astype(F32)).astype(BF16)
    return high, low


def remap(handed, w_ref, src_ref, tgt_ref, out_refs, offsets, groups, blk_ref, wide_ref):
    rows, width = handed.shape
    block = w_ref.shape[-1]
    per_row = width // block
    count = rows * per_row
    margins, band = w_ref.shape[1], w_ref.shape[2]
    for c in range(per_row):
        blk_ref[pl.ds(c, rows, stride=per_row), :] = handed[:, c * block : (c + 1) * block]
    blocks = blk_ref[...].astype(BF16)
    pick = (lax.broadcasted_iota(jnp.int32, (count, margins), 0) == src_ref[...]).astype(F32).astype(BF16)
    picked = lax.dot_general(pick, blocks, (((0,), (0,)), ((), ())), preferred_element_type=F32)
    wide_ref[...] = w_ref[0].reshape(margins * band, block).astype(F32)
    contrib = wide_ref[pl.ds(0, margins, stride=band), :] * picked
    for j in range(1, band):
        turned = pltpu.roll(picked, block - j, 1)
        contrib = contrib + wide_ref[pl.ds(j, margins, stride=band), :] * turned
    high, low = split_high_low(contrib)
    both = jnp.concatenate([high, low], axis=0)
    me = lax.axis_index("comp")
    slot = lax.broadcasted_iota(jnp.int32, (count, margins), 0)
    targets = tgt_ref[...]
    for out_ref, offset in zip(out_refs, offsets):
        base = lax.rem(me + offset, groups) * count
        chosen = (targets == slot + base).astype(F32).astype(BF16)
        out_ref[...] = jnp.dot(
            jnp.concatenate([chosen, chosen], axis=1), both, preferred_element_type=F32
        )


def open_kernel(offsets, groups, state, coupling, w, src, tgt, x1, x2, *rest):
    outs, (blk, wide) = rest[: len(offsets)], rest[len(offsets) :]
    odd = lax.rem(lax.axis_index("tile"), 2) == 1
    half = x1.shape[0]
    for i in range(half):
        head, tail = state[0, :, i, :], state[0, :, half + i, :]
        x1[i] = jnp.where(odd, head, tail)
        x2[i] = jnp.where(odd, tail, head)
    remap(coupling[0], w, src, tgt, outs, offsets, groups, blk, wide)


def surface_kernel(groups, n_rec, *refs):
    recs, (surface_ref, mask_ref, ns_ref, flux_ref, d1, d2, blk) = refs[:n_rec], refs[n_rec:]
    odd = lax.rem(lax.axis_index("tile"), 2) == 1
    air = lax.axis_index("comp") < 3 * groups // 4
    rows, width = ns_ref.shape
    block = blk.shape[-1]
    per_row = width // block
    total = recs[0][...]
    for rec in recs[1:]:
        total = total + rec[...]
    blk[...] = total
    received = jnp.concatenate(
        [blk[pl.ds(c, rows, stride=per_row), :] for c in range(per_row)], axis=1
    )
    surface = surface_ref[...].reshape(rows, width)
    flux = mask_ref[0].astype(F32) * EXCHANGE * (received - surface)
    new = surface + jnp.where(air, flux, -OCEAN_SHARE * received)
    ns_ref[...] = new
    flux_ref[...] = flux
    half = rows // 2
    head, tail = new[:half], new[half:]
    d1[...] = jnp.where(odd, head, tail)
    d2[...] = jnp.where(odd, tail, head)


def substep(f, up, down, c0, cu, m):
    width = f.shape[1]
    sides = pltpu.roll(f, 1, 1) + pltpu.roll(f, width - 1, 1)
    return c0 * f + cu * up + m * (down + sides)


def fields_kernel(x1, x2, y1, y2, coef, table, codes, part, grid_ref):
    odd = lax.rem(lax.axis_index("tile"), 2) == 1
    half, fields, width = x1.shape
    c0, cu, m = coef[0], coef[1], coef[2]
    branches = table.shape[0] // fields

    def row(i):
        group, at = divmod(i, half)
        first, second = ((y2, y1), (x2, x1), (x1, x2), (y1, y2))[group]
        return jnp.where(odd, second[at], first[at])

    above, here = row(0), row(1)
    for i in range(1, 4 * half - 1):
        below = row(i + 1)
        grid_ref[i - 1] = substep(here, above, below, c0, cu, m)
        above, here = here, below
    keep = lax.broadcasted_iota(jnp.int32, (fields, width), 0) > 0
    for r in range(2 * half):
        f = substep(grid_ref[r + 1], grid_ref[r], grid_ref[r + 2], c0, cu, m)
        high, low = split_high_low(jnp.tanh(f))
        terms = jnp.dot(
            table[...], jnp.concatenate([high, low, high], axis=0), preferred_element_type=F32
        )
        code = codes[0, r : r + 1, :]
        tendency = terms[:fields]
        for b in range(1, branches):
            tendency = jnp.where(code == b, terms[b * fields : (b + 1) * fields], tendency)
        part[r] = jnp.where(keep, f, 0.0) + tendency


def field0(ns, e1, e2, coef0, odd):
    half = e1.shape[0]
    first, last = e1[...], e2[...]
    f = jnp.concatenate(
        [jnp.where(odd, first, last), ns[...], jnp.where(odd, last, first)], axis=0
    )
    rows = f.shape[0]
    for _ in range(SUBSTEPS):
        f = substep(f, pltpu.roll(f, 1, 0), pltpu.roll(f, rows - 1, 0), coef0[0], coef0[1], coef0[2])
    return f[half : rows - half]


def evolve_rows(part, f0, codes, col0, mask, sea):
    rows, fields, width = part.shape
    branches = col0.shape[0]
    squashed = jnp.tanh(f0)
    top = lax.broadcasted_iota(jnp.int32, (fields, width), 0) == 0
    done = []
    for r in range(rows):
        code = codes[0, r : r + 1, :]
        gain = jnp.broadcast_to(col0[0], (fields, width))
        for b in range(1, branches):
            gain = jnp.where(code == b, col0[b], gain)
        value = part[r] + gain * squashed[r : r + 1, :] + jnp.where(top, f0[r : r + 1, :], 0.0)
        wet = jnp.where(sea, mask[0, r : r + 1, :].astype(F32), 1.0)
        done.append(value * wet)
    return done


def middle_kernel(
    offsets, groups, part, ns, flux, e1, e2, coef0, codes, col0, mask, w, src, tgt, x1, x2, surf, *rest
):
    outs, (blk, wide) = rest[: len(offsets)], rest[len(offsets) :]
    odd = lax.rem(lax.axis_index("tile"), 2) == 1
    sea = lax.axis_index("comp") >= 3 * groups // 4
    f0 = field0(ns, e1, e2, coef0, odd)
    rows = evolve_rows(part, f0, codes, col0, mask, sea)
    half = x1.shape[0]
    for i in range(half):
        x1[i] = jnp.where(odd, rows[i], rows[half + i])
        x2[i] = jnp.where(odd, rows[half + i], rows[i])
    for r, value in enumerate(rows):
        surf[r : r + 1, :] = value[:1]
    handed = jnp.where(sea, surf[...], flux[...])
    remap(handed, w, src, tgt, outs, offsets, groups, blk, wide)


def close_kernel(groups, part, ns, flux, e1, e2, coef0, codes, col0, mask, new_state, new_coupling):
    odd = lax.rem(lax.axis_index("tile"), 2) == 1
    sea = lax.axis_index("comp") >= 3 * groups // 4
    f0 = field0(ns, e1, e2, coef0, odd)
    rows = evolve_rows(part, f0, codes, col0, mask, sea)
    for r, value in enumerate(rows):
        new_state[0, :, r, :] = value
        new_coupling[0, r : r + 1, :] = jnp.where(sea, value[:1], flux[r : r + 1, :])


def call(kernel, name, outs, args, scratch=(), in_specs=None, flops=0, grid=()):
    moved = sum(a.size * a.dtype.itemsize for a in list(args) + list(outs))
    return pl.pallas_call(
        kernel,
        name=name,
        grid=grid,
        out_shape=outs,
        in_specs=in_specs or [VMEM] * len(args),
        out_specs=[VMEM] * len(outs),
        scratch_shapes=list(scratch),
        compiler_params=PARAMS,
        cost_estimate=pl.CostEstimate(flops=flops, bytes_accessed=moved, transcendentals=0),
    )(*args)


def on_device(
    state, coupling, land_mask, codes, mixing, courant, matrices, weights, sources, targets
):
    groups = lax.axis_size("comp")
    tiles = lax.axis_size("tile")
    offsets = partner_offsets(groups)
    _, fields, rows, width = state.shape
    _, margins, band, block = weights.shape
    count = rows * width // block
    half = rows // 2
    branches = matrices.shape[1]
    shape = jax.ShapeDtypeStruct

    m, c = mixing[0][:, None], courant[0][:, None]
    coef = jnp.stack([1.0 - 4.0 * m - c, m + c, m])
    coef0 = coef[:, :1]
    flat = matrices[0].reshape(branches * fields, fields)
    col0 = matrices[0][:, :, :1]
    flat = jnp.where(jnp.arange(fields)[None] == 0, 0.0, flat)
    high = lax.reduce_precision(flat, 8, 7)
    table = jnp.concatenate([high, high, flat - high], axis=1).astype(BF16)

    halves = [shape((half, fields, width), F32)] * 2
    payloads = [shape((count, block), F32)] * len(offsets)
    remap_scratch = [pltpu.VMEM((count, block), F32), pltpu.VMEM((margins * band, block), F32)]
    x1, x2, *sent = call(
        functools.partial(open_kernel, offsets, groups),
        "open",
        halves + payloads,
        (state, coupling, weights, sources, targets),
        remap_scratch,
    )
    surface, surface_spec = state, pl.BlockSpec((1, 1, rows, width), lambda i: (0, 0, 0, 0))
    for interval in range(INTERVALS):
        y2 = lax.ppermute(x2, "tile", outer_pairs(tiles))
        y1 = lax.ppermute(x1, "tile", inner_pairs(tiles))
        recs = [
            lax.ppermute(value, "comp", ring_pairs(groups, offset))
            for value, offset in zip(sent, offsets)
        ]
        ns, flux, d1, d2 = call(
            functools.partial(surface_kernel, groups, len(recs)),
            "surface",
            [shape((rows, width), F32)] * 2 + [shape((half, width), F32)] * 2,
            (*recs, surface, land_mask),
            [pltpu.VMEM((count, block), F32)],
            [VMEM] * len(recs) + [surface_spec, VMEM],
            grid=(1,),
        )
        e2 = lax.ppermute(d2, "tile", outer_pairs(tiles))
        e1 = lax.ppermute(d1, "tile", inner_pairs(tiles))
        (part,) = call(
            fields_kernel,
            "fields",
            [shape((rows, fields, width), F32)],
            (x1, x2, y1, y2, coef, table, codes),
            [pltpu.VMEM((rows + 2, fields, width), F32)],
            flops=4_000_000_000,
        )
        common = (part, ns, flux, e1, e2, coef0, codes, col0, land_mask)
        if interval < INTERVALS - 1:
            x1, x2, surface, *sent = call(
                functools.partial(middle_kernel, offsets, groups),
                "middle",
                halves + [shape((rows, width), F32)] + payloads,
                common + (weights, sources, targets),
                remap_scratch,
            )
            surface_spec = VMEM
        else:
            new_state, new_coupling = call(
                functools.partial(close_kernel, groups),
                "close",
                [shape(state.shape, F32), shape(coupling.shape, F32)],
                common,
            )
    return new_state, new_coupling


def solution(mesh):
    placed = (
        P("comp", None, "tile", None),
        P("comp", "tile", None),
        P("comp", "tile", None),
        P("comp", "tile", None),
        P("comp", None),
        P("comp", None),
        P("comp", None, None, None),
        P("comp", "tile", None, None),
        P("comp", "tile"),
        P("comp", "tile"),
    )
    return jax.shard_map(
        on_device,
        mesh=mesh,
        in_specs=placed,
        out_specs=(P("comp", None, "tile", None), P("comp", "tile", None)),
        check_vma=False,
    )
```

```python
import functools

import jax
import jax.numpy as jnp
from jax import lax
from jax.experimental import pallas as pl
from jax.experimental.pallas import tpu as pltpu
from jax.sharding import PartitionSpec as P

SUBSTEPS = 2
INTERVALS = 2
EXCHANGE = 0.5
OCEAN_SHARE = 0.3

F32 = jnp.float32
BF16 = jnp.bfloat16
VMEM = pl.BlockSpec(memory_space=pltpu.VMEM)
PARAMS = pltpu.CompilerParams(vmem_limit_bytes=40 * 1024 * 1024)


def partner_offsets(groups):
    air_count = 3 * groups // 4
    upward = [(air_count + member // 3 - member) % groups for member in range(air_count)]
    downward = [
        (3 * member + offset - air_count - member) % groups
        for member in range(groups - air_count)
        for offset in range(3)
    ]
    return sorted(set(upward + downward))


def ring_pairs(count, steps):
    return [(source, (source + steps) % count) for source in range(count)]


def inner_pairs(count):
    return [(tile, tile ^ 1) for tile in range(count)]


def outer_pairs(count):
    return [(tile, (tile + 1) % count if tile % 2 else (tile - 1) % count) for tile in range(count)]


def split_high_low(value):
    high = value.astype(BF16)
    low = (value - high.astype(F32)).astype(BF16)
    return high, low


def payload(handed, wide_ref, pick_ref, chosen_ref, out_refs, blk_ref):
    rows, width = handed.shape
    count, block = blk_ref.shape
    per_row = width // block
    margins = pick_ref.shape[1]
    band = wide_ref.shape[0] // margins
    for c in range(per_row):
        blk_ref[pl.ds(c, rows, stride=per_row), :] = handed[:, c * block : (c + 1) * block]
    picked = lax.dot_general(
        pick_ref[...], blk_ref[...].astype(BF16), (((0,), (0,)), ((), ())), preferred_element_type=F32
    )
    contrib = wide_ref[pl.ds(0, margins, stride=band), :] * picked
    for j in range(1, band):
        turned = pltpu.roll(picked, block - j, 1)
        contrib = contrib + wide_ref[pl.ds(j, margins, stride=band), :] * turned
    high, low = split_high_low(contrib)
    both = jnp.concatenate([high, low], axis=0)
    for n, out_ref in enumerate(out_refs):
        out_ref[...] = jnp.dot(chosen_ref[n], both, preferred_element_type=F32)


def column(row):
    n = row.shape[1]
    diagonal = lax.broadcasted_iota(jnp.int32, (n, n), 0) == lax.broadcasted_iota(jnp.int32, (n, n), 1)
    return jnp.sum(jnp.where(diagonal, row, 0.0), axis=1, keepdims=True)


def open_kernel(offsets, groups, *refs):
    args, refs = refs[:10], refs[10:]
    state, coupling, mask, codes, mixing, courant, matrices, weights, sources, targets = args
    x1, x2, surface, mask_out, codes_out, coef, table, col0, wide, pick, chosen, *refs = refs
    outs, refs = refs[: len(offsets)], refs[len(offsets) :]
    state_v, coupling_v, weights_v, mixing_v, courant_v, matrices_v, sources_v, targets_v, blk, sems = refs
    pairs = (
        (coupling, coupling_v),
        (sources, sources_v),
        (targets, targets_v),
        (weights, weights_v),
        (state, state_v),
        (mixing, mixing_v),
        (courant, courant_v),
        (matrices, matrices_v),
        (mask, mask_out),
        (codes, codes_out),
    )
    copies = [pltpu.make_async_copy(src, dst, sems.at[n]) for n, (src, dst) in enumerate(pairs)]
    for copy in copies:
        copy.start()
    for copy in copies[:4]:
        copy.wait()
    count, margins = pick.shape
    block = blk.shape[1]
    slot = lax.broadcasted_iota(jnp.int32, (count, margins), 0)
    pick[...] = (slot == sources_v[...]).astype(F32).astype(BF16)
    me = lax.axis_index("comp")
    for n, offset in enumerate(offsets):
        base = lax.rem(me + offset, groups) * count
        hit = (targets_v[...] == slot + base).astype(F32).astype(BF16)
        chosen[n] = jnp.concatenate([hit, hit], axis=1)
    wide[...] = weights_v[0].reshape(wide.shape).astype(F32)
    payload(coupling_v[0], wide, pick, chosen, outs, blk)
    for copy in copies[4:]:
        copy.wait()
    odd = lax.rem(lax.axis_index("tile"), 2) == 1
    half = x1.shape[0]
    for i in range(half):
        head, tail = state_v[0, :, i, :], state_v[0, :, half + i, :]
        x1[i] = jnp.where(odd, head, tail)
        x2[i] = jnp.where(odd, tail, head)
    surface[...] = state_v[0, 0]
    m, c = column(mixing_v[...]), column(courant_v[...])
    coef[0], coef[1], coef[2] = 1.0 - 4.0 * m - c, m + c, m
    branches, fields = matrices_v.shape[1:3]
    flat = matrices_v[0].reshape(branches * fields, fields)
    col0[...] = flat[:, :1].reshape(branches, fields, 1)
    flat = jnp.where(lax.broadcasted_iota(jnp.int32, flat.shape, 1) == 0, 0.0, flat)
    high, low = split_high_low(flat)
    table[...] = jnp.concatenate([high, high, low], axis=1)


def surface_kernel(groups, n_rec, *refs):
    recs, (surface_ref, mask_ref, ns_ref, flux_ref, d1, d2, blk) = refs[:n_rec], refs[n_rec:]
    odd = lax.rem(lax.axis_index("tile"), 2) == 1
    air = lax.axis_index("comp") < 3 * groups // 4
    rows, width = ns_ref.shape
    block = blk.shape[-1]
    per_row = width // block
    total = recs[0][...]
    for rec in recs[1:]:
        total = total + rec[...]
    blk[...] = total
    received = jnp.concatenate(
        [blk[pl.ds(c, rows, stride=per_row), :] for c in range(per_row)], axis=1
    )
    surface = surface_ref[...]
    flux = mask_ref[0].astype(F32) * EXCHANGE * (received - surface)
    new = surface + jnp.where(air, flux, -OCEAN_SHARE * received)
    ns_ref[...] = new
    flux_ref[...] = flux
    half = rows // 2
    head, tail = new[:half], new[half:]
    d1[...] = jnp.where(odd, head, tail)
    d2[...] = jnp.where(odd, tail, head)


def substep(f, up, down, c0, cu, m):
    width = f.shape[1]
    sides = pltpu.roll(f, 1, 1) + pltpu.roll(f, width - 1, 1)
    return c0 * f + cu * up + m * (down + sides)


def fields_kernel(x1, x2, y1, y2, coef, table, codes, part, grid_ref):
    odd = lax.rem(lax.axis_index("tile"), 2) == 1
    half, fields, width = x1.shape
    c0, cu, m = coef[0], coef[1], coef[2]
    branches = table.shape[0] // fields

    def row(i):
        group, at = divmod(i, half)
        first, second = ((y2, y1), (x2, x1), (x1, x2), (y1, y2))[group]
        return jnp.where(odd, second[at], first[at])

    above, here = row(0), row(1)
    for i in range(1, 4 * half - 1):
        below = row(i + 1)
        grid_ref[i - 1] = substep(here, above, below, c0, cu, m)
        above, here = here, below
    keep = lax.broadcasted_iota(jnp.int32, (fields, width), 0) > 0
    for r in range(2 * half):
        f = substep(grid_ref[r + 1], grid_ref[r], grid_ref[r + 2], c0, cu, m)
        high, low = split_high_low(jnp.tanh(f))
        terms = jnp.dot(
            table[...], jnp.concatenate([high, low, high], axis=0), preferred_element_type=F32
        )
        code = codes[0, r : r + 1, :]
        tendency = terms[:fields]
        for b in range(1, branches):
            tendency = jnp.where(code == b, terms[b * fields : (b + 1) * fields], tendency)
        part[r] = jnp.where(keep, f, 0.0) + tendency


def field0(ns, e1, e2, coef, odd):
    c0, cu, m = coef[0, :1], coef[1, :1], coef[2, :1]
    half = e1.shape[0]
    first, last = e1[...], e2[...]
    f = jnp.concatenate(
        [jnp.where(odd, first, last), ns[...], jnp.where(odd, last, first)], axis=0
    )
    rows = f.shape[0]
    for _ in range(SUBSTEPS):
        f = substep(f, pltpu.roll(f, 1, 0), pltpu.roll(f, rows - 1, 0), c0, cu, m)
    return f[half : rows - half]


def evolve_rows(part, f0, codes, col0, mask, sea):
    rows, fields, width = part.shape
    branches = col0.shape[0]
    squashed = jnp.tanh(f0)
    top = lax.broadcasted_iota(jnp.int32, (fields, width), 0) == 0
    done = []
    for r in range(rows):
        code = codes[0, r : r + 1, :]
        gain = jnp.broadcast_to(col0[0], (fields, width))
        for b in range(1, branches):
            gain = jnp.where(code == b, col0[b], gain)
        value = part[r] + gain * squashed[r : r + 1, :] + jnp.where(top, f0[r : r + 1, :], 0.0)
        wet = jnp.where(sea, mask[0, r : r + 1, :].astype(F32), 1.0)
        done.append(value * wet)
    return done


def middle_kernel(
    groups, part, ns, flux, e1, e2, coef, codes, col0, mask, wide, pick, chosen, x1, x2, surf, *rest
):
    outs, blk = rest[:-1], rest[-1]
    odd = lax.rem(lax.axis_index("tile"), 2) == 1
    sea = lax.axis_index("comp") >= 3 * groups // 4
    f0 = field0(ns, e1, e2, coef, odd)
    rows = evolve_rows(part, f0, codes, col0, mask, sea)
    half = x1.shape[0]
    for i in range(half):
        x1[i] = jnp.where(odd, rows[i], rows[half + i])
        x2[i] = jnp.where(odd, rows[half + i], rows[i])
    for r, value in enumerate(rows):
        surf[r : r + 1, :] = value[:1]
    handed = jnp.where(sea, surf[...], flux[...])
    payload(handed, wide, pick, chosen, outs, blk)


def close_kernel(groups, part, ns, flux, e1, e2, coef, codes, col0, mask, new_state, new_coupling):
    odd = lax.rem(lax.axis_index("tile"), 2) == 1
    sea = lax.axis_index("comp") >= 3 * groups // 4
    f0 = field0(ns, e1, e2, coef, odd)
    rows = evolve_rows(part, f0, codes, col0, mask, sea)
    for r, value in enumerate(rows):
        new_state[0, :, r, :] = value
        new_coupling[0, r : r + 1, :] = jnp.where(sea, value[:1], flux[r : r + 1, :])


def call(kernel, name, outs, args, scratch=(), in_specs=None, flops=0):
    moved = sum(a.size * a.dtype.itemsize for a in list(args) + list(outs))
    return pl.pallas_call(
        kernel,
        name=name,
        out_shape=outs,
        in_specs=in_specs or [VMEM] * len(args),
        out_specs=[VMEM] * len(outs),
        scratch_shapes=list(scratch),
        compiler_params=PARAMS,
        cost_estimate=pl.CostEstimate(flops=flops, bytes_accessed=moved, transcendentals=0),
    )(*args)


def on_device(
    state, coupling, land_mask, codes, mixing, courant, matrices, weights, sources, targets
):
    groups = lax.axis_size("comp")
    tiles = lax.axis_size("tile")
    offsets = partner_offsets(groups)
    _, fields, rows, width = state.shape
    _, margins, band, block = weights.shape
    count = rows * width // block
    half = rows // 2
    branches = matrices.shape[1]
    shape = jax.ShapeDtypeStruct

    halves = [shape((half, fields, width), F32)] * 2
    payloads = [shape((count, block), F32)] * len(offsets)
    blocks = pltpu.VMEM((count, block), F32)
    tables = [
        shape(land_mask.shape, jnp.int32),
        shape(codes.shape, jnp.int32),
        shape((3, fields, 1), F32),
        shape((branches * fields, 3 * fields), BF16),
        shape((branches, fields, 1), F32),
        shape((margins * band, block), F32),
        shape((count, margins), BF16),
        shape((len(offsets), count, 2 * margins), BF16),
    ]
    args = (
        state, coupling, land_mask, codes, mixing, courant, matrices, weights, sources, targets
    )
    staged = (state, coupling, weights, mixing, courant, matrices, sources, targets)
    x1, x2, surface, mask, codes, coef, table, col0, wide, pick, chosen, *sent = call(
        functools.partial(open_kernel, offsets, groups),
        "open",
        halves + [shape((rows, width), F32)] + tables + payloads,
        [pltpu.with_memory_space_constraint(a, pltpu.HBM) for a in args],
        [pltpu.VMEM(a.shape, a.dtype) for a in staged] + [blocks, pltpu.SemaphoreType.DMA((10,))],
        [pl.BlockSpec(memory_space=pltpu.HBM)] * len(args),
    )
    for interval in range(INTERVALS):
        y2 = lax.ppermute(x2, "tile", outer_pairs(tiles))
        y1 = lax.ppermute(x1, "tile", inner_pairs(tiles))
        recs = [
            lax.ppermute(value, "comp", ring_pairs(groups, offset))
            for value, offset in zip(sent, offsets)
        ]
        ns, flux, d1, d2 = call(
            functools.partial(surface_kernel, groups, len(recs)),
            "surface",
            [shape((rows, width), F32)] * 2 + [shape((half, width), F32)] * 2,
            (*recs, surface, mask),
            [blocks],
        )
        e2 = lax.ppermute(d2, "tile", outer_pairs(tiles))
        e1 = lax.ppermute(d1, "tile", inner_pairs(tiles))
        (part,) = call(
            fields_kernel,
            "fields",
            [shape((rows, fields, width), F32)],
            (x1, x2, y1, y2, coef, table, codes),
            [pltpu.VMEM((rows + 2, fields, width), F32)],
            flops=4_000_000_000,
        )
        common = (part, ns, flux, e1, e2, coef, codes, col0, mask)
        if interval < INTERVALS - 1:
            x1, x2, surface, *sent = call(
                functools.partial(middle_kernel, groups),
                "middle",
                halves + [shape((rows, width), F32)] + payloads,
                common + (wide, pick, chosen),
                [blocks],
            )
        else:
            new_state, new_coupling = call(
                functools.partial(close_kernel, groups),
                "close",
                [shape(state.shape, F32), shape(coupling.shape, F32)],
                common,
            )
    return new_state, new_coupling


def solution(mesh):
    placed = (
        P("comp", None, "tile", None),
        P("comp", "tile", None),
        P("comp", "tile", None),
        P("comp", "tile", None),
        P("comp", None),
        P("comp", None),
        P("comp", None, None, None),
        P("comp", "tile", None, None),
        P("comp", "tile"),
        P("comp", "tile"),
    )
    return jax.shard_map(
        on_device,
        mesh=mesh,
        in_specs=placed,
        out_specs=(P("comp", None, "tile", None), P("comp", "tile", None)),
        check_vma=False,
    )
```

```python
import functools

import jax
import jax.numpy as jnp
from jax import lax
from jax.experimental import pallas as pl
from jax.experimental.pallas import tpu as pltpu
from jax.sharding import PartitionSpec as P

SUBSTEPS = 2
INTERVALS = 2
EXCHANGE = 0.5
OCEAN_SHARE = 0.3

F32 = jnp.float32
BF16 = jnp.bfloat16
VMEM = pl.BlockSpec(memory_space=pltpu.VMEM)
PARAMS = pltpu.CompilerParams(vmem_limit_bytes=40 * 1024 * 1024)


def partner_offsets(groups):
    air_count = 3 * groups // 4
    upward = [(air_count + member // 3 - member) % groups for member in range(air_count)]
    downward = [
        (3 * member + offset - air_count - member) % groups
        for member in range(groups - air_count)
        for offset in range(3)
    ]
    return sorted(set(upward + downward))


def ring_pairs(count, steps):
    return [(source, (source + steps) % count) for source in range(count)]


def inner_pairs(count):
    return [(tile, tile ^ 1) for tile in range(count)]


def outer_pairs(count):
    return [(tile, (tile + 1) % count if tile % 2 else (tile - 1) % count) for tile in range(count)]


def split_high_low(value):
    high = value.astype(BF16)
    low = (value - high.astype(F32)).astype(BF16)
    return high, low


def payload(handed, wide_ref, pick_ref, chosen_ref, out_refs, blk_ref):
    rows, width = handed.shape
    count, block = blk_ref.shape
    per_row = width // block
    margins = pick_ref.shape[1]
    band = wide_ref.shape[0] // margins
    for c in range(per_row):
        blk_ref[pl.ds(c, rows, stride=per_row), :] = handed[:, c * block : (c + 1) * block]
    picked = lax.dot_general(
        pick_ref[...], blk_ref[...].astype(BF16), (((0,), (0,)), ((), ())), preferred_element_type=F32
    )
    contrib = wide_ref[pl.ds(0, margins, stride=band), :] * picked
    for j in range(1, band):
        turned = pltpu.roll(picked, block - j, 1)
        contrib = contrib + wide_ref[pl.ds(j, margins, stride=band), :] * turned
    high, low = split_high_low(contrib)
    both = jnp.concatenate([high, low], axis=0)
    blocks = jnp.dot(chosen_ref[...], both, preferred_element_type=F32)
    for n, out_ref in enumerate(out_refs):
        out_ref[...] = blocks[n * count : (n + 1) * count]


def column(row):
    n = row.shape[1]
    diagonal = lax.broadcasted_iota(jnp.int32, (n, n), 0) == lax.broadcasted_iota(jnp.int32, (n, n), 1)
    return jnp.sum(jnp.where(diagonal, row, 0.0), axis=1, keepdims=True)


def open_kernel(offsets, groups, *refs):
    args, refs = refs[:10], refs[10:]
    state, coupling, mask, codes, mixing, courant, matrices, weights, sources, targets = args
    x1, x2, surface, mask_out, codes_out, coef, table, col0, wide, pick, chosen, *refs = refs
    outs, refs = refs[: len(offsets)], refs[len(offsets) :]
    state_v, coupling_v, weights_v, mixing_v, courant_v, matrices_v, sources_v, targets_v, blk, sems = refs
    pairs = (
        (sources, sources_v),
        (targets, targets_v),
        (mixing, mixing_v),
        (courant, courant_v),
        (matrices, matrices_v),
        (coupling, coupling_v),
        (mask, mask_out),
        (codes, codes_out),
        (weights, weights_v),
        (state, state_v),
    )
    copies = [pltpu.make_async_copy(src, dst, sems.at[n]) for n, (src, dst) in enumerate(pairs)]
    for copy in copies:
        copy.start()
    small = 8
    for copy in copies[:small]:
        copy.wait()
    count, margins = pick.shape
    block = blk.shape[1]
    slot = lax.broadcasted_iota(jnp.int32, (count, margins), 0)
    pick[...] = (slot == sources_v[...]).astype(F32).astype(BF16)
    me = lax.axis_index("comp")
    for n, offset in enumerate(offsets):
        base = lax.rem(me + offset, groups) * count
        hit = (targets_v[...] == slot + base).astype(F32).astype(BF16)
        chosen[n * count : (n + 1) * count] = jnp.concatenate([hit, hit], axis=1)
    m, c = column(mixing_v[...]), column(courant_v[...])
    coef[0], coef[1], coef[2] = 1.0 - 4.0 * m - c, m + c, m
    branches, fields = matrices_v.shape[1:3]
    flat = matrices_v[0].reshape(branches * fields, fields)
    col0[...] = flat[:, :1].reshape(branches, fields, 1)
    flat = jnp.where(lax.broadcasted_iota(jnp.int32, flat.shape, 1) == 0, 0.0, flat)
    high, low = split_high_low(flat)
    table[...] = jnp.concatenate([high, high, low], axis=1)
    copies[small].wait()
    wide[...] = weights_v[0].reshape(wide.shape).astype(F32)
    payload(coupling_v[0], wide, pick, chosen, outs, blk)
    copies[small + 1].wait()
    odd = lax.rem(lax.axis_index("tile"), 2) == 1
    half = x1.shape[0]
    for i in range(half):
        head, tail = state_v[0, :, i, :], state_v[0, :, half + i, :]
        x1[i] = jnp.where(odd, head, tail)
        x2[i] = jnp.where(odd, tail, head)
    surface[...] = state_v[0, 0]


def surface_kernel(groups, n_rec, *refs):
    recs, (surface_ref, mask_ref, ns_ref, flux_ref, d1, d2, blk) = refs[:n_rec], refs[n_rec:]
    odd = lax.rem(lax.axis_index("tile"), 2) == 1
    air = lax.axis_index("comp") < 3 * groups // 4
    rows, width = ns_ref.shape
    block = blk.shape[-1]
    per_row = width // block
    total = recs[0][...]
    for rec in recs[1:]:
        total = total + rec[...]
    blk[...] = total
    received = jnp.concatenate(
        [blk[pl.ds(c, rows, stride=per_row), :] for c in range(per_row)], axis=1
    )
    surface = surface_ref[...]
    flux = mask_ref[0].astype(F32) * EXCHANGE * (received - surface)
    new = surface + jnp.where(air, flux, -OCEAN_SHARE * received)
    ns_ref[...] = new
    flux_ref[...] = flux
    half = rows // 2
    head, tail = new[:half], new[half:]
    d1[...] = jnp.where(odd, head, tail)
    d2[...] = jnp.where(odd, tail, head)


def substep(f, up, down, c0, cu, m):
    width = f.shape[1]
    sides = pltpu.roll(f, 1, 1) + pltpu.roll(f, width - 1, 1)
    return c0 * f + cu * up + m * (down + sides)


def sides(f):
    return pltpu.roll(f, 1, 1) + pltpu.roll(f, f.shape[1] - 1, 1)


def inner_kernel(x1, x2, coef, base):
    odd = lax.rem(lax.axis_index("tile"), 2) == 1
    c0, cu, m = coef[0], coef[1], coef[2]
    f0, f1 = (jnp.where(odd, x1[i], x2[i]) for i in range(2))
    f2, f3 = (jnp.where(odd, x2[i], x1[i]) for i in range(2))
    g0 = c0 * f0 + m * (f1 + sides(f0))
    g1 = substep(f1, f0, f2, c0, cu, m)
    g2 = substep(f2, f1, f3, c0, cu, m)
    g3 = c0 * f3 + cu * f2 + m * sides(f3)
    base[0] = c0 * g0 + m * (g1 + sides(g0)) + (cu * m) * f0
    base[1] = substep(g1, g0, g2, c0, cu, m)
    base[2] = substep(g2, g1, g3, c0, cu, m)
    base[3] = c0 * g3 + cu * g2 + m * sides(g3) + (cu * m) * f3


def fields_kernel(groups, base, y1, y2, coef, table, col0, codes, mask, part, gain):
    odd = lax.rem(lax.axis_index("tile"), 2) == 1
    sea = lax.axis_index("comp") >= 3 * groups // 4
    rows, fields, width = base.shape
    c0, cu, m = coef[0], coef[1], coef[2]
    branches = table.shape[0] // fields
    near, far = jnp.where(odd, y1[1], y2[1]), jnp.where(odd, y1[0], y2[0])
    top = (2.0 * cu * c0) * near + (2.0 * cu * m) * sides(near) + (cu * cu) * far
    top_next = (cu * cu) * near
    near, far = jnp.where(odd, y2[0], y1[0]), jnp.where(odd, y2[1], y1[1])
    bottom = (2.0 * m * c0) * near + (2.0 * m * m) * sides(near) + (m * m) * far
    bottom_next = (m * m) * near
    keep = lax.broadcasted_iota(jnp.int32, (fields, width), 0) > 0
    for r, halo in enumerate((top, top_next, bottom_next, bottom)):
        f = base[r] + halo
        high, low = split_high_low(jnp.tanh(f))
        terms = jnp.dot(
            table[...], jnp.concatenate([high, low, high], axis=0), preferred_element_type=F32
        )
        code = codes[0, r : r + 1, :]
        wet = jnp.where(sea, mask[0, r : r + 1, :].astype(F32), 1.0)
        tendency = terms[:fields]
        factor = jnp.broadcast_to(col0[0], (fields, width))
        for b in range(1, branches):
            tendency = jnp.where(code == b, terms[b * fields : (b + 1) * fields], tendency)
            factor = jnp.where(code == b, col0[b], factor)
        part[r] = (jnp.where(keep, f, 0.0) + tendency) * wet
        gain[r] = factor * wet


def field0(ns, e1, e2, coef, odd):
    c0, cu, m = coef[0, :1], coef[1, :1], coef[2, :1]
    half = e1.shape[0]
    first, last = e1[...], e2[...]
    f = jnp.concatenate(
        [jnp.where(odd, first, last), ns[...], jnp.where(odd, last, first)], axis=0
    )
    rows = f.shape[0]
    for _ in range(SUBSTEPS):
        f = substep(f, pltpu.roll(f, 1, 0), pltpu.roll(f, rows - 1, 0), c0, cu, m)
    return f[half : rows - half]


SUBLANES = 8


def evolve_rows(groups, part, gain, ns, e1, e2, coef, mask, f0_ref, squashed_ref):
    odd = lax.rem(lax.axis_index("tile"), 2) == 1
    sea = lax.axis_index("comp") >= 3 * groups // 4
    f0 = field0(ns, e1, e2, coef, odd)
    squashed_ref[...] = jnp.tanh(f0)
    f0_ref[...] = f0 * jnp.where(sea, mask[0].astype(F32), 1.0)
    width = part.shape[2]
    first = (lax.broadcasted_iota(jnp.int32, (SUBLANES, width), 0) == 0).astype(F32)

    def value(r, h):
        some = slice(h, h + SUBLANES)
        total = part[r, some] + gain[r, some] * squashed_ref[r : r + 1, :]
        return total + first * f0_ref[r : r + 1, :] if h == 0 else total

    return value


def evolve_kernel(groups, part, gain, ns, e1, e2, coef, mask, x1, x2, surf, *scratch):
    odd = lax.rem(lax.axis_index("tile"), 2) == 1
    value = evolve_rows(groups, part, gain, ns, e1, e2, coef, mask, *scratch)
    half, fields, _ = x1.shape
    for i in range(half):
        for h in range(0, fields, SUBLANES):
            head, tail = value(i, h), value(half + i, h)
            x1[i, h : h + SUBLANES] = jnp.where(odd, head, tail)
            x2[i, h : h + SUBLANES] = jnp.where(odd, tail, head)
            if h == 0:
                surf[i : i + 1, :] = head[:1]
                surf[half + i : half + i + 1, :] = tail[:1]


def payload_kernel(groups, surf, flux, wide, pick, chosen, *rest):
    sea = lax.axis_index("comp") >= 3 * groups // 4
    payload(jnp.where(sea, surf[...], flux[...]), wide, pick, chosen, rest[:-1], rest[-1])


def close_kernel(
    groups, part, gain, ns, flux, e1, e2, coef, mask, new_state, new_coupling, *scratch
):
    sea = lax.axis_index("comp") >= 3 * groups // 4
    value = evolve_rows(groups, part, gain, ns, e1, e2, coef, mask, *scratch)
    rows, fields, _ = part.shape
    for h in range(0, fields, SUBLANES):
        for r in range(rows):
            done = value(r, h)
            new_state[0, h : h + SUBLANES, r, :] = done
            if h == 0:
                new_coupling[0, r : r + 1, :] = jnp.where(sea, done[:1], flux[r : r + 1, :])


def call(kernel, name, outs, args, scratch=(), in_specs=None, flops=0):
    moved = sum(a.size * a.dtype.itemsize for a in list(args) + list(outs))
    return pl.pallas_call(
        kernel,
        name=name,
        out_shape=outs,
        in_specs=in_specs or [VMEM] * len(args),
        out_specs=[VMEM] * len(outs),
        scratch_shapes=list(scratch),
        compiler_params=PARAMS,
        cost_estimate=pl.CostEstimate(flops=flops, bytes_accessed=moved, transcendentals=0),
    )(*args)


def on_device(
    state, coupling, land_mask, codes, mixing, courant, matrices, weights, sources, targets
):
    groups = lax.axis_size("comp")
    tiles = lax.axis_size("tile")
    offsets = partner_offsets(groups)
    _, fields, rows, width = state.shape
    _, margins, band, block = weights.shape
    count = rows * width // block
    half = rows // 2
    branches = matrices.shape[1]
    shape = jax.ShapeDtypeStruct

    halves = [shape((half, fields, width), F32)] * 2
    payloads = [shape((count, block), F32)] * len(offsets)
    blocks = pltpu.VMEM((count, block), F32)
    tables = [
        shape(land_mask.shape, jnp.int32),
        shape(codes.shape, jnp.int32),
        shape((3, fields, 1), F32),
        shape((branches * fields, 3 * fields), BF16),
        shape((branches, fields, 1), F32),
        shape((margins * band, block), F32),
        shape((count, margins), BF16),
        shape((len(offsets) * count, 2 * margins), BF16),
    ]
    args = (
        state, coupling, land_mask, codes, mixing, courant, matrices, weights, sources, targets
    )
    staged = (state, coupling, weights, mixing, courant, matrices, sources, targets)
    x1, x2, surface, mask, codes, coef, table, col0, wide, pick, chosen, *sent = call(
        functools.partial(open_kernel, offsets, groups),
        "open",
        halves + [shape((rows, width), F32)] + tables + payloads,
        [pltpu.with_memory_space_constraint(a, pltpu.HBM) for a in args],
        [pltpu.VMEM(a.shape, a.dtype) for a in staged] + [blocks, pltpu.SemaphoreType.DMA((10,))],
        [pl.BlockSpec(memory_space=pltpu.HBM)] * len(args),
    )
    for interval in range(INTERVALS):
        y2 = lax.ppermute(x2, "tile", outer_pairs(tiles))
        y1 = lax.ppermute(x1, "tile", inner_pairs(tiles))
        recs = [
            lax.ppermute(value, "comp", ring_pairs(groups, offset))
            for value, offset in zip(sent, offsets)
        ]
        ns, flux, d1, d2 = call(
            functools.partial(surface_kernel, groups, len(recs)),
            "surface",
            [shape((rows, width), F32)] * 2 + [shape((half, width), F32)] * 2,
            (*recs, surface, mask),
            [blocks],
        )
        e2 = lax.ppermute(d2, "tile", outer_pairs(tiles))
        e1 = lax.ppermute(d1, "tile", inner_pairs(tiles))
        (base,) = call(
            inner_kernel, "inner", [shape((rows, fields, width), F32)], (x1, x2, coef)
        )
        part, gain = call(
            functools.partial(fields_kernel, groups),
            "fields",
            [shape((rows, fields, width), F32)] * 2,
            (base, y1, y2, coef, table, col0, codes, mask),
            flops=4_000_000_000,
        )
        lines = [pltpu.VMEM((rows, width), F32)] * 2
        if interval < INTERVALS - 1:
            x1, x2, surface = call(
                functools.partial(evolve_kernel, groups),
                "evolve",
                halves + [shape((rows, width), F32)],
                (part, gain, ns, e1, e2, coef, mask),
                lines,
            )
            sent = call(
                functools.partial(payload_kernel, groups),
                "payload",
                payloads,
                (surface, flux, wide, pick, chosen),
                [blocks],
            )
        else:
            new_state, new_coupling = call(
                functools.partial(close_kernel, groups),
                "close",
                [shape(state.shape, F32), shape(coupling.shape, F32)],
                (part, gain, ns, flux, e1, e2, coef, mask),
                lines,
            )
    return new_state, new_coupling


def solution(mesh):
    placed = (
        P("comp", None, "tile", None),
        P("comp", "tile", None),
        P("comp", "tile", None),
        P("comp", "tile", None),
        P("comp", None),
        P("comp", None),
        P("comp", None, None, None),
        P("comp", "tile", None, None),
        P("comp", "tile"),
        P("comp", "tile"),
    )
    return jax.shard_map(
        on_device,
        mesh=mesh,
        in_specs=placed,
        out_specs=(P("comp", None, "tile", None), P("comp", "tile", None)),
        check_vma=False,
    )
```

```python
import functools

import jax
import jax.numpy as jnp
from jax import lax
from jax.experimental import pallas as pl
from jax.experimental.pallas import tpu as pltpu
from jax.sharding import PartitionSpec as P

SUBSTEPS = 2
INTERVALS = 2
EXCHANGE = 0.5
OCEAN_SHARE = 0.3

F32 = jnp.float32
BF16 = jnp.bfloat16
VMEM = pl.BlockSpec(memory_space=pltpu.VMEM)
PARAMS = pltpu.CompilerParams(vmem_limit_bytes=40 * 1024 * 1024)


MEMBERS = 3


def partner_pairs(groups, tiles, member):
    air_count = MEMBERS * groups // 4
    pairs = []
    for group in range(groups):
        ocean = group >= air_count
        if ocean:
            partner = MEMBERS * (group - air_count) + member
        else:
            partner = air_count + group // MEMBERS if group % MEMBERS == member else group
        for tile in range(tiles):
            other = tile ^ 1 if partner == group else tile
            pairs.append((group * tiles + tile, partner * tiles + other))
    return pairs


def inner_pairs(count):
    return [(tile, tile ^ 1) for tile in range(count)]


def outer_pairs(count):
    return [(tile, (tile + 1) % count if tile % 2 else (tile - 1) % count) for tile in range(count)]


def split_high_low(value):
    high = value.astype(BF16)
    low = (value - high.astype(F32)).astype(BF16)
    return high, low


def payload(handed, wide_ref, pick_ref, chosen_ref, out_refs, blk_ref):
    rows, width = handed.shape
    count, block = blk_ref.shape
    per_row = width // block
    margins = pick_ref.shape[1]
    band = wide_ref.shape[0] // margins
    for c in range(per_row):
        blk_ref[pl.ds(c, rows, stride=per_row), :] = handed[:, c * block : (c + 1) * block]
    picked = lax.dot_general(
        pick_ref[...], blk_ref[...].astype(BF16), (((0,), (0,)), ((), ())), preferred_element_type=F32
    )
    contrib = wide_ref[pl.ds(0, margins, stride=band), :] * picked
    for j in range(1, band):
        turned = pltpu.roll(picked, block - j, 1)
        contrib = contrib + wide_ref[pl.ds(j, margins, stride=band), :] * turned
    high, low = split_high_low(contrib)
    both = jnp.concatenate([high, low], axis=0)
    blocks = jnp.dot(chosen_ref[...], both, preferred_element_type=F32)
    for n, out_ref in enumerate(out_refs):
        out_ref[...] = blocks[n * count : (n + 1) * count]


def column(row):
    n = row.shape[1]
    diagonal = lax.broadcasted_iota(jnp.int32, (n, n), 0) == lax.broadcasted_iota(jnp.int32, (n, n), 1)
    return jnp.sum(jnp.where(diagonal, row, 0.0), axis=1, keepdims=True)


def load_kernel(*refs):
    state, *args = refs[:10]
    x1, x2, surface = refs[10:13]
    outs, (state_v, sems) = refs[13:22], refs[22:]
    copies = [
        pltpu.make_async_copy(src, dst, sems.at[n])
        for n, (src, dst) in enumerate(zip((state, *args), (state_v, *outs)))
    ]
    for copy in copies:
        copy.start()
    copies[0].wait()
    odd = lax.rem(lax.axis_index("tile"), 2) == 1
    half = x1.shape[0]
    for i in range(half):
        head, tail = state_v[0, :, i, :], state_v[0, :, half + i, :]
        x1[i] = jnp.where(odd, head, tail)
        x2[i] = jnp.where(odd, tail, head)
    surface[...] = state_v[0, 0]
    for copy in copies[1:]:
        copy.wait()


def remap_kernel(groups, coupling, mixing, courant, matrices, weights, sources, targets, *refs):
    coef, table, col0, wide, pick, chosen, *outs, blk = refs
    count, margins = pick.shape
    slot = lax.broadcasted_iota(jnp.int32, (count, margins), 0)
    pick[...] = (slot == sources[...]).astype(F32).astype(BF16)
    me = lax.axis_index("comp")
    air_count = MEMBERS * groups // 4
    for n in range(MEMBERS):
        ocean = jnp.where(lax.rem(me, MEMBERS) == n, air_count + lax.div(me, MEMBERS), me)
        partner = jnp.where(me < air_count, ocean, MEMBERS * (me - air_count) + n)
        hit = (targets[...] == slot + partner * count).astype(F32).astype(BF16)
        chosen[n * count : (n + 1) * count] = jnp.concatenate([hit, hit], axis=1)
    wide[...] = weights[0].reshape(wide.shape).astype(F32)
    payload(coupling[0], wide, pick, chosen, outs, blk)
    m, c = column(mixing[...]), column(courant[...])
    coef[0], coef[1], coef[2] = 1.0 - 4.0 * m - c, m + c, m
    branches, fields = matrices.shape[1:3]
    flat = matrices[0].reshape(branches * fields, fields)
    col0[...] = flat[:, :1].reshape(branches, fields, 1)
    flat = jnp.where(lax.broadcasted_iota(jnp.int32, flat.shape, 1) == 0, 0.0, flat)
    high, low = split_high_low(flat)
    table[...] = jnp.concatenate([high, high, low], axis=1)


def surface_kernel(groups, n_rec, *refs):
    recs, (surface_ref, mask_ref, ns_ref, flux_ref, d1, d2, blk) = refs[:n_rec], refs[n_rec:]
    odd = lax.rem(lax.axis_index("tile"), 2) == 1
    air = lax.axis_index("comp") < 3 * groups // 4
    rows, width = ns_ref.shape
    block = blk.shape[-1]
    per_row = width // block
    total = recs[0][...]
    for rec in recs[1:]:
        total = total + rec[...]
    blk[...] = total
    received = jnp.concatenate(
        [blk[pl.ds(c, rows, stride=per_row), :] for c in range(per_row)], axis=1
    )
    surface = surface_ref[...]
    flux = mask_ref[0].astype(F32) * EXCHANGE * (received - surface)
    new = surface + jnp.where(air, flux, -OCEAN_SHARE * received)
    ns_ref[...] = new
    flux_ref[...] = flux
    half = rows // 2
    head, tail = new[:half], new[half:]
    d1[...] = jnp.where(odd, head, tail)
    d2[...] = jnp.where(odd, tail, head)


def substep(f, up, down, c0, cu, m):
    width = f.shape[1]
    sides = pltpu.roll(f, 1, 1) + pltpu.roll(f, width - 1, 1)
    return c0 * f + cu * up + m * (down + sides)


def sides(f):
    return pltpu.roll(f, 1, 1) + pltpu.roll(f, f.shape[1] - 1, 1)


def inner_kernel(x1, x2, coef, base):
    odd = lax.rem(lax.axis_index("tile"), 2) == 1
    c0, cu, m = coef[0], coef[1], coef[2]
    f0, f1 = (jnp.where(odd, x1[i], x2[i]) for i in range(2))
    f2, f3 = (jnp.where(odd, x2[i], x1[i]) for i in range(2))
    g0 = c0 * f0 + m * (f1 + sides(f0))
    g1 = substep(f1, f0, f2, c0, cu, m)
    g2 = substep(f2, f1, f3, c0, cu, m)
    g3 = c0 * f3 + cu * f2 + m * sides(f3)
    base[0] = c0 * g0 + m * (g1 + sides(g0)) + (cu * m) * f0
    base[1] = substep(g1, g0, g2, c0, cu, m)
    base[2] = substep(g2, g1, g3, c0, cu, m)
    base[3] = c0 * g3 + cu * g2 + m * sides(g3) + (cu * m) * f3


def fields_kernel(groups, base, y1, y2, coef, table, col0, codes, mask, part, gain):
    odd = lax.rem(lax.axis_index("tile"), 2) == 1
    sea = lax.axis_index("comp") >= 3 * groups // 4
    rows, fields, width = base.shape
    c0, cu, m = coef[0], coef[1], coef[2]
    branches = table.shape[0] // fields
    near, far = jnp.where(odd, y1[1], y2[1]), jnp.where(odd, y1[0], y2[0])
    top = (2.0 * cu * c0) * near + (2.0 * cu * m) * sides(near) + (cu * cu) * far
    top_next = (cu * cu) * near
    near, far = jnp.where(odd, y2[0], y1[0]), jnp.where(odd, y2[1], y1[1])
    bottom = (2.0 * m * c0) * near + (2.0 * m * m) * sides(near) + (m * m) * far
    bottom_next = (m * m) * near
    keep = lax.broadcasted_iota(jnp.int32, (fields, width), 0) > 0
    for r, halo in enumerate((top, top_next, bottom_next, bottom)):
        f = base[r] + halo
        high, low = split_high_low(jnp.tanh(f))
        terms = jnp.dot(
            table[...], jnp.concatenate([high, low, high], axis=0), preferred_element_type=F32
        )
        code = codes[0, r : r + 1, :]
        wet = jnp.where(sea, mask[0, r : r + 1, :].astype(F32), 1.0)
        tendency = terms[:fields]
        factor = jnp.broadcast_to(col0[0], (fields, width))
        for b in range(1, branches):
            tendency = jnp.where(code == b, terms[b * fields : (b + 1) * fields], tendency)
            factor = jnp.where(code == b, col0[b], factor)
        part[r] = (jnp.where(keep, f, 0.0) + tendency) * wet
        gain[r] = factor * wet


def field0(ns, e1, e2, coef, odd):
    c0, cu, m = coef[0, :1], coef[1, :1], coef[2, :1]
    half = e1.shape[0]
    first, last = e1[...], e2[...]
    f = jnp.concatenate(
        [jnp.where(odd, first, last), ns[...], jnp.where(odd, last, first)], axis=0
    )
    rows = f.shape[0]
    for _ in range(SUBSTEPS):
        f = substep(f, pltpu.roll(f, 1, 0), pltpu.roll(f, rows - 1, 0), c0, cu, m)
    return f[half : rows - half]


SUBLANES = 8


def evolve_rows(groups, part, gain, ns, e1, e2, coef, mask, f0_ref, squashed_ref):
    odd = lax.rem(lax.axis_index("tile"), 2) == 1
    sea = lax.axis_index("comp") >= 3 * groups // 4
    f0 = field0(ns, e1, e2, coef, odd)
    squashed_ref[...] = jnp.tanh(f0)
    f0_ref[...] = f0 * jnp.where(sea, mask[0].astype(F32), 1.0)
    width = part.shape[2]
    first = (lax.broadcasted_iota(jnp.int32, (SUBLANES, width), 0) == 0).astype(F32)

    def value(r, h):
        some = slice(h, h + SUBLANES)
        total = part[r, some] + gain[r, some] * squashed_ref[r : r + 1, :]
        return total + first * f0_ref[r : r + 1, :] if h == 0 else total

    return value


def evolve_kernel(groups, part, gain, ns, e1, e2, coef, mask, x1, x2, surf, *scratch):
    odd = lax.rem(lax.axis_index("tile"), 2) == 1
    value = evolve_rows(groups, part, gain, ns, e1, e2, coef, mask, *scratch)
    half, fields, _ = x1.shape
    for i in range(half):
        for h in range(0, fields, SUBLANES):
            head, tail = value(i, h), value(half + i, h)
            x1[i, h : h + SUBLANES] = jnp.where(odd, head, tail)
            x2[i, h : h + SUBLANES] = jnp.where(odd, tail, head)
            if h == 0:
                surf[i : i + 1, :] = head[:1]
                surf[half + i : half + i + 1, :] = tail[:1]


def payload_kernel(groups, surf, flux, wide, pick, chosen, *rest):
    sea = lax.axis_index("comp") >= 3 * groups // 4
    payload(jnp.where(sea, surf[...], flux[...]), wide, pick, chosen, rest[:-1], rest[-1])


def close_kernel(
    groups, part, gain, ns, flux, e1, e2, coef, mask, new_state, new_coupling, *scratch
):
    sea = lax.axis_index("comp") >= 3 * groups // 4
    value = evolve_rows(groups, part, gain, ns, e1, e2, coef, mask, *scratch)
    rows, fields, _ = part.shape
    for h in range(0, fields, SUBLANES):
        for r in range(rows):
            done = value(r, h)
            new_state[0, h : h + SUBLANES, r, :] = done
            if h == 0:
                new_coupling[0, r : r + 1, :] = jnp.where(sea, done[:1], flux[r : r + 1, :])


def call(kernel, name, outs, args, scratch=(), in_specs=None, flops=0):
    moved = sum(a.size * a.dtype.itemsize for a in list(args) + list(outs))
    return pl.pallas_call(
        kernel,
        name=name,
        out_shape=outs,
        in_specs=in_specs or [VMEM] * len(args),
        out_specs=[VMEM] * len(outs),
        scratch_shapes=list(scratch),
        compiler_params=PARAMS,
        cost_estimate=pl.CostEstimate(flops=flops, bytes_accessed=moved, transcendentals=0),
    )(*args)


def on_device(
    state, coupling, land_mask, codes, mixing, courant, matrices, weights, sources, targets
):
    groups = lax.axis_size("comp")
    tiles = lax.axis_size("tile")
    _, fields, rows, width = state.shape
    _, margins, band, block = weights.shape
    count = rows * width // block
    half = rows // 2
    branches = matrices.shape[1]
    shape = jax.ShapeDtypeStruct

    halves = [shape((half, fields, width), F32)] * 2
    payloads = [shape((count, block), F32)] * MEMBERS
    blocks = pltpu.VMEM((count, block), F32)
    args = (
        state, coupling, land_mask, codes, mixing, courant, matrices, weights, sources, targets
    )
    x1, x2, surface, handed, mask, codes, *raw = call(
        load_kernel,
        "load",
        halves + [shape((rows, width), F32)] + [shape(a.shape, a.dtype) for a in args[1:]],
        [pltpu.with_memory_space_constraint(a, pltpu.HBM) for a in args],
        [pltpu.VMEM(state.shape, F32), pltpu.SemaphoreType.DMA((len(args),))],
        [pl.BlockSpec(memory_space=pltpu.HBM)] * len(args),
    )
    tables = [
        shape((3, fields, 1), F32),
        shape((branches * fields, 3 * fields), BF16),
        shape((branches, fields, 1), F32),
        shape((margins * band, block), F32),
        shape((count, margins), BF16),
        shape((MEMBERS * count, 2 * margins), BF16),
    ]
    coef, table, col0, wide, pick, chosen, *sent = call(
        functools.partial(remap_kernel, groups),
        "remap",
        tables + payloads,
        (handed, *raw),
        [blocks],
    )
    for interval in range(INTERVALS):
        y2 = lax.ppermute(x2, "tile", outer_pairs(tiles))
        y1 = lax.ppermute(x1, "tile", inner_pairs(tiles))
        recs = [
            lax.ppermute(value, ("comp", "tile"), partner_pairs(groups, tiles, member))
            for member, value in enumerate(sent)
        ]
        ns, flux, d1, d2 = call(
            functools.partial(surface_kernel, groups, len(recs)),
            "surface",
            [shape((rows, width), F32)] * 2 + [shape((half, width), F32)] * 2,
            (*recs, surface, mask),
            [blocks],
        )
        e2 = lax.ppermute(d2, "tile", outer_pairs(tiles))
        e1 = lax.ppermute(d1, "tile", inner_pairs(tiles))
        (base,) = call(
            inner_kernel, "inner", [shape((rows, fields, width), F32)], (x1, x2, coef)
        )
        part, gain = call(
            functools.partial(fields_kernel, groups),
            "fields",
            [shape((rows, fields, width), F32)] * 2,
            (base, y1, y2, coef, table, col0, codes, mask),
            flops=4_000_000_000,
        )
        lines = [pltpu.VMEM((rows, width), F32)] * 2
        if interval < INTERVALS - 1:
            x1, x2, surface = call(
                functools.partial(evolve_kernel, groups),
                "evolve",
                halves + [shape((rows, width), F32)],
                (part, gain, ns, e1, e2, coef, mask),
                lines,
            )
            sent = call(
                functools.partial(payload_kernel, groups),
                "payload",
                payloads,
                (surface, flux, wide, pick, chosen),
                [blocks],
            )
        else:
            new_state, new_coupling = call(
                functools.partial(close_kernel, groups),
                "close",
                [shape(state.shape, F32), shape(coupling.shape, F32)],
                (part, gain, ns, flux, e1, e2, coef, mask),
                lines,
            )
    return new_state, new_coupling


def solution(mesh):
    placed = (
        P("comp", None, "tile", None),
        P("comp", "tile", None),
        P("comp", "tile", None),
        P("comp", "tile", None),
        P("comp", None),
        P("comp", None),
        P("comp", None, None, None),
        P("comp", "tile", None, None),
        P("comp", "tile"),
        P("comp", "tile"),
    )
    return jax.shard_map(
        on_device,
        mesh=mesh,
        in_specs=placed,
        out_specs=(P("comp", None, "tile", None), P("comp", "tile", None)),
        check_vma=False,
    )
```

```python
import functools

import jax
import jax.numpy as jnp
from jax import lax
from jax.experimental import pallas as pl
from jax.experimental.pallas import tpu as pltpu
from jax.sharding import PartitionSpec as P

SUBSTEPS = 2
INTERVALS = 2
EXCHANGE = 0.5
OCEAN_SHARE = 0.3

F32 = jnp.float32
BF16 = jnp.bfloat16
VMEM = pl.BlockSpec(memory_space=pltpu.VMEM)
PARAMS = pltpu.CompilerParams(vmem_limit_bytes=40 * 1024 * 1024)


MEMBERS = 3
SUBLANES = 8


def partner_pairs(groups, tiles, member):
    air_count = MEMBERS * groups // 4
    pairs = []
    for group in range(groups):
        ocean = group >= air_count
        if ocean:
            partner = MEMBERS * (group - air_count) + member
        else:
            partner = air_count + group // MEMBERS if group % MEMBERS == member else group
        for tile in range(tiles):
            other = tile ^ 1 if partner == group else tile
            pairs.append((group * tiles + tile, partner * tiles + other))
    return pairs


def inner_pairs(count):
    return [(tile, tile ^ 1) for tile in range(count)]


def outer_pairs(count):
    return [(tile, (tile + 1) % count if tile % 2 else (tile - 1) % count) for tile in range(count)]


def split_high_low(value):
    high = value.astype(BF16)
    low = (value - high.astype(F32)).astype(BF16)
    return high, low


def payload(handed, wide_ref, pick_ref, chosen_ref, out_refs, blk_ref):
    rows, width = handed.shape
    count, block = blk_ref.shape
    per_row = width // block
    margins = pick_ref.shape[1]
    band = wide_ref.shape[0] // margins
    for c in range(per_row):
        blk_ref[pl.ds(c, rows, stride=per_row), :] = handed[:, c * block : (c + 1) * block]
    picked = lax.dot_general(
        pick_ref[...], blk_ref[...].astype(BF16), (((0,), (0,)), ((), ())), preferred_element_type=F32
    )
    contrib = wide_ref[pl.ds(0, margins, stride=band), :] * picked
    for j in range(1, band):
        turned = pltpu.roll(picked, block - j, 1)
        contrib = contrib + wide_ref[pl.ds(j, margins, stride=band), :] * turned
    high, low = split_high_low(contrib)
    both = jnp.concatenate([high, low], axis=0)
    blocks = jnp.dot(chosen_ref[...], both, preferred_element_type=F32)
    for n, out_ref in enumerate(out_refs):
        out_ref[...] = blocks[n * count : (n + 1) * count]


def column(row):
    n = row.shape[1]
    diagonal = lax.broadcasted_iota(jnp.int32, (n, n), 0) == lax.broadcasted_iota(jnp.int32, (n, n), 1)
    return jnp.sum(jnp.where(diagonal, row, 0.0), axis=1, keepdims=True)


def is_odd():
    return lax.rem(lax.axis_index("tile"), 2) == 1


def is_sea(groups):
    return lax.axis_index("comp") >= MEMBERS * groups // 4


def halves_of(rows):
    half = len(rows) // 2
    head, tail = rows[:half], rows[half:]
    inner = [jnp.where(is_odd(), h, t) for h, t in zip(head, tail)]
    outer = [jnp.where(is_odd(), t, h) for h, t in zip(head, tail)]
    return inner, outer


def rows_of(inner, outer):
    head = [jnp.where(is_odd(), i, o) for i, o in zip(inner, outer)]
    tail = [jnp.where(is_odd(), o, i) for i, o in zip(inner, outer)]
    return head + tail


def lines_of(lines):
    return [lines[r : r + 1] for r in range(lines.shape[0])]


def load_kernel(groups, *refs):
    state, *args = refs[:10]
    x1, x2, surface, wet = refs[10:14]
    outs, (state_v, sems) = refs[14:23], refs[23:]
    copies = [
        pltpu.make_async_copy(src, dst, sems.at[n])
        for n, (src, dst) in enumerate(zip((state, *args), (state_v, *outs)))
    ]
    for copy in copies:
        copy.start()
    copies[0].wait()
    for ref, half in zip((x1, x2), halves_of([state_v[0, :, r, :] for r in range(state_v.shape[2])])):
        for i, value in enumerate(half):
            ref[i] = value
    surface[...] = state_v[0, 0]
    for copy in copies[1:]:
        copy.wait()
    mask, codes = outs[1], outs[2]
    wet[...] = jnp.where(is_sea(groups), mask[0].astype(F32), 1.0)
    for ref, half in zip((x1, x2), halves_of(lines_of(codes[0].astype(F32)))):
        for i, value in enumerate(half):
            ref[i, 0:1, :] = value


def remap_kernel(groups, coupling, mixing, courant, matrices, weights, sources, targets, *refs):
    coef, table, col0, wide, pick, chosen, *outs, blk = refs
    count, margins = pick.shape
    slot = lax.broadcasted_iota(jnp.int32, (count, margins), 0)
    pick[...] = (slot == sources[...]).astype(F32).astype(BF16)
    me = lax.axis_index("comp")
    air_count = MEMBERS * groups // 4
    for n in range(MEMBERS):
        ocean = jnp.where(lax.rem(me, MEMBERS) == n, air_count + lax.div(me, MEMBERS), me)
        partner = jnp.where(me < air_count, ocean, MEMBERS * (me - air_count) + n)
        hit = (targets[...] == slot + partner * count).astype(F32).astype(BF16)
        chosen[n * count : (n + 1) * count] = jnp.concatenate([hit, hit], axis=1)
    wide[...] = weights[0].reshape(wide.shape).astype(F32)
    payload(coupling[0], wide, pick, chosen, outs, blk)
    m, c = column(mixing[...]), column(courant[...])
    coef[0], coef[1], coef[2] = 1.0 - 4.0 * m - c, m + c, m
    branches, fields = matrices.shape[1:3]
    flat = matrices[0].reshape(branches * fields, fields)
    col0[...] = flat[:, :1].reshape(branches, fields, 1)
    flat = jnp.where(lax.broadcasted_iota(jnp.int32, flat.shape, 1) == 0, 0.0, flat)
    high, low = split_high_low(flat)
    table[...] = jnp.concatenate([high, high, low], axis=1)


def surface_kernel(groups, late, *refs):
    recs, (surface_ref, mask_ref, *refs) = refs[:MEMBERS], refs[MEMBERS:]
    ns_ref, flux_ref, *ends, blk = refs if late else refs[1:]
    rows, width = ns_ref.shape
    block = blk.shape[-1]
    per_row = width // block
    total = recs[0][...]
    for rec in recs[1:]:
        total = total + rec[...]
    blk[...] = total
    received = jnp.concatenate(
        [blk[pl.ds(c, rows, stride=per_row), :] for c in range(per_row)], axis=1
    )
    surface = surface_ref[...]
    flux = mask_ref[0].astype(F32) * EXCHANGE * (received - surface)
    new = surface + jnp.where(is_sea(groups), -OCEAN_SHARE * received, flux)
    ns_ref[...] = new
    flux_ref[...] = flux
    for ref, half in zip(ends, halves_of([new[: rows // 2], new[rows // 2 :]])):
        ref[...] = half[0]


def substep(f, up, down, c0, cu, m):
    width = f.shape[1]
    sides = pltpu.roll(f, 1, 1) + pltpu.roll(f, width - 1, 1)
    return c0 * f + cu * up + m * (down + sides)


def sides(f):
    return pltpu.roll(f, 1, 1) + pltpu.roll(f, f.shape[1] - 1, 1)


def own_rows(f0, f1, f2, f3, coef, base1, base2):
    c0, cu, m = coef[0], coef[1], coef[2]
    g0 = c0 * f0 + m * (f1 + sides(f0))
    g1 = substep(f1, f0, f2, c0, cu, m)
    g2 = substep(f2, f1, f3, c0, cu, m)
    g3 = c0 * f3 + cu * f2 + m * sides(f3)
    rows = [
        c0 * g0 + m * (g1 + sides(g0)) + (cu * m) * f0,
        substep(g1, g0, g2, c0, cu, m),
        substep(g2, g1, g3, c0, cu, m),
        c0 * g3 + cu * g2 + m * sides(g3) + (cu * m) * f3,
    ]
    for ref, half in zip((base1, base2), halves_of(rows)):
        for i, value in enumerate(half):
            ref[i] = value


def start_kernel(x1, x2, coef, base1, base2):
    own_rows(*rows_of([x1[0], x1[1]], [x2[0], x2[1]]), coef, base1, base2)


def evolve_kernel(part1, part2, gain1, gain2, squashed, coef, base1, base2):
    half = part1.shape[0]
    lines = [squashed[r : r + 1, :] for r in range(half, 3 * half)]
    line1, line2 = halves_of(lines)
    inner = [part1[i] + gain1[i] * line1[i] for i in range(half)]
    outer = [part2[i] + gain2[i] * line2[i] for i in range(half)]
    own_rows(*rows_of(inner, outer), coef, base1, base2)


def branch_factor(col0, code, shape):
    factor = jnp.broadcast_to(col0[0], shape)
    for b in range(1, col0.shape[0]):
        factor = jnp.where(code == b, col0[b], factor)
    return factor


def fields_kernel(inner, late, base, y, coef, table, col0, codes, wet, after, *refs):
    part, part0, gain = refs[-3:]
    z, squashed = refs[:2] if late else (None, None)
    half, fields, width = base.shape
    at_top = is_odd() if inner else jnp.logical_not(is_odd())
    c0, cu, m = coef[0], coef[1], coef[2]
    q = jnp.where(at_top, cu, m)
    branches = table.shape[0] // fields

    def halo_row(top, bottom):
        value = jnp.where(at_top, y[top], y[bottom])
        if not late:
            return value
        code = jnp.where(at_top, z[top, 0:1], z[bottom, 0:1]).astype(jnp.int32)
        line = jnp.where(
            at_top, squashed[top : top + 1, :], squashed[3 * half + bottom : 3 * half + bottom + 1, :]
        )
        return value + branch_factor(col0, code, (fields, width)) * (value[:1] * line)

    near, far = halo_row(1, 0), halo_row(0, 1)
    edge = (2.0 * q * c0) * near + (2.0 * q * m) * sides(near) + (q * q) * far
    next_to_edge = (q * q) * near
    halos = jnp.where(at_top, edge, next_to_edge), jnp.where(at_top, next_to_edge, edge)
    code_lines = halves_of([codes[0, r : r + 1, :] for r in range(2 * half)])[0 if inner else 1]
    wet_lines = halves_of([wet[r : r + 1, :] for r in range(2 * half)])[0 if inner else 1]
    top_field = lax.broadcasted_iota(jnp.int32, (fields, width), 0) == 0
    for i in range(half):
        f = base[i] + halos[i]
        high, low = split_high_low(jnp.tanh(f))
        terms = jnp.dot(
            table[...], jnp.concatenate([high, low, high], axis=0), preferred_element_type=F32
        )
        tendency = terms[:fields]
        for b in range(1, branches):
            chosen = code_lines[i] == b
            tendency = jnp.where(chosen, terms[b * fields : (b + 1) * fields], tendency)
        part0[i : i + 1, :] = tendency[:1] * wet_lines[i]
        part[i] = jnp.where(top_field, 1.0, f + tendency) * wet_lines[i]
        gain[i] = branch_factor(col0, code_lines[i], (fields, width)) * wet_lines[i]


def field0(ns, e2, e1, coef, wet, part01, part02, gain1, gain2):
    c0, cu, m = coef[0, :1], coef[1, :1], coef[2, :1]
    odd = is_odd()
    first, last = e1[...], e2[...]
    f = jnp.concatenate(
        [jnp.where(odd, first, last), ns[...], jnp.where(odd, last, first)], axis=0
    )
    rows = f.shape[0]
    for _ in range(SUBSTEPS):
        f = substep(f, pltpu.roll(f, 1, 0), pltpu.roll(f, rows - 1, 0), c0, cu, m)
    f = f[SUBSTEPS : rows - SUBSTEPS]
    squashed = jnp.tanh(f)
    extra = (f.shape[0] - ns.shape[0]) // 2
    own = slice(extra, extra + ns.shape[0])
    part = jnp.concatenate(rows_of([part01[...]], [part02[...]]), axis=0)
    gain = jnp.concatenate(rows_of([gain1[:, 0, :]], [gain2[:, 0, :]]), axis=0)
    return part + gain * squashed[own] + f[own] * wet[...], squashed


def hand_kernel(
    groups, ns, e2, e1, coef, wet, part01, part02, gain1, gain2, flux, wide, pick, chosen, *refs
):
    surf, squashed, *outs, blk = refs
    surf[...], squashed[...] = field0(ns, e2, e1, coef, wet, part01, part02, gain1, gain2)
    payload(jnp.where(is_sea(groups), surf[...], flux[...]), wide, pick, chosen, outs, blk)


def close_kernel(
    groups, ns, e2, e1, coef, wet, part01, part02, gain1, gain2, flux, part1, part2, *refs
):
    new_state, new_coupling, surf, squashed = refs
    surf[...], squashed[...] = field0(ns, e2, e1, coef, wet, part01, part02, gain1, gain2)
    new_coupling[0] = jnp.where(is_sea(groups), surf[...], flux[...])
    half, fields, width = part1.shape
    top_field = lax.broadcasted_iota(jnp.int32, (SUBLANES, width), 0) == 0
    line1, line2 = halves_of([squashed[r : r + 1, :] for r in range(2 * half)])
    for h in range(0, fields, SUBLANES):
        some = slice(h, h + SUBLANES)
        for i in range(half):
            inner = part1[i, some] + gain1[i, some] * line1[i]
            outer = part2[i, some] + gain2[i, some] * line2[i]
            for r, done in zip((i, half + i), rows_of([inner], [outer])):
                if h == 0:
                    done = jnp.where(top_field, surf[r : r + 1, :], done)
                new_state[0, some, r, :] = done


def call(kernel, name, outs, args, scratch=(), in_specs=None, flops=0):
    moved = sum(a.size * a.dtype.itemsize for a in list(args) + list(outs))
    return pl.pallas_call(
        kernel,
        name=name,
        out_shape=outs,
        in_specs=in_specs or [VMEM] * len(args),
        out_specs=[VMEM] * len(outs),
        scratch_shapes=list(scratch),
        compiler_params=PARAMS,
        cost_estimate=pl.CostEstimate(flops=flops, bytes_accessed=moved, transcendentals=0),
    )(*args)


def on_device(
    state, coupling, land_mask, codes, mixing, courant, matrices, weights, sources, targets
):
    groups = lax.axis_size("comp")
    tiles = lax.axis_size("tile")
    _, fields, rows, width = state.shape
    _, margins, band, block = weights.shape
    count = rows * width // block
    half = rows // 2
    branches = matrices.shape[1]
    shape = jax.ShapeDtypeStruct

    halves = [shape((half, fields, width), F32)] * 2
    payloads = [shape((count, block), F32)] * MEMBERS
    blocks = pltpu.VMEM((count, block), F32)
    args = (
        state, coupling, land_mask, codes, mixing, courant, matrices, weights, sources, targets
    )
    x1, x2, surface, wet, handed, mask, codes, *raw = call(
        functools.partial(load_kernel, groups),
        "load",
        halves + [shape((rows, width), F32)] * 2 + [shape(a.shape, a.dtype) for a in args[1:]],
        [pltpu.with_memory_space_constraint(a, pltpu.HBM) for a in args],
        [pltpu.VMEM(state.shape, F32), pltpu.SemaphoreType.DMA((len(args),))],
        [pl.BlockSpec(memory_space=pltpu.HBM)] * len(args),
    )
    tables = [
        shape((3, fields, 1), F32),
        shape((branches * fields, 3 * fields), BF16),
        shape((branches, fields, 1), F32),
        shape((margins * band, block), F32),
        shape((count, margins), BF16),
        shape((MEMBERS * count, 2 * margins), BF16),
    ]
    coef, table, col0, wide, pick, chosen, *sent = call(
        functools.partial(remap_kernel, groups),
        "remap",
        tables + payloads,
        (handed, *raw),
        [blocks],
    )
    for interval in range(INTERVALS):
        y1 = lax.ppermute(x1, "tile", inner_pairs(tiles))
        y2 = lax.ppermute(x2, "tile", outer_pairs(tiles))
        recs = [
            lax.ppermute(value, ("comp", "tile"), partner_pairs(groups, tiles, member))
            for member, value in enumerate(sent)
        ]
        late, last = interval > 0, interval == INTERVALS - 1
        line, pair = shape((rows, width), F32), shape((half, width), F32)
        if late:
            base1, base2 = call(
                evolve_kernel, "evolve", halves, (part1, part2, gain1, gain2, squashed, coef)
            )
        else:
            base1, base2 = call(start_kernel, "start", halves, (x1, x2, coef))
        kept = (coef, table, col0, codes, wet)
        part1, part01, gain1 = call(
            functools.partial(fields_kernel, True, late),
            "inner",
            [halves[0], pair, halves[0]],
            (base1, y1, *kept, base1) + ((z1, squashed) if late else ()),
        )
        ns, flux, *edges = call(
            functools.partial(surface_kernel, groups, late),
            "surface",
            [line] * 2 + ([pair] * 2 if last else []),
            (*recs, surface, mask) + (() if late else (part01,)),
            [blocks],
        )
        d1, d2 = edges if last else (ns, ns)
        e1 = lax.ppermute(d1, "tile", inner_pairs(tiles))
        e2 = lax.ppermute(d2, "tile", outer_pairs(tiles))
        part2, part02, gain2 = call(
            functools.partial(fields_kernel, False, late),
            "outer",
            [halves[0], pair, halves[0]],
            (base2, y2, *kept, part01 if late else ns) + ((z2, squashed) if late else ()),
            flops=4_000_000_000,
        )
        z1, z2 = y1, y2
        x1, x2 = part1, part2
        common = (ns, e2, e1, coef, wet, part01, part02, gain1, gain2, flux)
        if not last:
            surface, squashed, *sent = call(
                functools.partial(hand_kernel, groups),
                "hand",
                [line, shape((2 * rows, width), F32)] + payloads,
                (*common, wide, pick, chosen),
                [blocks],
                flops=20_000_000_000,
            )
        else:
            new_state, new_coupling = call(
                functools.partial(close_kernel, groups),
                "close",
                [shape(state.shape, F32), shape(coupling.shape, F32)],
                (*common, part1, part2),
                [pltpu.VMEM((rows, width), F32)] * 2,
            )
    return new_state, new_coupling


def solution(mesh):
    placed = (
        P("comp", None, "tile", None),
        P("comp", "tile", None),
        P("comp", "tile", None),
        P("comp", "tile", None),
        P("comp", None),
        P("comp", None),
        P("comp", None, None, None),
        P("comp", "tile", None, None),
        P("comp", "tile"),
        P("comp", "tile"),
    )
    return jax.shard_map(
        on_device,
        mesh=mesh,
        in_specs=placed,
        out_specs=(P("comp", None, "tile", None), P("comp", "tile", None)),
        check_vma=False,
    )
```

```python
import functools

import jax
import jax.numpy as jnp
from jax import lax
from jax.experimental import pallas as pl
from jax.experimental.pallas import tpu as pltpu
from jax.sharding import PartitionSpec as P

SUBSTEPS = 2
INTERVALS = 2
EXCHANGE = 0.5
OCEAN_SHARE = 0.3

F32 = jnp.float32
BF16 = jnp.bfloat16
VMEM = pl.BlockSpec(memory_space=pltpu.VMEM)
PARAMS = pltpu.CompilerParams(vmem_limit_bytes=40 * 1024 * 1024)


MEMBERS = 3
SUBLANES = 8
BAND = 8


def partner_pairs(groups, tiles, member):
    air_count = MEMBERS * groups // 4
    pairs = []
    for group in range(groups):
        ocean = group >= air_count
        if ocean:
            partner = MEMBERS * (group - air_count) + member
        else:
            partner = air_count + group // MEMBERS if group % MEMBERS == member else group
        for tile in range(tiles):
            other = tile ^ 1 if partner == group else tile
            pairs.append((group * tiles + tile, partner * tiles + other))
    return pairs


def inner_pairs(count):
    return [(tile, tile ^ 1) for tile in range(count)]


def outer_pairs(count):
    return [(tile, (tile + 1) % count if tile % 2 else (tile - 1) % count) for tile in range(count)]


def split_high_low(value):
    high = value.astype(BF16)
    low = (value - high.astype(F32)).astype(BF16)
    return high, low


def products(handed, picked_by, weight, blk_ref):
    rows, width = handed.shape
    count, block = blk_ref.shape
    per_row = width // block
    for c in range(per_row):
        blk_ref[pl.ds(c, rows, stride=per_row), :] = handed[:, c * block : (c + 1) * block]
    picked = picked_by(blk_ref[...].astype(BF16))
    total = weight(0) * picked
    for j in range(1, BAND):
        total = total + weight(j) * pltpu.roll(picked, block - j, 1)
    return total


def column(row):
    n = row.shape[1]
    diagonal = lax.broadcasted_iota(jnp.int32, (n, n), 0) == lax.broadcasted_iota(jnp.int32, (n, n), 1)
    return jnp.sum(jnp.where(diagonal, row, 0.0), axis=1, keepdims=True)


def is_odd():
    return lax.rem(lax.axis_index("tile"), 2) == 1


def is_sea(groups):
    return lax.axis_index("comp") >= MEMBERS * groups // 4


def halves_of(rows):
    half = len(rows) // 2
    head, tail = rows[:half], rows[half:]
    inner = [jnp.where(is_odd(), h, t) for h, t in zip(head, tail)]
    outer = [jnp.where(is_odd(), t, h) for h, t in zip(head, tail)]
    return inner, outer


def rows_of(inner, outer):
    head = [jnp.where(is_odd(), i, o) for i, o in zip(inner, outer)]
    tail = [jnp.where(is_odd(), o, i) for i, o in zip(inner, outer)]
    return head + tail


def lines_of(lines):
    return [lines[r : r + 1] for r in range(lines.shape[0])]


def load_kernel(groups, *refs):
    state, *args = refs[:10]
    x1, x2, surface, wet = refs[10:14]
    outs, (state_v, sems) = refs[14:23], refs[23:]
    copies = [
        pltpu.make_async_copy(src, dst, sems.at[n])
        for n, (src, dst) in enumerate(zip((state, *args), (state_v, *outs)))
    ]
    for copy in copies:
        copy.start()
    copies[0].wait()
    for ref, half in zip((x1, x2), halves_of([state_v[0, 1:, r, :] for r in range(state_v.shape[2])])):
        for i, value in enumerate(half):
            ref[:, i, :] = value
    surface[...] = state_v[0, 0]
    for copy in copies[1:]:
        copy.wait()
    wet[...] = jnp.where(is_sea(groups), outs[1][0].astype(F32), 1.0)


def all_fields(x, i):
    width = x.shape[2]
    if x.shape[0] % SUBLANES:
        cut = SUBLANES - 1
        top = jnp.concatenate([jnp.zeros((1, width), F32), x[:cut, i, :]], axis=0)
        return jnp.concatenate([top, x[cut:, i, :]], axis=0)
    return x[:, i, :]


def remap_kernel(groups, coupling, mixing, courant, matrices, weights, sources, targets, *refs):
    coef, table, col0, wide, pick, *outs, blk = refs
    count, margins = pick.shape
    slot = lax.broadcasted_iota(jnp.int32, (count, margins), 0)
    pick[...] = (slot == sources[...]).astype(F32).astype(BF16)
    me = lax.axis_index("comp")
    air_count = MEMBERS * groups // 4
    wide[...] = weights[0].reshape(wide.shape).astype(F32)
    contrib = products(
        coupling[0],
        lambda blocks: lax.dot_general(
            pick[...], blocks, (((0,), (0,)), ((), ())), preferred_element_type=F32
        ),
        lambda j: wide[pl.ds(j, margins, stride=BAND), :],
        blk,
    )
    both = jnp.concatenate(split_high_low(contrib), axis=0)
    chosen = []
    for n in range(MEMBERS):
        ocean = jnp.where(lax.rem(me, MEMBERS) == n, air_count + lax.div(me, MEMBERS), me)
        partner = jnp.where(me < air_count, ocean, MEMBERS * (me - air_count) + n)
        hit = (targets[...] == slot + partner * count).astype(F32).astype(BF16)
        chosen.append(jnp.concatenate([hit, hit], axis=1))
    blocks = jnp.dot(jnp.concatenate(chosen, axis=0), both, preferred_element_type=F32)
    for n, out in enumerate(outs):
        out[...] = blocks[n * count : (n + 1) * count]
    m, c = column(mixing[...]), column(courant[...])
    coef[0], coef[1], coef[2] = 1.0 - 4.0 * m - c, m + c, m
    branches, fields = matrices.shape[1:3]
    flat = matrices[0].reshape(branches * fields, fields)
    col0[...] = flat[:, :1].reshape(branches, fields, 1)
    flat = jnp.where(lax.broadcasted_iota(jnp.int32, flat.shape, 1) == 0, 0.0, flat)
    high, low = split_high_low(flat)
    table[...] = jnp.concatenate([high, high, low], axis=1)


def sort_kernel(groups, targets, wide, pick, after, wide_out, pick_out):
    count, margins = pick.shape
    me = lax.axis_index("comp")
    air_count = MEMBERS * groups // 4
    first = jnp.where(is_sea(groups), MEMBERS * (me - air_count), air_count + lax.div(me, MEMBERS))
    place = targets[...] - first * count
    here = lax.broadcasted_iota(jnp.int32, (margins, margins), 0)
    there = lax.broadcasted_iota(jnp.int32, (margins, margins), 1)
    level = place.astype(F32)
    same = jnp.logical_and(column(level) == level, here < there)
    rank = jnp.sum(jnp.where(same, 1.0, 0.0), axis=0, keepdims=True).astype(jnp.int32)
    place = place + jnp.where(is_sea(groups), 0, rank * count)
    order = (here == place).astype(F32).astype(BF16)
    pick_out[...] = lax.dot_general(
        order, pick[...], (((1,), (1,)), ((), ())), preferred_element_type=F32
    ).astype(BF16)
    for j in range(BAND):
        band = wide[pl.ds(j, margins, stride=BAND), :].astype(BF16)
        wide_out[j] = jnp.dot(order, band, preferred_element_type=F32)


def surface_kernel(groups, *refs):
    recs, refs = refs[:MEMBERS], refs[MEMBERS:]
    surface_ref, mask_ref, _, ns_ref, flux_ref, *ends, blk = refs
    rows, width = ns_ref.shape
    block = blk.shape[-1]
    per_row = width // block
    total = recs[0][...]
    for rec in recs[1:]:
        total = total + rec[...]
    blk[...] = total
    received = jnp.concatenate(
        [blk[pl.ds(c, rows, stride=per_row), :] for c in range(per_row)], axis=1
    )
    surface = surface_ref[...]
    flux = mask_ref[0].astype(F32) * EXCHANGE * (received - surface)
    new = surface + jnp.where(is_sea(groups), -OCEAN_SHARE * received, flux)
    ns_ref[...] = new
    flux_ref[...] = flux
    for ref, half in zip(ends, halves_of([new[: rows // 2], new[rows // 2 :]])):
        ref[...] = half[0]


def substep(f, up, down, c0, cu, m):
    width = f.shape[1]
    sides = pltpu.roll(f, 1, 1) + pltpu.roll(f, width - 1, 1)
    return c0 * f + cu * up + m * (down + sides)


def sides(f):
    return pltpu.roll(f, 1, 1) + pltpu.roll(f, f.shape[1] - 1, 1)


def own_rows(f0, f1, f2, f3, coef, base1, base2):
    c0, cu, m = coef[0], coef[1], coef[2]
    g0 = c0 * f0 + m * (f1 + sides(f0))
    g1 = substep(f1, f0, f2, c0, cu, m)
    g2 = substep(f2, f1, f3, c0, cu, m)
    g3 = c0 * f3 + cu * f2 + m * sides(f3)
    rows = [
        c0 * g0 + m * (g1 + sides(g0)) + (cu * m) * f0,
        substep(g1, g0, g2, c0, cu, m),
        substep(g2, g1, g3, c0, cu, m),
        c0 * g3 + cu * g2 + m * sides(g3) + (cu * m) * f3,
    ]
    for ref, half in zip((base1, base2), halves_of(rows)):
        for i, value in enumerate(half):
            ref[i] = value


def start_kernel(x1, x2, coef, col0, codes, wet, base1, base2, gain1, gain2):
    inner, outer = ([all_fields(x, i) for i in range(x.shape[1])] for x in (x1, x2))
    own_rows(*rows_of(inner, outer), coef, base1, base2)
    shape = gain1.shape[1:]
    rows = [
        branch_factor(col0, code, shape) * line
        for code, line in zip(lines_of(codes[0]), lines_of(wet[...]))
    ]
    for ref, half in zip((gain1, gain2), halves_of(rows)):
        for i, value in enumerate(half):
            ref[i] = value


def evolve_kernel(part1, part2, gain1, gain2, ns, e2, e1, coef, base1, base2, squashed):
    squashed[...] = jnp.tanh(field0_rows(ns, e2[...], e1[...], coef))
    half, fields, _ = gain1.shape
    line1, line2 = halves_of([squashed[r : r + 1, :] for r in range(half, 3 * half)])
    inner = [part1[:fields, i, :] + gain1[i] * line1[i] for i in range(half)]
    outer = [part2[:fields, i, :] + gain2[i] * line2[i] for i in range(half)]
    own_rows(*rows_of(inner, outer), coef, base1, base2)


def branch_factor(col0, code, shape):
    factor = jnp.broadcast_to(col0[0], shape)
    for b in range(1, col0.shape[0]):
        factor = jnp.where(code == b, col0[b], factor)
    return factor


def fields_kernel(inner, late, base, y, after, coef, table, codes, wet, *refs):
    part, part0 = refs[-2:]
    col0, squashed = refs[:2] if late else (None, None)
    half, fields, width = base.shape
    at_top = is_odd() if inner else jnp.logical_not(is_odd())
    c0, cu, m = coef[0], coef[1], coef[2]
    q = jnp.where(at_top, cu, m)
    branches = table.shape[0] // fields

    def halo_row(top, bottom):
        if not late:
            return jnp.where(at_top, all_fields(y, top), all_fields(y, bottom))
        value = jnp.where(at_top, y[:fields, top, :], y[:fields, bottom, :])
        code = jnp.where(at_top, y[fields:, top, :], y[fields:, bottom, :]).astype(jnp.int32)
        line = jnp.where(
            at_top, squashed[top : top + 1, :], squashed[3 * half + bottom : 3 * half + bottom + 1, :]
        )
        return value + branch_factor(col0, code, (fields, width)) * (value[:1] * line)

    near, far = halo_row(1, 0), halo_row(0, 1)
    edge = (2.0 * q * c0) * near + (2.0 * q * m) * sides(near) + (q * q) * far
    next_to_edge = (q * q) * near
    halos = jnp.where(at_top, edge, next_to_edge), jnp.where(at_top, next_to_edge, edge)
    code_lines = halves_of([codes[0, r : r + 1, :] for r in range(2 * half)])[0 if inner else 1]
    wet_lines = halves_of([wet[r : r + 1, :] for r in range(2 * half)])[0 if inner else 1]
    top_field = lax.broadcasted_iota(jnp.int32, (fields, width), 0) == 0
    for i in range(half):
        f = base[i] + halos[i]
        high, low = split_high_low(jnp.tanh(f))
        terms = jnp.dot(
            table[...], jnp.concatenate([high, low, high], axis=0), preferred_element_type=F32
        )
        tendency = terms[:fields]
        for b in range(1, branches):
            chosen = code_lines[i] == b
            tendency = jnp.where(chosen, terms[b * fields : (b + 1) * fields], tendency)
        part0[i : i + 1, :] = tendency[:1] * wet_lines[i]
        part[:fields, i, :] = jnp.where(top_field, 1.0, f + tendency) * wet_lines[i]
        part[fields:, i, :] = code_lines[i].astype(F32)


def field0_rows(ns, e2, e1, coef):
    c0, cu, m = coef[0, :1], coef[1, :1], coef[2, :1]
    odd = is_odd()
    f = jnp.concatenate([jnp.where(odd, e1, e2), ns[...], jnp.where(odd, e2, e1)], axis=0)
    rows = f.shape[0]
    for _ in range(SUBSTEPS):
        f = substep(f, pltpu.roll(f, 1, 0), pltpu.roll(f, rows - 1, 0), c0, cu, m)
    return f[SUBSTEPS : rows - SUBSTEPS]


def field0(ns, e2, e1, coef, wet, part01, part02, gain1, gain2):
    odd = is_odd()
    above, below = jnp.where(odd, e1[...], e2[...])[-SUBSTEPS:], jnp.where(odd, e2[...], e1[...])[:SUBSTEPS]
    f = field0_rows(ns, jnp.where(odd, below, above), jnp.where(odd, above, below), coef)
    squashed = jnp.tanh(f)
    part = jnp.concatenate(rows_of([part01[...]], [part02[...]]), axis=0)
    gain = jnp.concatenate(rows_of([gain1[:, 0, :]], [gain2[:, 0, :]]), axis=0)
    return part + gain * squashed + f * wet[...], squashed


def hand_kernel(
    groups, ns, e1, e2, coef, wet, part01, part02, gain1, gain2, flux, wide, pick, *refs
):
    surf, *outs, blk = refs
    surf[...], _ = field0(ns, e2, e1, coef, wet, part01, part02, gain1, gain2)
    sea = is_sea(groups)
    contrib = products(
        jnp.where(sea, surf[...], flux[...]),
        lambda blocks: jnp.dot(pick[...], blocks, preferred_element_type=F32),
        lambda j: wide[j],
        blk,
    )
    count = blk.shape[0]
    thirds = [contrib[n * count : (n + 1) * count] for n in range(MEMBERS)]
    member = lax.rem(lax.axis_index("comp"), MEMBERS)
    for n, (out, third) in enumerate(zip(outs, thirds)):
        out[...] = jnp.where(sea, third, jnp.where(member == n, sum(thirds), 0.0))


def close_kernel(
    groups, ns, e2, e1, coef, wet, part01, part02, gain1, gain2, flux, part1, part2, *refs
):
    new_state, new_coupling, surf, squashed = refs
    surf[...], squashed[...] = field0(ns, e2, e1, coef, wet, part01, part02, gain1, gain2)
    new_coupling[0] = jnp.where(is_sea(groups), surf[...], flux[...])
    half, fields, width = gain1.shape
    top_field = lax.broadcasted_iota(jnp.int32, (SUBLANES, width), 0) == 0
    line1, line2 = halves_of([squashed[r : r + 1, :] for r in range(2 * half)])
    for h in range(0, fields, SUBLANES):
        some = slice(h, h + SUBLANES)
        for i in range(half):
            inner = part1[some, i, :] + gain1[i, some] * line1[i]
            outer = part2[some, i, :] + gain2[i, some] * line2[i]
            for r, done in zip((i, half + i), rows_of([inner], [outer])):
                if h == 0:
                    done = jnp.where(top_field, surf[r : r + 1, :], done)
                new_state[0, some, r, :] = done


def call(kernel, name, outs, args, scratch=(), in_specs=None, flops=0):
    moved = sum(a.size * a.dtype.itemsize for a in list(args) + list(outs))
    return pl.pallas_call(
        kernel,
        name=name,
        out_shape=outs,
        in_specs=in_specs or [VMEM] * len(args),
        out_specs=[VMEM] * len(outs),
        scratch_shapes=list(scratch),
        compiler_params=PARAMS,
        cost_estimate=pl.CostEstimate(flops=flops, bytes_accessed=moved, transcendentals=0),
    )(*args)


def fields_half(late, parts, kept, inner, base, y, after, *rest):
    return call(
        functools.partial(fields_kernel, inner, late),
        "inner" if inner else "outer",
        parts,
        (base, y, after, *kept, *rest),
        flops=0 if inner else 4_000_000_000,
    )


def on_device(
    state, coupling, land_mask, codes, mixing, courant, matrices, weights, sources, targets
):
    groups = lax.axis_size("comp")
    tiles = lax.axis_size("tile")
    _, fields, rows, width = state.shape
    _, margins, band, block = weights.shape
    count = rows * width // block
    half = rows // 2
    branches = matrices.shape[1]
    shape = jax.ShapeDtypeStruct

    halves = [shape((half, fields, width), F32)] * 2
    payloads = [shape((count, block), F32)] * MEMBERS
    blocks = pltpu.VMEM((count, block), F32)
    args = (
        state, coupling, land_mask, codes, mixing, courant, matrices, weights, sources, targets
    )
    x1, x2, surface, wet, handed, mask, codes, *raw = call(
        functools.partial(load_kernel, groups),
        "load",
        [shape((fields - 1, half, width), F32)] * 2
        + [shape((rows, width), F32)] * 2
        + [shape(a.shape, a.dtype) for a in args[1:]],
        [pltpu.with_memory_space_constraint(a, pltpu.HBM) for a in args],
        [pltpu.VMEM(state.shape, F32), pltpu.SemaphoreType.DMA((len(args),))],
        [pl.BlockSpec(memory_space=pltpu.HBM)] * len(args),
    )
    tables = [
        shape((3, fields, 1), F32),
        shape((branches * fields, 3 * fields), BF16),
        shape((branches, fields, 1), F32),
        shape((margins * band, block), F32),
        shape((count, margins), BF16),
    ]
    coef, table, col0, wide, pick, *sent = call(
        functools.partial(remap_kernel, groups),
        "remap",
        tables + payloads,
        (handed, *raw),
        [blocks],
    )
    for interval in range(INTERVALS):
        y1 = lax.ppermute(x1, "tile", inner_pairs(tiles))
        y2 = lax.ppermute(x2, "tile", outer_pairs(tiles))
        recs = [
            lax.ppermute(value, ("comp", "tile"), partner_pairs(groups, tiles, member))
            for member, value in enumerate(sent)
        ]
        late, last = interval > 0, interval == INTERVALS - 1
        line, pair = shape((rows, width), F32), shape((half, width), F32)
        if late:
            base1, base2, squashed = call(
                evolve_kernel,
                "evolve",
                halves + [shape((2 * rows, width), F32)],
                (part1, part2, gain1, gain2, ns, e2, e1, coef),
            )
        else:
            base1, base2, gain1, gain2 = call(
                start_kernel, "start", halves * 2, (x1, x2, coef, col0, codes, wet)
            )
            wide, pick = call(
                functools.partial(sort_kernel, groups),
                "sort",
                [shape((band, margins, block), F32), shape((margins, count), BF16)],
                (raw[-1], wide, pick, base1),
            )
        kept = (coef, table, codes, wet)
        parts = [shape((fields + 1, half, width), F32), pair]
        run_fields = functools.partial(fields_half, late, parts, kept)
        ns, flux, *edges = call(
            functools.partial(surface_kernel, groups),
            "surface",
            [line] * 2 + ([pair] * 2 if last else []),
            (*recs, surface, mask, pick),
            [blocks],
        )
        d1, d2 = edges if last else (ns, ns)
        e1 = lax.ppermute(d1, "tile", inner_pairs(tiles))
        e2 = lax.ppermute(d2, "tile", outer_pairs(tiles))
        if late:
            part2, part02 = run_fields(False, base2, y2, ns, col0, squashed)
            part1, part01 = run_fields(True, base1, y1, part02, col0, squashed)
        else:
            part2, part02 = run_fields(False, base2, y2, ns)
            part1, part01 = run_fields(True, base1, y1, part02)
        x1, x2 = part1, part2
        common = (ns, e2, e1, coef, wet, part01, part02, gain1, gain2, flux)
        if not last:
            surface, *sent = call(
                functools.partial(hand_kernel, groups),
                "hand",
                [line] + payloads,
                (ns, e1, e2, *common[3:], wide, pick),
                [blocks],
                flops=20_000_000_000,
            )
        else:
            new_state, new_coupling = call(
                functools.partial(close_kernel, groups),
                "close",
                [shape(state.shape, F32), shape(coupling.shape, F32)],
                (*common, part1, part2),
                [pltpu.VMEM((rows, width), F32)] * 2,
            )
    return new_state, new_coupling


def solution(mesh):
    placed = (
        P("comp", None, "tile", None),
        P("comp", "tile", None),
        P("comp", "tile", None),
        P("comp", "tile", None),
        P("comp", None),
        P("comp", None),
        P("comp", None, None, None),
        P("comp", "tile", None, None),
        P("comp", "tile"),
        P("comp", "tile"),
    )
    return jax.shard_map(
        on_device,
        mesh=mesh,
        in_specs=placed,
        out_specs=(P("comp", None, "tile", None), P("comp", "tile", None)),
        check_vma=False,
    )
```

```python
import functools

import jax
import jax.numpy as jnp
from jax import lax
from jax.experimental import pallas as pl
from jax.experimental.pallas import tpu as pltpu
from jax.sharding import PartitionSpec as P

SUBSTEPS = 2
INTERVALS = 2
EXCHANGE = 0.5
OCEAN_SHARE = 0.3

F32 = jnp.float32
BF16 = jnp.bfloat16
VMEM = pl.BlockSpec(memory_space=pltpu.VMEM)
HBM = pl.BlockSpec(memory_space=pltpu.HBM)
PARAMS = pltpu.CompilerParams(vmem_limit_bytes=40 * 1024 * 1024)


MEMBERS = 3
SUBLANES = 8
BAND = 8


def partner_pairs(groups, tiles, member):
    air_count = MEMBERS * groups // 4
    pairs = []
    for group in range(groups):
        ocean = group >= air_count
        if ocean:
            partner = MEMBERS * (group - air_count) + member
        else:
            partner = air_count + group // MEMBERS if group % MEMBERS == member else group
        for tile in range(tiles):
            other = tile ^ 1 if partner == group else tile
            pairs.append((group * tiles + tile, partner * tiles + other))
    return pairs


def inner_pairs(count):
    return [(tile, tile ^ 1) for tile in range(count)]


def outer_pairs(count):
    return [(tile, (tile + 1) % count if tile % 2 else (tile - 1) % count) for tile in range(count)]


def split_high_low(value):
    high = value.astype(BF16)
    low = (value - high.astype(F32)).astype(BF16)
    return high, low


def products(handed, picked_by, weight, blk_ref):
    rows, width = handed.shape
    count, block = blk_ref.shape
    per_row = width // block
    for c in range(per_row):
        blk_ref[pl.ds(c, rows, stride=per_row), :] = handed[:, c * block : (c + 1) * block]
    picked = picked_by(blk_ref[...].astype(BF16))
    total = weight(0) * picked
    for j in range(1, BAND):
        total = total + weight(j) * pltpu.roll(picked, block - j, 1)
    return total


def column(row):
    n = row.shape[1]
    diagonal = lax.broadcasted_iota(jnp.int32, (n, n), 0) == lax.broadcasted_iota(jnp.int32, (n, n), 1)
    return jnp.sum(jnp.where(diagonal, row, 0.0), axis=1, keepdims=True)


def is_odd():
    return lax.rem(lax.axis_index("tile"), 2) == 1


def is_sea(groups):
    return lax.axis_index("comp") >= MEMBERS * groups // 4


def halves_of(rows):
    half = len(rows) // 2
    head, tail = rows[:half], rows[half:]
    inner = [jnp.where(is_odd(), h, t) for h, t in zip(head, tail)]
    outer = [jnp.where(is_odd(), t, h) for h, t in zip(head, tail)]
    return inner, outer


def rows_of(inner, outer):
    head = [jnp.where(is_odd(), i, o) for i, o in zip(inner, outer)]
    tail = [jnp.where(is_odd(), o, i) for i, o in zip(inner, outer)]
    return head + tail


def lines_of(lines):
    return [lines[r : r + 1] for r in range(lines.shape[0])]


def copy_all(pairs, sems):
    copies = [pltpu.make_async_copy(src, dst, sems.at[n]) for n, (src, dst) in enumerate(pairs)]
    for copy in copies:
        copy.start()
    return copies


def load_kernel(groups, state, sources, targets, coupling, weights, *refs):
    x1, x2, surface, pick, chosen, targets_v, coupling_v, weights_v, state_v, sources_v, sems = refs
    copies = copy_all(
        (
            (state, state_v),
            (sources, sources_v),
            (targets, targets_v),
            (coupling, coupling_v),
            (weights, weights_v),
        ),
        sems,
    )
    copies[1].wait()
    copies[2].wait()
    count, margins = pick.shape
    slot = lax.broadcasted_iota(jnp.int32, (count, margins), 0)
    pick[...] = (slot == sources_v[...]).astype(F32).astype(BF16)
    me = lax.axis_index("comp")
    air_count = MEMBERS * groups // 4
    for n in range(MEMBERS):
        ocean = jnp.where(lax.rem(me, MEMBERS) == n, air_count + lax.div(me, MEMBERS), me)
        partner = jnp.where(me < air_count, ocean, MEMBERS * (me - air_count) + n)
        hit = (targets_v[...] == slot + partner * count).astype(F32).astype(BF16)
        chosen[n * count : (n + 1) * count] = jnp.concatenate([hit, hit], axis=1)
    copies[0].wait()
    for ref, half in zip((x1, x2), halves_of([state_v[0, 1:, r, :] for r in range(state_v.shape[2])])):
        for i, value in enumerate(half):
            ref[:, i, :] = value
    surface[...] = state_v[0, 0]
    for copy in copies[3:]:
        copy.wait()


def all_fields(x, i):
    width = x.shape[2]
    if x.shape[0] % SUBLANES:
        cut = SUBLANES - 1
        top = jnp.concatenate([jnp.zeros((1, width), F32), x[:cut, i, :]], axis=0)
        return jnp.concatenate([top, x[cut:, i, :]], axis=0)
    return x[:, i, :]


def remap_kernel(coupling, weights, pick, chosen, wide, *refs):
    outs, blk = refs[:-1], refs[-1]
    count, margins = pick.shape
    wide[...] = weights[0].reshape(wide.shape).astype(F32)
    contrib = products(
        coupling[0],
        lambda blocks: lax.dot_general(
            pick[...], blocks, (((0,), (0,)), ((), ())), preferred_element_type=F32
        ),
        lambda j: wide[pl.ds(j, margins, stride=BAND), :],
        blk,
    )
    both = jnp.concatenate(split_high_low(contrib), axis=0)
    blocks = jnp.dot(chosen[...], both, preferred_element_type=F32)
    for n, out in enumerate(outs):
        out[...] = blocks[n * count : (n + 1) * count]


def sort_kernel(groups, targets, wide, pick, *refs):
    args, refs = refs[:5], refs[5:]
    wide_out, pick_out, mask, codes, wet, coef, table, col0, mixing, courant, matrices, sems = refs
    copies = copy_all(tuple(zip(args, (mask, codes, mixing, courant, matrices))), sems)
    count, margins = pick.shape
    me = lax.axis_index("comp")
    air_count = MEMBERS * groups // 4
    first = jnp.where(is_sea(groups), MEMBERS * (me - air_count), air_count + lax.div(me, MEMBERS))
    place = targets[...] - first * count
    here = lax.broadcasted_iota(jnp.int32, (margins, margins), 0)
    there = lax.broadcasted_iota(jnp.int32, (margins, margins), 1)
    level = place.astype(F32)
    same = jnp.logical_and(column(level) == level, here < there)
    rank = jnp.sum(jnp.where(same, 1.0, 0.0), axis=0, keepdims=True).astype(jnp.int32)
    place = place + jnp.where(is_sea(groups), 0, rank * count)
    order = (here == place).astype(F32).astype(BF16)
    pick_out[...] = lax.dot_general(
        order, pick[...], (((1,), (1,)), ((), ())), preferred_element_type=F32
    ).astype(BF16)
    for j in range(BAND):
        band = wide[pl.ds(j, margins, stride=BAND), :].astype(BF16)
        wide_out[j] = jnp.dot(order, band, preferred_element_type=F32)
    for copy in copies:
        copy.wait()
    wet[...] = jnp.where(is_sea(groups), mask[0].astype(F32), 1.0)
    m, c = column(mixing[...]), column(courant[...])
    coef[0], coef[1], coef[2] = 1.0 - 4.0 * m - c, m + c, m
    branches, fields = matrices.shape[1:3]
    flat = matrices[0].reshape(branches * fields, fields)
    col0[...] = flat[:, :1].reshape(branches, fields, 1)
    flat = jnp.where(lax.broadcasted_iota(jnp.int32, flat.shape, 1) == 0, 0.0, flat)
    high, low = split_high_low(flat)
    table[...] = jnp.concatenate([high, high, low], axis=1)


def surface_kernel(groups, *refs):
    recs, refs = refs[:MEMBERS], refs[MEMBERS:]
    surface_ref, mask_ref, _, ns_ref, flux_ref, *ends, blk = refs
    rows, width = ns_ref.shape
    block = blk.shape[-1]
    per_row = width // block
    total = recs[0][...]
    for rec in recs[1:]:
        total = total + rec[...]
    blk[...] = total
    received = jnp.concatenate(
        [blk[pl.ds(c, rows, stride=per_row), :] for c in range(per_row)], axis=1
    )
    surface = surface_ref[...]
    flux = mask_ref[0].astype(F32) * EXCHANGE * (received - surface)
    new = surface + jnp.where(is_sea(groups), -OCEAN_SHARE * received, flux)
    ns_ref[...] = new
    flux_ref[...] = flux
    for ref, half in zip(ends, halves_of([new[: rows // 2], new[rows // 2 :]])):
        ref[...] = half[0]


def substep(f, up, down, c0, cu, m):
    width = f.shape[1]
    sides = pltpu.roll(f, 1, 1) + pltpu.roll(f, width - 1, 1)
    return c0 * f + cu * up + m * (down + sides)


def sides(f):
    return pltpu.roll(f, 1, 1) + pltpu.roll(f, f.shape[1] - 1, 1)


def own_rows(f0, f1, f2, f3, coef, base1, base2):
    c0, cu, m = coef[0], coef[1], coef[2]
    g0 = c0 * f0 + m * (f1 + sides(f0))
    g1 = substep(f1, f0, f2, c0, cu, m)
    g2 = substep(f2, f1, f3, c0, cu, m)
    g3 = c0 * f3 + cu * f2 + m * sides(f3)
    rows = [
        c0 * g0 + m * (g1 + sides(g0)) + (cu * m) * f0,
        substep(g1, g0, g2, c0, cu, m),
        substep(g2, g1, g3, c0, cu, m),
        c0 * g3 + cu * g2 + m * sides(g3) + (cu * m) * f3,
    ]
    for ref, half in zip((base1, base2), halves_of(rows)):
        for i, value in enumerate(half):
            ref[i] = value


def start_kernel(x1, x2, coef, col0, codes, wet, base1, base2, gain1, gain2, gain0):
    inner, outer = ([all_fields(x, i) for i in range(x.shape[1])] for x in (x1, x2))
    own_rows(*rows_of(inner, outer), coef, base1, base2)
    shape = gain1.shape[1:]
    rows = [
        branch_factor(col0, code, shape) * line
        for code, line in zip(lines_of(codes[0]), lines_of(wet[...]))
    ]
    for ref, half in zip((gain1, gain2), halves_of(rows)):
        for i, value in enumerate(half):
            ref[i] = value
    for r, value in enumerate(rows):
        gain0[r : r + 1, :] = value[:1]


def evolve_kernel(part1, part2, gain1, gain2, ns, e2, e1, coef, base1, base2, squashed):
    squashed[...] = jnp.tanh(field0_rows(ns, e2[...], e1[...], coef))
    half, fields, _ = gain1.shape
    line1, line2 = halves_of([squashed[r : r + 1, :] for r in range(half, 3 * half)])
    inner = [part1[:fields, i, :] + gain1[i] * line1[i] for i in range(half)]
    outer = [part2[:fields, i, :] + gain2[i] * line2[i] for i in range(half)]
    own_rows(*rows_of(inner, outer), coef, base1, base2)


def branch_factor(col0, code, shape):
    factor = jnp.broadcast_to(col0[0], shape)
    for b in range(1, col0.shape[0]):
        factor = jnp.where(code == b, col0[b], factor)
    return factor


def fields_kernel(inner, late, base, y, after, coef, table, codes, wet, *refs):
    part, part0 = refs[-2:] if inner else refs[-3:-1]
    if not inner:
        none = jnp.zeros((SUBSTEPS, base.shape[2]), F32)
        refs[-1][...] = field0_rows(after, none, none, coef)
    col0, squashed = refs[:2] if late else (None, None)
    half, fields, width = base.shape
    at_top = is_odd() if inner else jnp.logical_not(is_odd())
    c0, cu, m = coef[0], coef[1], coef[2]
    q = jnp.where(at_top, cu, m)
    branches = table.shape[0] // fields

    def halo_row(top, bottom):
        if not late:
            return jnp.where(at_top, all_fields(y, top), all_fields(y, bottom))
        value = jnp.where(at_top, y[:fields, top, :], y[:fields, bottom, :])
        code = jnp.where(at_top, y[fields:, top, :], y[fields:, bottom, :]).astype(jnp.int32)
        line = jnp.where(
            at_top, squashed[top : top + 1, :], squashed[3 * half + bottom : 3 * half + bottom + 1, :]
        )
        return value + branch_factor(col0, code, (fields, width)) * (value[:1] * line)

    near, far = halo_row(1, 0), halo_row(0, 1)
    edge = (2.0 * q * c0) * near + (2.0 * q * m) * sides(near) + (q * q) * far
    next_to_edge = (q * q) * near
    halos = jnp.where(at_top, edge, next_to_edge), jnp.where(at_top, next_to_edge, edge)
    code_lines = halves_of([codes[0, r : r + 1, :] for r in range(2 * half)])[0 if inner else 1]
    wet_lines = halves_of([wet[r : r + 1, :] for r in range(2 * half)])[0 if inner else 1]
    top_field = lax.broadcasted_iota(jnp.int32, (fields, width), 0) == 0
    for i in range(half):
        f = base[i] + halos[i]
        high, low = split_high_low(jnp.tanh(f))
        terms = jnp.dot(
            table[...], jnp.concatenate([high, low, high], axis=0), preferred_element_type=F32
        )
        tendency = terms[:fields]
        for b in range(1, branches):
            chosen = code_lines[i] == b
            tendency = jnp.where(chosen, terms[b * fields : (b + 1) * fields], tendency)
        part0[i : i + 1, :] = tendency[:1] * wet_lines[i]
        if late:
            part[i] = (f + tendency) * wet_lines[i]
        else:
            part[:fields, i, :] = jnp.where(top_field, 1.0, f + tendency) * wet_lines[i]
            part[fields:, i, :] = code_lines[i].astype(F32)


def field0_rows(ns, e2, e1, coef):
    c0, cu, m = coef[0, :1], coef[1, :1], coef[2, :1]
    odd = is_odd()
    f = jnp.concatenate([jnp.where(odd, e1, e2), ns[...], jnp.where(odd, e2, e1)], axis=0)
    rows = f.shape[0]
    for _ in range(SUBSTEPS):
        f = substep(f, pltpu.roll(f, 1, 0), pltpu.roll(f, rows - 1, 0), c0, cu, m)
    return f[SUBSTEPS : rows - SUBSTEPS]


def field0(own, e2, e1, coef, wet, part01, part02, gain0):
    odd = is_odd()
    rows = own.shape[0]
    end = e1.shape[0]
    pick = lambda even, other, at: jnp.where(odd, other[at : at + 1, :], even[at : at + 1, :])
    near = jnp.concatenate([pick(e2, e1, end - 1), pick(e1, e2, 0)], axis=0)
    far = jnp.concatenate([pick(e2, e1, end - 2), pick(e1, e2, 1)], axis=0)
    c0, cu, m = coef[0, :1], coef[1, :1], coef[2, :1]
    q = jnp.concatenate([cu, m], axis=0)
    edge = (2.0 * q * c0) * near + (2.0 * q * m) * sides(near) + (q * q) * far
    inside = (q * q) * near
    f = own[...] + jnp.concatenate([edge[:1], inside, edge[1:]], axis=0)
    squashed = jnp.tanh(f)
    part = jnp.concatenate(rows_of([part01[...]], [part02[...]]), axis=0)
    return part + gain0[...] * squashed + f * wet[...], squashed


def hand_kernel(
    groups, own, e2, e1, coef, wet, part01, part02, gain0, flux, wide, pick, *refs
):
    surf, *outs, blk = refs
    surf[...], _ = field0(own, e2, e1, coef, wet, part01, part02, gain0)
    sea = is_sea(groups)
    contrib = products(
        jnp.where(sea, surf[...], flux[...]),
        lambda blocks: jnp.dot(pick[...], blocks, preferred_element_type=F32),
        lambda j: wide[j],
        blk,
    )
    count = blk.shape[0]
    thirds = [contrib[n * count : (n + 1) * count] for n in range(MEMBERS)]
    member = lax.rem(lax.axis_index("comp"), MEMBERS)
    for n, (out, third) in enumerate(zip(outs, thirds)):
        out[...] = jnp.where(sea, third, jnp.where(member == n, sum(thirds), 0.0))


def close_kernel(
    groups, own, e2, e1, coef, wet, part01, part02, gain0, flux, gain1, gain2, part1, part2, *refs
):
    new_state, new_coupling, surf, squashed, stage, handed, sems = refs
    surf[...], squashed[...] = field0(own, e2, e1, coef, wet, part01, part02, gain0)
    handed[0] = jnp.where(is_sea(groups), surf[...], flux[...])
    copies = [pltpu.make_async_copy(handed, new_coupling, sems.at[0])]
    copies[0].start()
    half, fields, width = gain1.shape
    top_field = lax.broadcasted_iota(jnp.int32, (SUBLANES, width), 0) == 0
    line1, line2 = halves_of([squashed[r : r + 1, :] for r in range(2 * half)])
    for h in range(0, fields, SUBLANES):
        some = slice(h, h + SUBLANES)
        for i in range(half):
            inner = part1[i, some] + gain1[i, some] * line1[i]
            outer = part2[i, some] + gain2[i, some] * line2[i]
            for r, done in zip((i, half + i), rows_of([inner], [outer])):
                if h == 0:
                    done = jnp.where(top_field, surf[r : r + 1, :], done)
                stage[0, some, r, :] = done
        window = pl.ds(h, SUBLANES)
        copies.append(
            pltpu.make_async_copy(
                stage.at[:, window], new_state.at[:, window], sems.at[len(copies)]
            )
        )
        copies[-1].start()
    for copy in copies:
        copy.wait()


def call(kernel, name, outs, args, scratch=(), in_specs=None, out_specs=None, flops=0):
    moved = sum(a.size * a.dtype.itemsize for a in list(args) + list(outs))
    return pl.pallas_call(
        kernel,
        name=name,
        out_shape=outs,
        in_specs=in_specs or [VMEM] * len(args),
        out_specs=out_specs or [VMEM] * len(outs),
        scratch_shapes=list(scratch),
        compiler_params=PARAMS,
        cost_estimate=pl.CostEstimate(flops=flops, bytes_accessed=moved, transcendentals=0),
    )(*args)


def fields_half(late, parts, kept, inner, base, y, after, *rest):
    return call(
        functools.partial(fields_kernel, inner, late),
        "inner" if inner else "outer",
        parts[:2] if inner else parts,
        (base, y, after, *kept, *rest),
        flops=0 if inner else 4_000_000_000,
    )


def on_device(
    state, coupling, land_mask, codes, mixing, courant, matrices, weights, sources, targets
):
    groups = lax.axis_size("comp")
    tiles = lax.axis_size("tile")
    _, fields, rows, width = state.shape
    _, margins, band, block = weights.shape
    count = rows * width // block
    half = rows // 2
    branches = matrices.shape[1]
    shape = jax.ShapeDtypeStruct

    halves = [shape((half, fields, width), F32)] * 2
    payloads = [shape((count, block), F32)] * MEMBERS
    blocks = pltpu.VMEM((count, block), F32)
    line, pair = shape((rows, width), F32), shape((half, width), F32)
    far = lambda args: [pltpu.with_memory_space_constraint(a, pltpu.HBM) for a in args]
    like = lambda args: [shape(a.shape, a.dtype) for a in args]
    room = lambda args: [pltpu.VMEM(a.shape, a.dtype) for a in args]
    x1, x2, surface, pick, chosen, targets, handed, raw = call(
        functools.partial(load_kernel, groups),
        "load",
        [shape((fields - 1, half, width), F32)] * 2
        + [line, shape((count, margins), BF16), shape((MEMBERS * count, 2 * margins), BF16)]
        + like((targets, coupling, weights)),
        far((state, sources, targets, coupling, weights)),
        room((state, sources)) + [pltpu.SemaphoreType.DMA((5,))],
        [HBM] * 5,
    )
    wide, *sent = call(
        remap_kernel,
        "remap",
        [shape((margins * band, block), F32)] + payloads,
        (handed, raw, pick, chosen),
        [blocks],
    )
    wide, pick, mask, codes, wet, coef, table, col0 = call(
        functools.partial(sort_kernel, groups),
        "sort",
        [shape((band, margins, block), F32), shape((margins, count), BF16)]
        + like((land_mask, codes))
        + [
            line,
            shape((3, fields, 1), F32),
            shape((branches * fields, 3 * fields), BF16),
            shape((branches, fields, 1), F32),
        ],
        (targets, wide, pick, *far((land_mask, codes, mixing, courant, matrices))),
        room((mixing, courant, matrices)) + [pltpu.SemaphoreType.DMA((5,))],
        [VMEM] * 3 + [HBM] * 5,
    )
    for interval in range(INTERVALS):
        y1 = lax.ppermute(x1, "tile", inner_pairs(tiles))
        y2 = lax.ppermute(x2, "tile", outer_pairs(tiles))
        recs = [
            lax.ppermute(value, ("comp", "tile"), partner_pairs(groups, tiles, member))
            for member, value in enumerate(sent)
        ]
        late, last = interval > 0, interval == INTERVALS - 1
        if late:
            base1, base2, squashed = call(
                evolve_kernel,
                "evolve",
                halves + [shape((2 * rows, width), F32)],
                (part1, part2, gain1, gain2, ns, e2, e1, coef),
            )
        else:
            base1, base2, gain1, gain2, gain0 = call(
                start_kernel, "start", halves * 2 + [line], (x1, x2, coef, col0, codes, wet)
            )
        kept = (coef, table, codes, wet)
        parts = [halves[0] if late else shape((fields + 1, half, width), F32), pair, line]
        run_fields = functools.partial(fields_half, late, parts, kept)
        ns, flux, *edges = call(
            functools.partial(surface_kernel, groups),
            "surface",
            [line] * 2 + ([pair] * 2 if last else []),
            (*(recs[1:] + recs[:1] if last else recs), surface, mask, pick),
            [blocks],
        )
        d1, d2 = edges if last else (ns, ns)
        e1 = lax.ppermute(d1, "tile", inner_pairs(tiles))
        e2 = lax.ppermute(d2, "tile", outer_pairs(tiles))
        if late:
            part2, part02, own = run_fields(False, base2, y2, ns, col0, squashed)
            part1, part01 = run_fields(True, base1, y1, part02, col0, squashed)
        else:
            part2, part02, own = run_fields(False, base2, y2, ns)
            part1, part01 = run_fields(True, base1, y1, part02)
        x1, x2 = part1, part2
        common = (own, e2, e1, coef, wet, part01, part02, gain0, flux)
        if not last:
            surface, *sent = call(
                functools.partial(hand_kernel, groups),
                "hand",
                [line] + payloads,
                (*common, wide, pick),
                [blocks],
                flops=20_000_000_000,
            )
        else:
            new_state, new_coupling = call(
                functools.partial(close_kernel, groups),
                "close",
                [shape(state.shape, F32), shape(coupling.shape, F32)],
                (*common, gain1, gain2, part1, part2),
                [pltpu.VMEM((rows, width), F32)] * 2
                + [
                    pltpu.VMEM(state.shape, F32),
                    pltpu.VMEM(coupling.shape, F32),
                    pltpu.SemaphoreType.DMA((1 + fields // SUBLANES,)),
                ],
                out_specs=[HBM] * 2,
            )
    return new_state, new_coupling


def solution(mesh):
    placed = (
        P("comp", None, "tile", None),
        P("comp", "tile", None),
        P("comp", "tile", None),
        P("comp", "tile", None),
        P("comp", None),
        P("comp", None),
        P("comp", None, None, None),
        P("comp", "tile", None, None),
        P("comp", "tile"),
        P("comp", "tile"),
    )
    return jax.shard_map(
        on_device,
        mesh=mesh,
        in_specs=placed,
        out_specs=(P("comp", None, "tile", None), P("comp", "tile", None)),
        check_vma=False,
    )
```

```python
import functools

import jax
import jax.numpy as jnp
from jax import lax
from jax.experimental import pallas as pl
from jax.experimental.pallas import tpu as pltpu
from jax.sharding import PartitionSpec as P

SUBSTEPS = 2
INTERVALS = 2
EXCHANGE = 0.5
OCEAN_SHARE = 0.3

F32 = jnp.float32
BF16 = jnp.bfloat16
VMEM = pl.BlockSpec(memory_space=pltpu.VMEM)
HBM = pl.BlockSpec(memory_space=pltpu.HBM)
PARAMS = pltpu.CompilerParams(vmem_limit_bytes=40 * 1024 * 1024)


MEMBERS = 3
SUBLANES = 8
BAND = 8


def partner_pairs(groups, tiles, member):
    air_count = MEMBERS * groups // 4
    pairs = []
    for group in range(groups):
        ocean = group >= air_count
        if ocean:
            partner = MEMBERS * (group - air_count) + member
        else:
            partner = air_count + group // MEMBERS if group % MEMBERS == member else group
        for tile in range(tiles):
            other = tile ^ 1 if partner == group else tile
            pairs.append((group * tiles + tile, partner * tiles + other))
    return pairs


def inner_pairs(count):
    return [(tile, tile ^ 1) for tile in range(count)]


def outer_pairs(count):
    return [(tile, (tile + 1) % count if tile % 2 else (tile - 1) % count) for tile in range(count)]


def split_high_low(value):
    high = value.astype(BF16)
    low = (value - high.astype(F32)).astype(BF16)
    return high, low


def products(handed, picked_by, weight, blk_ref):
    rows, width = handed.shape
    count, block = blk_ref.shape
    per_row = width // block
    for c in range(per_row):
        blk_ref[pl.ds(c, rows, stride=per_row), :] = handed[:, c * block : (c + 1) * block]
    blocks = blk_ref[...].astype(BF16)
    even = blocks.astype(F32)
    turned = [blocks] + [pltpu.roll(even, block - j, 1).astype(BF16) for j in range(1, BAND)]
    picked = picked_by(jnp.concatenate(turned, axis=1))
    total = weight(0) * picked[:, :block]
    for j in range(1, BAND):
        total = total + weight(j) * picked[:, j * block : (j + 1) * block]
    return total


def column(row):
    n = row.shape[1]
    diagonal = lax.broadcasted_iota(jnp.int32, (n, n), 0) == lax.broadcasted_iota(jnp.int32, (n, n), 1)
    return jnp.sum(jnp.where(diagonal, row, 0.0), axis=1, keepdims=True)


def is_odd():
    return lax.rem(lax.axis_index("tile"), 2) == 1


def is_sea(groups):
    return lax.axis_index("comp") >= MEMBERS * groups // 4


def halves_of(rows):
    half = len(rows) // 2
    head, tail = rows[:half], rows[half:]
    inner = [jnp.where(is_odd(), h, t) for h, t in zip(head, tail)]
    outer = [jnp.where(is_odd(), t, h) for h, t in zip(head, tail)]
    return inner, outer


def rows_of(inner, outer):
    head = [jnp.where(is_odd(), i, o) for i, o in zip(inner, outer)]
    tail = [jnp.where(is_odd(), o, i) for i, o in zip(inner, outer)]
    return head + tail


def lines_of(lines):
    return [lines[r : r + 1] for r in range(lines.shape[0])]


def copy_all(pairs, sems):
    copies = [pltpu.make_async_copy(src, dst, sems.at[n]) for n, (src, dst) in enumerate(pairs)]
    for copy in copies:
        copy.start()
    return copies


def load_kernel(groups, state, sources, targets, coupling, weights, *refs):
    x1, x2, surface, pick, chosen, targets_v, coupling_v, weights_v, state_v, sources_v, sems = refs
    copies = copy_all(
        (
            (state, state_v),
            (sources, sources_v),
            (targets, targets_v),
            (coupling, coupling_v),
            (weights, weights_v),
        ),
        sems,
    )
    copies[1].wait()
    copies[2].wait()
    count, margins = pick.shape
    slot = lax.broadcasted_iota(jnp.int32, (count, margins), 0)
    pick[...] = (slot == sources_v[...]).astype(F32).astype(BF16)
    me = lax.axis_index("comp")
    air_count = MEMBERS * groups // 4
    for n in range(MEMBERS):
        ocean = jnp.where(lax.rem(me, MEMBERS) == n, air_count + lax.div(me, MEMBERS), me)
        partner = jnp.where(me < air_count, ocean, MEMBERS * (me - air_count) + n)
        hit = (targets_v[...] == slot + partner * count).astype(F32).astype(BF16)
        chosen[n * count : (n + 1) * count] = jnp.concatenate([hit, hit], axis=1)
    copies[0].wait()
    for ref, half in zip((x1, x2), halves_of([state_v[0, 1:, r, :] for r in range(state_v.shape[2])])):
        for i, value in enumerate(half):
            ref[:, i, :] = value
    surface[...] = state_v[0, 0]
    for copy in copies[3:]:
        copy.wait()


def all_fields(x, i):
    width = x.shape[2]
    if x.shape[0] % SUBLANES:
        cut = SUBLANES - 1
        top = jnp.concatenate([jnp.zeros((1, width), F32), x[:cut, i, :]], axis=0)
        return jnp.concatenate([top, x[cut:, i, :]], axis=0)
    return x[:, i, :]


def remap_kernel(coupling, weights, pick, chosen, wide, *refs):
    outs, blk = refs[:-1], refs[-1]
    count, margins = pick.shape
    wide[...] = weights[0].reshape(wide.shape).astype(F32)
    contrib = products(
        coupling[0],
        lambda blocks: lax.dot_general(
            pick[...], blocks, (((0,), (0,)), ((), ())), preferred_element_type=F32
        ),
        lambda j: wide[pl.ds(j, margins, stride=BAND), :],
        blk,
    )
    both = jnp.concatenate(split_high_low(contrib), axis=0)
    blocks = jnp.dot(chosen[...], both, preferred_element_type=F32)
    for n, out in enumerate(outs):
        out[...] = blocks[n * count : (n + 1) * count]


def sort_kernel(groups, targets, wide, pick, *refs):
    args, refs = refs[:5], refs[5:]
    wide_out, pick_out, mask, codes, wet, coef, table, col0, mixing, courant, matrices, sems = refs
    copies = copy_all(tuple(zip(args, (mask, codes, mixing, courant, matrices))), sems)
    count, margins = pick.shape
    me = lax.axis_index("comp")
    air_count = MEMBERS * groups // 4
    first = jnp.where(is_sea(groups), MEMBERS * (me - air_count), air_count + lax.div(me, MEMBERS))
    place = targets[...] - first * count
    here = lax.broadcasted_iota(jnp.int32, (margins, margins), 0)
    there = lax.broadcasted_iota(jnp.int32, (margins, margins), 1)
    level = place.astype(F32)
    same = jnp.logical_and(column(level) == level, here < there)
    rank = jnp.sum(jnp.where(same, 1.0, 0.0), axis=0, keepdims=True).astype(jnp.int32)
    place = place + jnp.where(is_sea(groups), 0, rank * count)
    order = (here == place).astype(F32).astype(BF16)
    pick_out[...] = lax.dot_general(
        order, pick[...], (((1,), (1,)), ((), ())), preferred_element_type=F32
    ).astype(BF16)
    for j in range(BAND):
        band = wide[pl.ds(j, margins, stride=BAND), :].astype(BF16)
        wide_out[j] = jnp.dot(order, band, preferred_element_type=F32)
    for copy in copies:
        copy.wait()
    wet[...] = jnp.where(is_sea(groups), mask[0].astype(F32), 1.0)
    m, c = column(mixing[...]), column(courant[...])
    coef[0], coef[1], coef[2] = 1.0 - 4.0 * m - c, m + c, m
    branches, fields = matrices.shape[1:3]
    flat = matrices[0].reshape(branches * fields, fields)
    col0[...] = flat[:, :1].reshape(branches, fields, 1)
    flat = jnp.where(lax.broadcasted_iota(jnp.int32, flat.shape, 1) == 0, 0.0, flat)
    high, low = split_high_low(flat)
    table[...] = jnp.concatenate([high, high, low], axis=1)


def surface_kernel(groups, *refs):
    recs, refs = refs[:MEMBERS], refs[MEMBERS:]
    surface_ref, mask_ref, _, ns_ref, flux_ref, *ends, blk = refs
    rows, width = ns_ref.shape
    block = blk.shape[-1]
    per_row = width // block
    total = recs[0][...]
    for rec in recs[1:]:
        total = total + rec[...]
    blk[...] = total
    received = jnp.concatenate(
        [blk[pl.ds(c, rows, stride=per_row), :] for c in range(per_row)], axis=1
    )
    surface = surface_ref[...]
    flux = mask_ref[0].astype(F32) * EXCHANGE * (received - surface)
    new = surface + jnp.where(is_sea(groups), -OCEAN_SHARE * received, flux)
    ns_ref[...] = new
    flux_ref[...] = flux
    for ref, half in zip(ends, halves_of([new[: rows // 2], new[rows // 2 :]])):
        ref[...] = half[0]


def substep(f, up, down, c0, cu, m):
    width = f.shape[1]
    sides = pltpu.roll(f, 1, 1) + pltpu.roll(f, width - 1, 1)
    return c0 * f + cu * up + m * (down + sides)


def sides(f):
    return pltpu.roll(f, 1, 1) + pltpu.roll(f, f.shape[1] - 1, 1)


def own_rows(f0, f1, f2, f3, coef, base1, base2):
    c0, cu, m = coef[0], coef[1], coef[2]
    g0 = c0 * f0 + m * (f1 + sides(f0))
    g1 = substep(f1, f0, f2, c0, cu, m)
    g2 = substep(f2, f1, f3, c0, cu, m)
    g3 = c0 * f3 + cu * f2 + m * sides(f3)
    rows = [
        c0 * g0 + m * (g1 + sides(g0)) + (cu * m) * f0,
        substep(g1, g0, g2, c0, cu, m),
        substep(g2, g1, g3, c0, cu, m),
        c0 * g3 + cu * g2 + m * sides(g3) + (cu * m) * f3,
    ]
    for ref, half in zip((base1, base2), halves_of(rows)):
        for i, value in enumerate(half):
            ref[i] = value


def start_kernel(x1, x2, coef, col0, codes, wet, base1, base2, gain1, gain2, gain0):
    inner, outer = ([all_fields(x, i) for i in range(x.shape[1])] for x in (x1, x2))
    own_rows(*rows_of(inner, outer), coef, base1, base2)
    shape = gain1.shape[1:]
    rows = [
        branch_factor(col0, code, shape) * line
        for code, line in zip(lines_of(codes[0]), lines_of(wet[...]))
    ]
    for ref, half in zip((gain1, gain2), halves_of(rows)):
        for i, value in enumerate(half):
            ref[i] = value
    for r, value in enumerate(rows):
        gain0[r : r + 1, :] = value[:1]


def evolve_kernel(part1, part2, gain1, gain2, ns, e2, e1, coef, base1, base2, squashed):
    squashed[...] = jnp.tanh(field0_rows(ns, e2[...], e1[...], coef))
    half, fields, _ = gain1.shape
    line1, line2 = halves_of([squashed[r : r + 1, :] for r in range(half, 3 * half)])
    inner = [part1[:fields, i, :] + gain1[i] * line1[i] for i in range(half)]
    outer = [part2[:fields, i, :] + gain2[i] * line2[i] for i in range(half)]
    own_rows(*rows_of(inner, outer), coef, base1, base2)


def branch_factor(col0, code, shape):
    factor = jnp.broadcast_to(col0[0], shape)
    for b in range(1, col0.shape[0]):
        factor = jnp.where(code == b, col0[b], factor)
    return factor


def fields_kernel(inner, late, base, y, after, coef, table, codes, wet, *refs):
    part, part0 = refs[-2:] if inner else refs[-3:-1]
    if not inner:
        none = jnp.zeros((SUBSTEPS, base.shape[2]), F32)
        refs[-1][...] = field0_rows(after, none, none, coef)
    col0, squashed = refs[:2] if late else (None, None)
    half, fields, width = base.shape
    at_top = is_odd() if inner else jnp.logical_not(is_odd())
    c0, cu, m = coef[0], coef[1], coef[2]
    q = jnp.where(at_top, cu, m)
    branches = table.shape[0] // fields

    def halo_row(top, bottom):
        if not late:
            return jnp.where(at_top, all_fields(y, top), all_fields(y, bottom))
        value = jnp.where(at_top, y[:fields, top, :], y[:fields, bottom, :])
        code = jnp.where(at_top, y[fields:, top, :], y[fields:, bottom, :]).astype(jnp.int32)
        line = jnp.where(
            at_top, squashed[top : top + 1, :], squashed[3 * half + bottom : 3 * half + bottom + 1, :]
        )
        return value + branch_factor(col0, code, (fields, width)) * (value[:1] * line)

    near, far = halo_row(1, 0), halo_row(0, 1)
    edge = (2.0 * q * c0) * near + (2.0 * q * m) * sides(near) + (q * q) * far
    next_to_edge = (q * q) * near
    halos = jnp.where(at_top, edge, next_to_edge), jnp.where(at_top, next_to_edge, edge)
    code_lines = halves_of([codes[0, r : r + 1, :] for r in range(2 * half)])[0 if inner else 1]
    wet_lines = halves_of([wet[r : r + 1, :] for r in range(2 * half)])[0 if inner else 1]
    top_field = lax.broadcasted_iota(jnp.int32, (fields, width), 0) == 0
    for i in range(half):
        f = base[i] + halos[i]
        high, low = split_high_low(jnp.tanh(f))
        terms = jnp.dot(
            table[...], jnp.concatenate([high, low, high], axis=0), preferred_element_type=F32
        )
        tendency = terms[:fields]
        for b in range(1, branches):
            chosen = code_lines[i] == b
            tendency = jnp.where(chosen, terms[b * fields : (b + 1) * fields], tendency)
        part0[i : i + 1, :] = tendency[:1] * wet_lines[i]
        if late:
            part[i] = (f + tendency) * wet_lines[i]
        else:
            part[:fields, i, :] = jnp.where(top_field, 1.0, f + tendency) * wet_lines[i]
            part[fields:, i, :] = code_lines[i].astype(F32)


def field0_rows(ns, e2, e1, coef):
    c0, cu, m = coef[0, :1], coef[1, :1], coef[2, :1]
    odd = is_odd()
    f = jnp.concatenate([jnp.where(odd, e1, e2), ns[...], jnp.where(odd, e2, e1)], axis=0)
    rows = f.shape[0]
    for _ in range(SUBSTEPS):
        f = substep(f, pltpu.roll(f, 1, 0), pltpu.roll(f, rows - 1, 0), c0, cu, m)
    return f[SUBSTEPS : rows - SUBSTEPS]


def field0(own, e2, e1, coef, wet, part01, part02, gain0):
    odd = is_odd()
    rows = own.shape[0]
    end = e1.shape[0]
    pick = lambda even, other, at: jnp.where(odd, other[at : at + 1, :], even[at : at + 1, :])
    near = jnp.concatenate([pick(e2, e1, end - 1), pick(e1, e2, 0)], axis=0)
    far = jnp.concatenate([pick(e2, e1, end - 2), pick(e1, e2, 1)], axis=0)
    c0, cu, m = coef[0, :1], coef[1, :1], coef[2, :1]
    q = jnp.concatenate([cu, m], axis=0)
    edge = (2.0 * q * c0) * near + (2.0 * q * m) * sides(near) + (q * q) * far
    inside = (q * q) * near
    f = own[...] + jnp.concatenate([edge[:1], inside, edge[1:]], axis=0)
    squashed = jnp.tanh(f)
    part = jnp.concatenate(rows_of([part01[...]], [part02[...]]), axis=0)
    return part + gain0[...] * squashed + f * wet[...], squashed


def hand_kernel(
    groups, own, e2, e1, coef, wet, part01, part02, gain0, flux, wide, pick, *refs
):
    surf, *outs, blk = refs
    surf[...], _ = field0(own, e2, e1, coef, wet, part01, part02, gain0)
    sea = is_sea(groups)
    contrib = products(
        jnp.where(sea, surf[...], flux[...]),
        lambda blocks: jnp.dot(pick[...], blocks, preferred_element_type=F32),
        lambda j: wide[j],
        blk,
    )
    count = blk.shape[0]
    thirds = [contrib[n * count : (n + 1) * count] for n in range(MEMBERS)]
    member = lax.rem(lax.axis_index("comp"), MEMBERS)
    for n, (out, third) in enumerate(zip(outs, thirds)):
        out[...] = jnp.where(sea, third, jnp.where(member == n, sum(thirds), 0.0))


def close_kernel(
    groups, own, e2, e1, coef, wet, part01, part02, gain0, flux, gain1, gain2, part1, part2, *refs
):
    new_state, new_coupling, surf, squashed, stage, handed, sems = refs
    surf[...], squashed[...] = field0(own, e2, e1, coef, wet, part01, part02, gain0)
    handed[0] = jnp.where(is_sea(groups), surf[...], flux[...])
    copies = [pltpu.make_async_copy(handed, new_coupling, sems.at[0])]
    copies[0].start()
    half, fields, width = gain1.shape
    top_field = lax.broadcasted_iota(jnp.int32, (SUBLANES, width), 0) == 0
    line1, line2 = halves_of([squashed[r : r + 1, :] for r in range(2 * half)])
    for h in range(0, fields, SUBLANES):
        some = slice(h, h + SUBLANES)
        for i in range(half):
            inner = part1[i, some] + gain1[i, some] * line1[i]
            outer = part2[i, some] + gain2[i, some] * line2[i]
            for r, done in zip((i, half + i), rows_of([inner], [outer])):
                if h == 0:
                    done = jnp.where(top_field, surf[r : r + 1, :], done)
                stage[0, some, r, :] = done
        window = pl.ds(h, SUBLANES)
        copies.append(
            pltpu.make_async_copy(
                stage.at[:, window], new_state.at[:, window], sems.at[len(copies)]
            )
        )
        copies[-1].start()
    for copy in copies:
        copy.wait()


def call(kernel, name, outs, args, scratch=(), in_specs=None, out_specs=None, flops=0):
    moved = sum(a.size * a.dtype.itemsize for a in list(args) + list(outs))
    return pl.pallas_call(
        kernel,
        name=name,
        out_shape=outs,
        in_specs=in_specs or [VMEM] * len(args),
        out_specs=out_specs or [VMEM] * len(outs),
        scratch_shapes=list(scratch),
        compiler_params=PARAMS,
        cost_estimate=pl.CostEstimate(flops=flops, bytes_accessed=moved, transcendentals=0),
    )(*args)


def fields_half(late, parts, kept, inner, base, y, after, *rest):
    return call(
        functools.partial(fields_kernel, inner, late),
        "inner" if inner else "outer",
        parts[:2] if inner else parts,
        (base, y, after, *kept, *rest),
        flops=0 if inner else 4_000_000_000,
    )


def on_device(
    state, coupling, land_mask, codes, mixing, courant, matrices, weights, sources, targets
):
    groups = lax.axis_size("comp")
    tiles = lax.axis_size("tile")
    _, fields, rows, width = state.shape
    _, margins, band, block = weights.shape
    count = rows * width // block
    half = rows // 2
    branches = matrices.shape[1]
    shape = jax.ShapeDtypeStruct

    halves = [shape((half, fields, width), F32)] * 2
    payloads = [shape((count, block), F32)] * MEMBERS
    blocks = pltpu.VMEM((count, block), F32)
    line, pair = shape((rows, width), F32), shape((half, width), F32)
    far = lambda args: [pltpu.with_memory_space_constraint(a, pltpu.HBM) for a in args]
    like = lambda args: [shape(a.shape, a.dtype) for a in args]
    room = lambda args: [pltpu.VMEM(a.shape, a.dtype) for a in args]
    x1, x2, surface, pick, chosen, targets, handed, raw = call(
        functools.partial(load_kernel, groups),
        "load",
        [shape((fields - 1, half, width), F32)] * 2
        + [line, shape((count, margins), BF16), shape((MEMBERS * count, 2 * margins), BF16)]
        + like((targets, coupling, weights)),
        far((state, sources, targets, coupling, weights)),
        room((state, sources)) + [pltpu.SemaphoreType.DMA((5,))],
        [HBM] * 5,
    )
    wide, *sent = call(
        remap_kernel,
        "remap",
        [shape((margins * band, block), F32)] + payloads,
        (handed, raw, pick, chosen),
        [blocks],
    )
    wide, pick, mask, codes, wet, coef, table, col0 = call(
        functools.partial(sort_kernel, groups),
        "sort",
        [shape((band, margins, block), F32), shape((margins, count), BF16)]
        + like((land_mask, codes))
        + [
            line,
            shape((3, fields, 1), F32),
            shape((branches * fields, 3 * fields), BF16),
            shape((branches, fields, 1), F32),
        ],
        (targets, wide, pick, *far((land_mask, codes, mixing, courant, matrices))),
        room((mixing, courant, matrices)) + [pltpu.SemaphoreType.DMA((5,))],
        [VMEM] * 3 + [HBM] * 5,
    )
    for interval in range(INTERVALS):
        y1 = lax.ppermute(x1, "tile", inner_pairs(tiles))
        y2 = lax.ppermute(x2, "tile", outer_pairs(tiles))
        recs = [
            lax.ppermute(value, ("comp", "tile"), partner_pairs(groups, tiles, member))
            for member, value in enumerate(sent)
        ]
        late, last = interval > 0, interval == INTERVALS - 1
        if late:
            base1, base2, squashed = call(
                evolve_kernel,
                "evolve",
                halves + [shape((2 * rows, width), F32)],
                (part1, part2, gain1, gain2, ns, e2, e1, coef),
            )
        else:
            base1, base2, gain1, gain2, gain0 = call(
                start_kernel, "start", halves * 2 + [line], (x1, x2, coef, col0, codes, wet)
            )
        kept = (coef, table, codes, wet)
        parts = [halves[0] if late else shape((fields + 1, half, width), F32), pair, line]
        run_fields = functools.partial(fields_half, late, parts, kept)
        ns, flux, *edges = call(
            functools.partial(surface_kernel, groups),
            "surface",
            [line] * 2 + ([pair] * 2 if last else []),
            (*(recs[1:] + recs[:1] if last else recs), surface, mask, pick),
            [blocks],
        )
        d1, d2 = edges if last else (ns, ns)
        e1 = lax.ppermute(d1, "tile", inner_pairs(tiles))
        e2 = lax.ppermute(d2, "tile", outer_pairs(tiles))
        if late:
            part2, part02, own = run_fields(False, base2, y2, ns, col0, squashed)
            part1, part01 = run_fields(True, base1, y1, part02, col0, squashed)
        else:
            part2, part02, own = run_fields(False, base2, y2, ns)
            part1, part01 = run_fields(True, base1, y1, part02)
        x1, x2 = part1, part2
        common = (own, e2, e1, coef, wet, part01, part02, gain0, flux)
        if not last:
            surface, *sent = call(
                functools.partial(hand_kernel, groups),
                "hand",
                [line] + payloads,
                (*common, wide, pick),
                [blocks],
                flops=20_000_000_000,
            )
        else:
            new_state, new_coupling = call(
                functools.partial(close_kernel, groups),
                "close",
                [shape(state.shape, F32), shape(coupling.shape, F32)],
                (*common, gain1, gain2, part1, part2),
                [pltpu.VMEM((rows, width), F32)] * 2
                + [
                    pltpu.VMEM(state.shape, F32),
                    pltpu.VMEM(coupling.shape, F32),
                    pltpu.SemaphoreType.DMA((1 + fields // SUBLANES,)),
                ],
                out_specs=[HBM] * 2,
            )
    return new_state, new_coupling


def solution(mesh):
    placed = (
        P("comp", None, "tile", None),
        P("comp", "tile", None),
        P("comp", "tile", None),
        P("comp", "tile", None),
        P("comp", None),
        P("comp", None),
        P("comp", None, None, None),
        P("comp", "tile", None, None),
        P("comp", "tile"),
        P("comp", "tile"),
    )
    return jax.shard_map(
        on_device,
        mesh=mesh,
        in_specs=placed,
        out_specs=(P("comp", None, "tile", None), P("comp", "tile", None)),
        check_vma=False,
    )
```

```python
import functools

import jax
import jax.numpy as jnp
from jax import lax
from jax.experimental import pallas as pl
from jax.experimental.pallas import tpu as pltpu
from jax.sharding import PartitionSpec as P

SUBSTEPS = 2
INTERVALS = 2
EXCHANGE = 0.5
OCEAN_SHARE = 0.3

F32 = jnp.float32
BF16 = jnp.bfloat16
VMEM = pl.BlockSpec(memory_space=pltpu.VMEM)
HBM = pl.BlockSpec(memory_space=pltpu.HBM)
PARAMS = pltpu.CompilerParams(vmem_limit_bytes=40 * 1024 * 1024)


MEMBERS = 3
SUBLANES = 8
BAND = 8


def partner_pairs(groups, tiles, member):
    air_count = MEMBERS * groups // 4
    pairs = []
    for group in range(groups):
        ocean = group >= air_count
        if ocean:
            partner = MEMBERS * (group - air_count) + member
        else:
            partner = air_count + group // MEMBERS if group % MEMBERS == member else group
        for tile in range(tiles):
            other = tile ^ 1 if partner == group else tile
            pairs.append((group * tiles + tile, partner * tiles + other))
    return pairs


def inner_pairs(count):
    return [(tile, tile ^ 1) for tile in range(count)]


def outer_pairs(count):
    return [(tile, (tile + 1) % count if tile % 2 else (tile - 1) % count) for tile in range(count)]


def split_high_low(value):
    high = value.astype(BF16)
    low = (value - high.astype(F32)).astype(BF16)
    return high, low


def products(handed, picked_by, weight, blk_ref):
    rows, width = handed.shape
    block = blk_ref.shape[1]
    per_row = width // block
    for c in range(per_row):
        blk_ref[pl.ds(c, rows, stride=per_row), :] = handed[:, c * block : (c + 1) * block]
    blocks = blk_ref[: rows * per_row, :].astype(BF16)
    even = blocks.astype(F32)
    turned = [blocks] + [pltpu.roll(even, block - j, 1).astype(BF16) for j in range(1, BAND)]
    picked = picked_by(jnp.concatenate(turned, axis=1))
    total = weight(0) * picked[:, :block]
    for j in range(1, BAND):
        total = total + weight(j) * picked[:, j * block : (j + 1) * block]
    return total


def column(row):
    n = row.shape[1]
    diagonal = lax.broadcasted_iota(jnp.int32, (n, n), 0) == lax.broadcasted_iota(jnp.int32, (n, n), 1)
    return jnp.sum(jnp.where(diagonal, row, 0.0), axis=1, keepdims=True)


def is_odd():
    return lax.rem(lax.axis_index("tile"), 2) == 1


def is_sea(groups):
    return lax.axis_index("comp") >= MEMBERS * groups // 4


def halves_of(rows):
    half = len(rows) // 2
    head, tail = rows[:half], rows[half:]
    inner = [jnp.where(is_odd(), h, t) for h, t in zip(head, tail)]
    outer = [jnp.where(is_odd(), t, h) for h, t in zip(head, tail)]
    return inner, outer


def rows_of(inner, outer):
    head = [jnp.where(is_odd(), i, o) for i, o in zip(inner, outer)]
    tail = [jnp.where(is_odd(), o, i) for i, o in zip(inner, outer)]
    return head + tail


def lines_of(lines):
    return [lines[r : r + 1] for r in range(lines.shape[0])]


def copy_all(pairs, sems):
    copies = [pltpu.make_async_copy(src, dst, sems.at[n]) for n, (src, dst) in enumerate(pairs)]
    for copy in copies:
        copy.start()
    return copies


def load_kernel(groups, state, sources, targets, coupling, weights, *refs):
    x1, x2, surface, pick, chosen, targets_v, coupling_v, weights_v, state_v, sources_v, sems = refs
    copies = copy_all(
        (
            (state, state_v),
            (sources, sources_v),
            (targets, targets_v),
            (coupling, coupling_v),
            (weights, weights_v),
        ),
        sems,
    )
    copies[1].wait()
    copies[2].wait()
    count, margins = pick.shape
    slot = lax.broadcasted_iota(jnp.int32, (count, margins), 0)
    pick[...] = (slot == sources_v[...]).astype(F32).astype(BF16)
    me = lax.axis_index("comp")
    air_count = MEMBERS * groups // 4
    for n in range(MEMBERS):
        ocean = jnp.where(lax.rem(me, MEMBERS) == n, air_count + lax.div(me, MEMBERS), me)
        partner = jnp.where(me < air_count, ocean, MEMBERS * (me - air_count) + n)
        hit = (targets_v[...] == slot + partner * count).astype(F32).astype(BF16)
        chosen[n * count : (n + 1) * count] = jnp.concatenate([hit, hit], axis=1)
    copies[0].wait()
    for ref, half in zip((x1, x2), halves_of([state_v[0, 1:, r, :] for r in range(state_v.shape[2])])):
        for i, value in enumerate(half):
            ref[:, i, :] = value
    surface[...] = state_v[0, 0]
    for copy in copies[3:]:
        copy.wait()


def all_fields(x, i):
    width = x.shape[2]
    if x.shape[0] % SUBLANES:
        cut = SUBLANES - 1
        top = jnp.concatenate([jnp.zeros((1, width), F32), x[:cut, i, :]], axis=0)
        return jnp.concatenate([top, x[cut:, i, :]], axis=0)
    return x[:, i, :]


def remap_kernel(coupling, weights, pick, chosen, wide, *refs):
    outs, blk = refs[:-1], refs[-1]
    count, margins = pick.shape
    wide[...] = weights[0].reshape(wide.shape).astype(F32)
    contrib = products(
        coupling[0],
        lambda blocks: lax.dot_general(
            pick[...], blocks, (((0,), (0,)), ((), ())), preferred_element_type=F32
        ),
        lambda j: wide[pl.ds(j, margins, stride=BAND), :],
        blk,
    )
    both = jnp.concatenate(split_high_low(contrib), axis=0)
    blocks = jnp.dot(chosen[...], both, preferred_element_type=F32)
    for n, out in enumerate(outs):
        out[...] = blocks[n * count : (n + 1) * count]


def sort_kernel(groups, targets, wide, pick, *refs):
    args, refs = refs[:5], refs[5:]
    wide_out, pick_out, mask, codes, wet, coef, table, col0, mixing, courant, matrices, sems = refs
    copies = copy_all(tuple(zip(args, (mask, codes, mixing, courant, matrices))), sems)
    count, margins = pick.shape
    me = lax.axis_index("comp")
    air_count = MEMBERS * groups // 4
    first = jnp.where(is_sea(groups), MEMBERS * (me - air_count), air_count + lax.div(me, MEMBERS))
    place = targets[...] - first * count
    here = lax.broadcasted_iota(jnp.int32, (margins, margins), 0)
    there = lax.broadcasted_iota(jnp.int32, (margins, margins), 1)
    level = place.astype(F32)
    same = jnp.logical_and(column(level) == level, here < there)
    rank = jnp.sum(jnp.where(same, 1.0, 0.0), axis=0, keepdims=True).astype(jnp.int32)
    place = place + jnp.where(is_sea(groups), 0, rank * count)
    order = (here == place).astype(F32).astype(BF16)
    pick_out[...] = lax.dot_general(
        order, pick[...], (((1,), (1,)), ((), ())), preferred_element_type=F32
    ).astype(BF16)
    for j in range(BAND):
        band = wide[pl.ds(j, margins, stride=BAND), :].astype(BF16)
        wide_out[j] = jnp.dot(order, band, preferred_element_type=F32)
    for copy in copies:
        copy.wait()
    wet[...] = jnp.where(is_sea(groups), mask[0].astype(F32), 1.0)
    m, c = column(mixing[...]), column(courant[...])
    coef[0], coef[1], coef[2] = 1.0 - 4.0 * m - c, m + c, m
    branches, fields = matrices.shape[1:3]
    flat = matrices[0].reshape(branches * fields, fields)
    col0[...] = flat[:, :1].reshape(branches, fields, 1)
    flat = jnp.where(lax.broadcasted_iota(jnp.int32, flat.shape, 1) == 0, 0.0, flat)
    high, low = split_high_low(flat)
    table[...] = jnp.concatenate([high, high, low], axis=1)


def surface_kernel(groups, *refs):
    recs, refs = refs[:MEMBERS], refs[MEMBERS:]
    surface_ref, mask_ref, _, ns_ref, flux_ref, *ends, blk = refs
    rows, width = ns_ref.shape
    block = blk.shape[-1]
    per_row = width // block
    total = recs[0][...]
    for rec in recs[1:]:
        total = total + rec[...]
    blk[: total.shape[0], :] = total
    received = jnp.concatenate(
        [blk[pl.ds(c, rows, stride=per_row), :] for c in range(per_row)], axis=1
    )
    surface = surface_ref[...]
    flux = mask_ref[0].astype(F32) * EXCHANGE * (received - surface)
    new = surface + jnp.where(is_sea(groups), -OCEAN_SHARE * received, flux)
    ns_ref[...] = new
    flux_ref[...] = flux
    for ref, half in zip(ends, halves_of([new[: rows // 2], new[rows // 2 :]])):
        ref[...] = half[0]


def substep(f, up, down, c0, cu, m):
    width = f.shape[1]
    sides = pltpu.roll(f, 1, 1) + pltpu.roll(f, width - 1, 1)
    return c0 * f + cu * up + m * (down + sides)


def sides(f):
    return pltpu.roll(f, 1, 1) + pltpu.roll(f, f.shape[1] - 1, 1)


def own_rows(f0, f1, f2, f3, coef, base1, base2):
    c0, cu, m = coef[0], coef[1], coef[2]
    g0 = c0 * f0 + m * (f1 + sides(f0))
    g1 = substep(f1, f0, f2, c0, cu, m)
    g2 = substep(f2, f1, f3, c0, cu, m)
    g3 = c0 * f3 + cu * f2 + m * sides(f3)
    rows = [
        c0 * g0 + m * (g1 + sides(g0)) + (cu * m) * f0,
        substep(g1, g0, g2, c0, cu, m),
        substep(g2, g1, g3, c0, cu, m),
        c0 * g3 + cu * g2 + m * sides(g3) + (cu * m) * f3,
    ]
    for ref, half in zip((base1, base2), halves_of(rows)):
        for i, value in enumerate(half):
            ref[i] = value


def start_kernel(x1, x2, coef, col0, codes, wet, base1, base2, gain1, gain2, gain0):
    inner, outer = ([all_fields(x, i) for i in range(x.shape[1])] for x in (x1, x2))
    own_rows(*rows_of(inner, outer), coef, base1, base2)
    shape = gain1.shape[1:]
    rows = [
        branch_factor(col0, code, shape) * line
        for code, line in zip(lines_of(codes[0]), lines_of(wet[...]))
    ]
    for ref, half in zip((gain1, gain2), halves_of(rows)):
        for i, value in enumerate(half):
            ref[i] = value
    for r, value in enumerate(rows):
        gain0[r : r + 1, :] = value[:1]


def evolve_kernel(part1, part2, gain1, gain2, ns, e2, e1, coef, base1, base2, squashed):
    squashed[...] = jnp.tanh(field0_rows(ns, e2[...], e1[...], coef))
    half, fields, _ = gain1.shape
    line1, line2 = halves_of([squashed[r : r + 1, :] for r in range(half, 3 * half)])
    inner = [part1[:fields, i, :] + gain1[i] * line1[i] for i in range(half)]
    outer = [part2[:fields, i, :] + gain2[i] * line2[i] for i in range(half)]
    own_rows(*rows_of(inner, outer), coef, base1, base2)


def branch_factor(col0, code, shape):
    factor = jnp.broadcast_to(col0[0], shape)
    for b in range(1, col0.shape[0]):
        factor = jnp.where(code == b, col0[b], factor)
    return factor


def fields_kernel(inner, late, base, y, after, coef, table, codes, wet, *refs):
    part, part0 = refs[-2:] if inner else refs[-3:-1]
    if not inner:
        none = jnp.zeros((SUBSTEPS, base.shape[2]), F32)
        refs[-1][...] = field0_rows(after, none, none, coef)
    col0, squashed = refs[:2] if late else (None, None)
    half, fields, width = base.shape
    at_top = is_odd() if inner else jnp.logical_not(is_odd())
    c0, cu, m = coef[0], coef[1], coef[2]
    q = jnp.where(at_top, cu, m)
    branches = table.shape[0] // fields

    def halo_row(top, bottom):
        if not late:
            return jnp.where(at_top, all_fields(y, top), all_fields(y, bottom))
        value = jnp.where(at_top, y[:fields, top, :], y[:fields, bottom, :])
        code = jnp.where(at_top, y[fields:, top, :], y[fields:, bottom, :]).astype(jnp.int32)
        line = jnp.where(
            at_top, squashed[top : top + 1, :], squashed[3 * half + bottom : 3 * half + bottom + 1, :]
        )
        return value + branch_factor(col0, code, (fields, width)) * (value[:1] * line)

    near, far = halo_row(1, 0), halo_row(0, 1)
    edge = (2.0 * q * c0) * near + (2.0 * q * m) * sides(near) + (q * q) * far
    next_to_edge = (q * q) * near
    halos = jnp.where(at_top, edge, next_to_edge), jnp.where(at_top, next_to_edge, edge)
    code_lines = halves_of([codes[0, r : r + 1, :] for r in range(2 * half)])[0 if inner else 1]
    wet_lines = halves_of([wet[r : r + 1, :] for r in range(2 * half)])[0 if inner else 1]
    top_field = lax.broadcasted_iota(jnp.int32, (fields, width), 0) == 0
    for i in range(half):
        f = base[i] + halos[i]
        high, low = split_high_low(jnp.tanh(f))
        terms = jnp.dot(
            table[...], jnp.concatenate([high, low, high], axis=0), preferred_element_type=F32
        )
        tendency = terms[:fields]
        for b in range(1, branches):
            chosen = code_lines[i] == b
            tendency = jnp.where(chosen, terms[b * fields : (b + 1) * fields], tendency)
        part0[i : i + 1, :] = tendency[:1] * wet_lines[i]
        if late:
            part[i] = (f + tendency) * wet_lines[i]
        else:
            part[:fields, i, :] = jnp.where(top_field, 1.0, f + tendency) * wet_lines[i]
            part[fields:, i, :] = code_lines[i].astype(F32)


def field0_rows(ns, e2, e1, coef):
    c0, cu, m = coef[0, :1], coef[1, :1], coef[2, :1]
    odd = is_odd()
    f = jnp.concatenate([jnp.where(odd, e1, e2), ns[...], jnp.where(odd, e2, e1)], axis=0)
    rows = f.shape[0]
    for _ in range(SUBSTEPS):
        f = substep(f, pltpu.roll(f, 1, 0), pltpu.roll(f, rows - 1, 0), c0, cu, m)
    return f[SUBSTEPS : rows - SUBSTEPS]


def field0(own, e2, e1, coef, wet, part01, part02, gain0):
    odd = is_odd()
    rows = own.shape[0]
    end = e1.shape[0]
    pick = lambda even, other, at: jnp.where(odd, other[at : at + 1, :], even[at : at + 1, :])
    near = jnp.concatenate([pick(e2, e1, end - 1), pick(e1, e2, 0)], axis=0)
    far = jnp.concatenate([pick(e2, e1, end - 2), pick(e1, e2, 1)], axis=0)
    c0, cu, m = coef[0, :1], coef[1, :1], coef[2, :1]
    q = jnp.concatenate([cu, m], axis=0)
    edge = (2.0 * q * c0) * near + (2.0 * q * m) * sides(near) + (q * q) * far
    inside = (q * q) * near
    f = own[...] + jnp.concatenate([edge[:1], inside, edge[1:]], axis=0)
    squashed = jnp.tanh(f)
    part = jnp.concatenate(rows_of([part01[...]], [part02[...]]), axis=0)
    return part + gain0[...] * squashed + f * wet[...], squashed


def hand_kernel(
    groups, own, e2, e1, coef, wet, part01, part02, gain0, flux, wide, pick, *refs
):
    surf, *outs, blk = refs
    surf[...], _ = field0(own, e2, e1, coef, wet, part01, part02, gain0)
    sea = is_sea(groups)
    contrib = products(
        jnp.where(sea, surf[...], flux[...]),
        lambda blocks: jnp.dot(pick[...], blocks, preferred_element_type=F32),
        lambda j: wide[j],
        blk,
    )
    count = outs[0].shape[0]
    thirds = [contrib[n * count : (n + 1) * count] for n in range(MEMBERS)]
    member = lax.rem(lax.axis_index("comp"), MEMBERS)
    for n, (out, third) in enumerate(zip(outs, thirds)):
        out[...] = jnp.where(sea, third, jnp.where(member == n, sum(thirds), 0.0))


def close_kernel(
    groups, own, e2, e1, coef, wet, part01, part02, gain0, flux, gain1, gain2, part1, part2, *refs
):
    new_state, new_coupling, surf, squashed, stage, handed, sems = refs
    surf[...], squashed[...] = field0(own, e2, e1, coef, wet, part01, part02, gain0)
    handed[0] = jnp.where(is_sea(groups), surf[...], flux[...])
    copies = [pltpu.make_async_copy(handed, new_coupling, sems.at[0])]
    copies[0].start()
    half, fields, width = gain1.shape
    top_field = lax.broadcasted_iota(jnp.int32, (SUBLANES, width), 0) == 0
    line1, line2 = halves_of([squashed[r : r + 1, :] for r in range(2 * half)])
    for h in range(0, fields, SUBLANES):
        some = slice(h, h + SUBLANES)
        for i in range(half):
            inner = part1[i, some] + gain1[i, some] * line1[i]
            outer = part2[i, some] + gain2[i, some] * line2[i]
            for r, done in zip((i, half + i), rows_of([inner], [outer])):
                if h == 0:
                    done = jnp.where(top_field, surf[r : r + 1, :], done)
                stage[0, some, r, :] = done
        window = pl.ds(h, SUBLANES)
        copies.append(
            pltpu.make_async_copy(
                stage.at[:, window], new_state.at[:, window], sems.at[len(copies)]
            )
        )
        copies[-1].start()
    for copy in copies:
        copy.wait()


def call(kernel, name, outs, args, scratch=(), in_specs=None, out_specs=None, flops=0):
    moved = sum(a.size * a.dtype.itemsize for a in list(args) + list(outs))
    return pl.pallas_call(
        kernel,
        name=name,
        out_shape=outs,
        in_specs=in_specs or [VMEM] * len(args),
        out_specs=out_specs or [VMEM] * len(outs),
        scratch_shapes=list(scratch),
        compiler_params=PARAMS,
        cost_estimate=pl.CostEstimate(flops=flops, bytes_accessed=moved, transcendentals=0),
    )(*args)


def fields_half(late, parts, kept, inner, base, y, after, *rest):
    return call(
        functools.partial(fields_kernel, inner, late),
        "inner" if inner else "outer",
        parts[:2] if inner else parts,
        (base, y, after, *kept, *rest),
        flops=0 if inner else 4_000_000_000,
    )


def on_device(
    state, coupling, land_mask, codes, mixing, courant, matrices, weights, sources, targets
):
    groups = lax.axis_size("comp")
    tiles = lax.axis_size("tile")
    _, fields, rows, width = state.shape
    _, margins, band, block = weights.shape
    count = rows * width // block
    half = rows // 2
    branches = matrices.shape[1]
    shape = jax.ShapeDtypeStruct

    halves = [shape((half, fields, width), F32)] * 2
    payloads = [shape((count, block), F32)] * MEMBERS
    blocks = pltpu.VMEM((max(SUBLANES // rows, 1) * count, block), F32)
    line, pair = shape((rows, width), F32), shape((half, width), F32)
    far = lambda args: [pltpu.with_memory_space_constraint(a, pltpu.HBM) for a in args]
    like = lambda args: [shape(a.shape, a.dtype) for a in args]
    room = lambda args: [pltpu.VMEM(a.shape, a.dtype) for a in args]
    x1, x2, surface, pick, chosen, targets, handed, raw = call(
        functools.partial(load_kernel, groups),
        "load",
        [shape((fields - 1, half, width), F32)] * 2
        + [line, shape((count, margins), BF16), shape((MEMBERS * count, 2 * margins), BF16)]
        + like((targets, coupling, weights)),
        far((state, sources, targets, coupling, weights)),
        room((state, sources)) + [pltpu.SemaphoreType.DMA((5,))],
        [HBM] * 5,
    )
    wide, *sent = call(
        remap_kernel,
        "remap",
        [shape((margins * band, block), F32)] + payloads,
        (handed, raw, pick, chosen),
        [blocks],
    )
    wide, pick, mask, codes, wet, coef, table, col0 = call(
        functools.partial(sort_kernel, groups),
        "sort",
        [shape((band, margins, block), F32), shape((margins, count), BF16)]
        + like((land_mask, codes))
        + [
            line,
            shape((3, fields, 1), F32),
            shape((branches * fields, 3 * fields), BF16),
            shape((branches, fields, 1), F32),
        ],
        (targets, wide, pick, *far((land_mask, codes, mixing, courant, matrices))),
        room((mixing, courant, matrices)) + [pltpu.SemaphoreType.DMA((5,))],
        [VMEM] * 3 + [HBM] * 5,
    )
    for interval in range(INTERVALS):
        y1 = lax.ppermute(x1, "tile", inner_pairs(tiles))
        y2 = lax.ppermute(x2, "tile", outer_pairs(tiles))
        recs = [
            lax.ppermute(value, ("comp", "tile"), partner_pairs(groups, tiles, member))
            for member, value in enumerate(sent)
        ]
        late, last = interval > 0, interval == INTERVALS - 1
        if late:
            base1, base2, squashed = call(
                evolve_kernel,
                "evolve",
                halves + [shape((2 * rows, width), F32)],
                (part1, part2, gain1, gain2, ns, e2, e1, coef),
            )
        else:
            base1, base2, gain1, gain2, gain0 = call(
                start_kernel, "start", halves * 2 + [line], (x1, x2, coef, col0, codes, wet)
            )
        kept = (coef, table, codes, wet)
        parts = [halves[0] if late else shape((fields + 1, half, width), F32), pair, line]
        run_fields = functools.partial(fields_half, late, parts, kept)
        ns, flux, *edges = call(
            functools.partial(surface_kernel, groups),
            "surface",
            [line] * 2 + ([pair] * 2 if last else []),
            (*(recs[1:] + recs[:1] if last else recs), surface, mask, pick),
            [blocks],
        )
        d1, d2 = edges if last else (ns, ns)
        e1 = lax.ppermute(d1, "tile", inner_pairs(tiles))
        e2 = lax.ppermute(d2, "tile", outer_pairs(tiles))
        if late:
            part2, part02, own = run_fields(False, base2, y2, ns, col0, squashed)
            part1, part01 = run_fields(True, base1, y1, part02, col0, squashed)
        else:
            part2, part02, own = run_fields(False, base2, y2, ns)
            part1, part01 = run_fields(True, base1, y1, part02)
        x1, x2 = part1, part2
        common = (own, e2, e1, coef, wet, part01, part02, gain0, flux)
        if not last:
            surface, *sent = call(
                functools.partial(hand_kernel, groups),
                "hand",
                [line] + payloads,
                (*common, wide, pick),
                [blocks],
                flops=20_000_000_000,
            )
        else:
            new_state, new_coupling = call(
                functools.partial(close_kernel, groups),
                "close",
                [shape(state.shape, F32), shape(coupling.shape, F32)],
                (*common, gain1, gain2, part1, part2),
                [pltpu.VMEM((rows, width), F32)] * 2
                + [
                    pltpu.VMEM(state.shape, F32),
                    pltpu.VMEM(coupling.shape, F32),
                    pltpu.SemaphoreType.DMA((1 + fields // SUBLANES,)),
                ],
                out_specs=[HBM] * 2,
            )
    return new_state, new_coupling


def solution(mesh):
    placed = (
        P("comp", None, "tile", None),
        P("comp", "tile", None),
        P("comp", "tile", None),
        P("comp", "tile", None),
        P("comp", None),
        P("comp", None),
        P("comp", None, None, None),
        P("comp", "tile", None, None),
        P("comp", "tile"),
        P("comp", "tile"),
    )
    return jax.shard_map(
        on_device,
        mesh=mesh,
        in_specs=placed,
        out_specs=(P("comp", None, "tile", None), P("comp", "tile", None)),
        check_vma=False,
    )
```

```python
import functools

import jax
import jax.numpy as jnp
from jax import lax
from jax.experimental import pallas as pl
from jax.experimental.pallas import tpu as pltpu
from jax.sharding import PartitionSpec as P

SUBSTEPS = 2
INTERVALS = 2
EXCHANGE = 0.5
OCEAN_SHARE = 0.3

F32 = jnp.float32
BF16 = jnp.bfloat16
VMEM = pl.BlockSpec(memory_space=pltpu.VMEM)
HBM = pl.BlockSpec(memory_space=pltpu.HBM)
PARAMS = pltpu.CompilerParams(vmem_limit_bytes=40 * 1024 * 1024)


MEMBERS = 3
SUBLANES = 8
BAND = 8


def partner_pairs(groups, tiles, member):
    air_count = MEMBERS * groups // 4
    pairs = []
    for group in range(groups):
        ocean = group >= air_count
        if ocean:
            partner = MEMBERS * (group - air_count) + member
        else:
            partner = air_count + group // MEMBERS if group % MEMBERS == member else group
        for tile in range(tiles):
            other = tile ^ 1 if partner == group else tile
            pairs.append((group * tiles + tile, partner * tiles + other))
    return pairs


def inner_pairs(count):
    return [(tile, tile ^ 1) for tile in range(count)]


def outer_pairs(count):
    return [(tile, (tile + 1) % count if tile % 2 else (tile - 1) % count) for tile in range(count)]


def split_high_low(value):
    high = value.astype(BF16)
    low = (value - high.astype(F32)).astype(BF16)
    return high, low


def products(handed, picked_by, weight, blk_ref):
    rows, width = handed.shape
    block = blk_ref.shape[1]
    per_row = width // block
    for c in range(per_row):
        blk_ref[pl.ds(c, rows, stride=per_row), :] = handed[:, c * block : (c + 1) * block]
    blocks = blk_ref[: rows * per_row, :].astype(BF16)
    even = blocks.astype(F32)
    turned = [blocks] + [pltpu.roll(even, block - j, 1).astype(BF16) for j in range(1, BAND)]
    picked = picked_by(jnp.concatenate(turned, axis=1))
    total = weight(0) * picked[:, :block]
    for j in range(1, BAND):
        total = total + weight(j) * picked[:, j * block : (j + 1) * block]
    return total


def column(row):
    n = row.shape[1]
    diagonal = lax.broadcasted_iota(jnp.int32, (n, n), 0) == lax.broadcasted_iota(jnp.int32, (n, n), 1)
    return jnp.sum(jnp.where(diagonal, row, 0.0), axis=1, keepdims=True)


def is_odd():
    return lax.rem(lax.axis_index("tile"), 2) == 1


def is_sea(groups):
    return lax.axis_index("comp") >= MEMBERS * groups // 4


def halves_of(rows):
    half = len(rows) // 2
    head, tail = rows[:half], rows[half:]
    inner = [jnp.where(is_odd(), h, t) for h, t in zip(head, tail)]
    outer = [jnp.where(is_odd(), t, h) for h, t in zip(head, tail)]
    return inner, outer


def rows_of(inner, outer):
    head = [jnp.where(is_odd(), i, o) for i, o in zip(inner, outer)]
    tail = [jnp.where(is_odd(), o, i) for i, o in zip(inner, outer)]
    return head + tail


def lines_of(lines):
    return [lines[r : r + 1] for r in range(lines.shape[0])]


def copy_all(pairs, sems):
    copies = [pltpu.make_async_copy(src, dst, sems.at[n]) for n, (src, dst) in enumerate(pairs)]
    for copy in copies:
        copy.start()
    return copies


def load_kernel(groups, state, sources, targets, coupling, weights, *refs):
    x1, x2, surface, pick, chosen, targets_v, coupling_v, weights_v, state_v, sources_v, sems = refs
    copies = copy_all(
        (
            (state, state_v),
            (sources, sources_v),
            (targets, targets_v),
            (coupling, coupling_v),
            (weights, weights_v),
        ),
        sems,
    )
    copies[1].wait()
    copies[2].wait()
    count, margins = pick.shape
    slot = lax.broadcasted_iota(jnp.int32, (count, margins), 0)
    pick[...] = (slot == sources_v[...]).astype(F32).astype(BF16)
    me = lax.axis_index("comp")
    air_count = MEMBERS * groups // 4
    for n in range(MEMBERS):
        ocean = jnp.where(lax.rem(me, MEMBERS) == n, air_count + lax.div(me, MEMBERS), me)
        partner = jnp.where(me < air_count, ocean, MEMBERS * (me - air_count) + n)
        hit = (targets_v[...] == slot + partner * count).astype(F32).astype(BF16)
        chosen[n * count : (n + 1) * count] = jnp.concatenate([hit, hit], axis=1)
    copies[0].wait()
    for ref, half in zip((x1, x2), halves_of([state_v[0, 1:, r, :] for r in range(state_v.shape[2])])):
        for i, value in enumerate(half):
            ref[:, i, :] = value
    surface[...] = state_v[0, 0]
    for copy in copies[3:]:
        copy.wait()


def all_fields(x, i):
    width = x.shape[2]
    if x.shape[0] % SUBLANES:
        cut = SUBLANES - 1
        top = jnp.concatenate([jnp.zeros((1, width), F32), x[:cut, i, :]], axis=0)
        return jnp.concatenate([top, x[cut:, i, :]], axis=0)
    return x[:, i, :]


def remap_kernel(coupling, weights, pick, chosen, wide, *refs):
    outs, blk = refs[:-1], refs[-1]
    count, margins = pick.shape
    wide[...] = weights[0].reshape(wide.shape).astype(F32)
    contrib = products(
        coupling[0],
        lambda blocks: lax.dot_general(
            pick[...], blocks, (((0,), (0,)), ((), ())), preferred_element_type=F32
        ),
        lambda j: wide[pl.ds(j, margins, stride=BAND), :],
        blk,
    )
    both = jnp.concatenate(split_high_low(contrib), axis=0)
    blocks = jnp.dot(chosen[...], both, preferred_element_type=F32)
    for n, out in enumerate(outs):
        out[...] = blocks[n * count : (n + 1) * count]


def sort_kernel(groups, targets, wide, pick, *refs):
    args, refs = refs[:5], refs[5:]
    wide_out, pick_out, mask, codes, wet, coef, table, col0, mixing, courant, matrices, sems = refs
    copies = copy_all(tuple(zip(args, (mask, codes, mixing, courant, matrices))), sems)
    count, margins = pick.shape
    me = lax.axis_index("comp")
    air_count = MEMBERS * groups // 4
    first = jnp.where(is_sea(groups), MEMBERS * (me - air_count), air_count + lax.div(me, MEMBERS))
    place = targets[...] - first * count
    here = lax.broadcasted_iota(jnp.int32, (margins, margins), 0)
    there = lax.broadcasted_iota(jnp.int32, (margins, margins), 1)
    level = place.astype(F32)
    same = jnp.logical_and(column(level) == level, here < there)
    rank = jnp.sum(jnp.where(same, 1.0, 0.0), axis=0, keepdims=True).astype(jnp.int32)
    place = place + jnp.where(is_sea(groups), 0, rank * count)
    order = (here == place).astype(F32).astype(BF16)
    pick_out[...] = lax.dot_general(
        order, pick[...], (((1,), (1,)), ((), ())), preferred_element_type=F32
    ).astype(BF16)
    for j in range(BAND):
        band = wide[pl.ds(j, margins, stride=BAND), :].astype(BF16)
        wide_out[j] = jnp.dot(order, band, preferred_element_type=F32)
    for copy in copies:
        copy.wait()
    wet[...] = jnp.where(is_sea(groups), mask[0].astype(F32), 1.0)
    m, c = column(mixing[...]), column(courant[...])
    coef[0], coef[1], coef[2] = 1.0 - 4.0 * m - c, m + c, m
    branches, fields = matrices.shape[1:3]
    flat = matrices[0].reshape(branches * fields, fields)
    col0[...] = flat[:, :1].reshape(branches, fields, 1)
    flat = jnp.where(lax.broadcasted_iota(jnp.int32, flat.shape, 1) == 0, 0.0, flat)
    high, low = split_high_low(flat)
    table[...] = jnp.concatenate([high, high, low], axis=1)


def surface_kernel(groups, *refs):
    recs, refs = refs[:MEMBERS], refs[MEMBERS:]
    surface_ref, mask_ref, _, ns_ref, flux_ref, *ends, blk = refs
    rows, width = ns_ref.shape
    block = blk.shape[-1]
    per_row = width // block
    total = recs[0][...]
    for rec in recs[1:]:
        total = total + rec[...]
    blk[: total.shape[0], :] = total
    received = jnp.concatenate(
        [blk[pl.ds(c, rows, stride=per_row), :] for c in range(per_row)], axis=1
    )
    surface = surface_ref[...]
    flux = mask_ref[0].astype(F32) * EXCHANGE * (received - surface)
    new = surface + jnp.where(is_sea(groups), -OCEAN_SHARE * received, flux)
    ns_ref[...] = new
    flux_ref[...] = flux
    for ref, half in zip(ends, halves_of([new[: rows // 2], new[rows // 2 :]])):
        ref[...] = half[0]


def substep(f, up, down, c0, cu, m):
    width = f.shape[1]
    sides = pltpu.roll(f, 1, 1) + pltpu.roll(f, width - 1, 1)
    return c0 * f + cu * up + m * (down + sides)


def sides(f):
    return pltpu.roll(f, 1, 1) + pltpu.roll(f, f.shape[1] - 1, 1)


def own_rows(f0, f1, f2, f3, coef, base1, base2):
    c0, cu, m = coef[0], coef[1], coef[2]
    g0 = c0 * f0 + m * (f1 + sides(f0))
    g1 = substep(f1, f0, f2, c0, cu, m)
    g2 = substep(f2, f1, f3, c0, cu, m)
    g3 = c0 * f3 + cu * f2 + m * sides(f3)
    rows = [
        c0 * g0 + m * (g1 + sides(g0)) + (cu * m) * f0,
        substep(g1, g0, g2, c0, cu, m),
        substep(g2, g1, g3, c0, cu, m),
        c0 * g3 + cu * g2 + m * sides(g3) + (cu * m) * f3,
    ]
    for ref, half in zip((base1, base2), halves_of(rows)):
        for i, value in enumerate(half):
            ref[i] = value


def start_kernel(x1, x2, coef, col0, codes, wet, base1, base2, gain1, gain2, gain0):
    inner, outer = ([all_fields(x, i) for i in range(x.shape[1])] for x in (x1, x2))
    own_rows(*rows_of(inner, outer), coef, base1, base2)
    shape = gain1.shape[1:]
    rows = [
        branch_factor(col0, code, shape) * line
        for code, line in zip(lines_of(codes[0]), lines_of(wet[...]))
    ]
    for ref, half in zip((gain1, gain2), halves_of(rows)):
        for i, value in enumerate(half):
            ref[i] = value
    for r, value in enumerate(rows):
        gain0[r : r + 1, :] = value[:1]


def evolve_kernel(part1, part2, gain1, gain2, ns, e2, e1, coef, base1, base2, squashed):
    squashed[...] = jnp.tanh(field0_rows(ns, e2[...], e1[...], coef))
    half, fields, _ = gain1.shape
    line1, line2 = halves_of([squashed[r : r + 1, :] for r in range(half, 3 * half)])
    inner = [part1[:fields, i, :] + gain1[i] * line1[i] for i in range(half)]
    outer = [part2[:fields, i, :] + gain2[i] * line2[i] for i in range(half)]
    own_rows(*rows_of(inner, outer), coef, base1, base2)


def branch_factor(col0, code, shape):
    factor = jnp.broadcast_to(col0[0], shape)
    for b in range(1, col0.shape[0]):
        factor = jnp.where(code == b, col0[b], factor)
    return factor


def fields_kernel(inner, late, base, y, after, coef, table, codes, wet, *refs):
    part, part0 = refs[-2:] if inner else refs[-3:-1]
    if not inner:
        none = jnp.zeros((SUBSTEPS, base.shape[2]), F32)
        refs[-1][...] = field0_rows(after, none, none, coef)
    col0, squashed = refs[:2] if late else (None, None)
    half, fields, width = base.shape
    at_top = is_odd() if inner else jnp.logical_not(is_odd())
    c0, cu, m = coef[0], coef[1], coef[2]
    q = jnp.where(at_top, cu, m)
    branches = table.shape[0] // fields

    def halo_row(top, bottom):
        if not late:
            return jnp.where(at_top, all_fields(y, top), all_fields(y, bottom))
        value = jnp.where(at_top, y[:fields, top, :], y[:fields, bottom, :])
        code = jnp.where(at_top, y[fields:, top, :], y[fields:, bottom, :]).astype(jnp.int32)
        line = jnp.where(
            at_top, squashed[top : top + 1, :], squashed[3 * half + bottom : 3 * half + bottom + 1, :]
        )
        return value + branch_factor(col0, code, (fields, width)) * (value[:1] * line)

    near, far = halo_row(1, 0), halo_row(0, 1)
    edge = (2.0 * q * c0) * near + (2.0 * q * m) * sides(near) + (q * q) * far
    next_to_edge = (q * q) * near
    halos = jnp.where(at_top, edge, next_to_edge), jnp.where(at_top, next_to_edge, edge)
    code_lines = halves_of([codes[0, r : r + 1, :] for r in range(2 * half)])[0 if inner else 1]
    wet_lines = halves_of([wet[r : r + 1, :] for r in range(2 * half)])[0 if inner else 1]
    top_field = lax.broadcasted_iota(jnp.int32, (fields, width), 0) == 0
    for i in range(half):
        f = base[i] + halos[i]
        high, low = split_high_low(jnp.tanh(f))
        terms = jnp.dot(
            table[...], jnp.concatenate([high, low, high], axis=0), preferred_element_type=F32
        )
        tendency = terms[:fields]
        for b in range(1, branches):
            chosen = code_lines[i] == b
            tendency = jnp.where(chosen, terms[b * fields : (b + 1) * fields], tendency)
        part0[i : i + 1, :] = tendency[:1] * wet_lines[i]
        if late:
            part[i] = (f + tendency) * wet_lines[i]
        else:
            part[:fields, i, :] = jnp.where(top_field, 1.0, f + tendency) * wet_lines[i]
            part[fields:, i, :] = code_lines[i].astype(F32)


def field0_rows(ns, e2, e1, coef):
    c0, cu, m = coef[0, :1], coef[1, :1], coef[2, :1]
    odd = is_odd()
    f = jnp.concatenate([jnp.where(odd, e1, e2), ns[...], jnp.where(odd, e2, e1)], axis=0)
    rows = f.shape[0]
    for _ in range(SUBSTEPS):
        f = substep(f, pltpu.roll(f, 1, 0), pltpu.roll(f, rows - 1, 0), c0, cu, m)
    return f[SUBSTEPS : rows - SUBSTEPS]


def field0(own, e2, e1, coef, wet, part01, part02, gain0):
    odd = is_odd()
    rows = own.shape[0]
    end = e1.shape[0]
    pick = lambda even, other, at: jnp.where(odd, other[at : at + 1, :], even[at : at + 1, :])
    near = jnp.concatenate([pick(e2, e1, end - 1), pick(e1, e2, 0)], axis=0)
    far = jnp.concatenate([pick(e2, e1, end - 2), pick(e1, e2, 1)], axis=0)
    c0, cu, m = coef[0, :1], coef[1, :1], coef[2, :1]
    q = jnp.concatenate([cu, m], axis=0)
    edge = (2.0 * q * c0) * near + (2.0 * q * m) * sides(near) + (q * q) * far
    inside = (q * q) * near
    f = own[...] + jnp.concatenate([edge[:1], inside, edge[1:]], axis=0)
    squashed = jnp.tanh(f)
    part = jnp.concatenate(rows_of([part01[...]], [part02[...]]), axis=0)
    return part + gain0[...] * squashed + f * wet[...], squashed


def hand_kernel(
    groups, own, e2, e1, coef, wet, part01, part02, gain0, flux, wide, pick, *refs
):
    surf, *outs, blk = refs
    surf[...], _ = field0(own, e2, e1, coef, wet, part01, part02, gain0)
    sea = is_sea(groups)
    contrib = products(
        jnp.where(sea, surf[...], flux[...]),
        lambda blocks: jnp.dot(pick[...], blocks, preferred_element_type=F32),
        lambda j: wide[j],
        blk,
    )
    count = outs[0].shape[0]
    thirds = [contrib[n * count : (n + 1) * count] for n in range(MEMBERS)]
    member = lax.rem(lax.axis_index("comp"), MEMBERS)
    for n, (out, third) in enumerate(zip(outs, thirds)):
        out[...] = jnp.where(sea, third, jnp.where(member == n, sum(thirds), 0.0))


def close_kernel(
    groups, own, e2, e1, coef, wet, part01, part02, gain0, flux, gain1, gain2, part1, part2, *refs
):
    new_state, new_coupling, surf, squashed, stage, handed, sems = refs
    surf[...], squashed[...] = field0(own, e2, e1, coef, wet, part01, part02, gain0)
    handed[0] = jnp.where(is_sea(groups), surf[...], flux[...])
    copies = [pltpu.make_async_copy(handed, new_coupling, sems.at[0])]
    copies[0].start()
    half, fields, width = gain1.shape
    top_field = lax.broadcasted_iota(jnp.int32, (SUBLANES, width), 0) == 0
    line1, line2 = halves_of([squashed[r : r + 1, :] for r in range(2 * half)])
    for h in reversed(range(0, fields, SUBLANES)):
        some = slice(h, h + SUBLANES)
        for i in range(half):
            inner = part1[i, some] + gain1[i, some] * line1[i]
            outer = part2[i, some] + gain2[i, some] * line2[i]
            for r, done in zip((i, half + i), rows_of([inner], [outer])):
                if h == 0:
                    done = jnp.where(top_field, surf[r : r + 1, :], done)
                stage[0, some, r, :] = done
        window = pl.ds(h, SUBLANES)
        copies.append(
            pltpu.make_async_copy(
                stage.at[:, window], new_state.at[:, window], sems.at[len(copies)]
            )
        )
        copies[-1].start()
    for copy in copies:
        copy.wait()


def call(kernel, name, outs, args, scratch=(), in_specs=None, out_specs=None, flops=0):
    moved = sum(a.size * a.dtype.itemsize for a in list(args) + list(outs))
    return pl.pallas_call(
        kernel,
        name=name,
        out_shape=outs,
        in_specs=in_specs or [VMEM] * len(args),
        out_specs=out_specs or [VMEM] * len(outs),
        scratch_shapes=list(scratch),
        compiler_params=PARAMS,
        cost_estimate=pl.CostEstimate(flops=flops, bytes_accessed=moved, transcendentals=0),
    )(*args)


def fields_half(late, parts, kept, inner, base, y, after, *rest):
    return call(
        functools.partial(fields_kernel, inner, late),
        "inner" if inner else "outer",
        parts[:2] if inner else parts,
        (base, y, after, *kept, *rest),
        flops=0 if inner else 4_000_000_000,
    )


def on_device(
    state, coupling, land_mask, codes, mixing, courant, matrices, weights, sources, targets
):
    groups = lax.axis_size("comp")
    tiles = lax.axis_size("tile")
    _, fields, rows, width = state.shape
    _, margins, band, block = weights.shape
    count = rows * width // block
    half = rows // 2
    branches = matrices.shape[1]
    shape = jax.ShapeDtypeStruct

    halves = [shape((half, fields, width), F32)] * 2
    payloads = [shape((count, block), F32)] * MEMBERS
    blocks = pltpu.VMEM((max(SUBLANES // rows, 1) * count, block), F32)
    line, pair = shape((rows, width), F32), shape((half, width), F32)
    far = lambda args: [pltpu.with_memory_space_constraint(a, pltpu.HBM) for a in args]
    like = lambda args: [shape(a.shape, a.dtype) for a in args]
    room = lambda args: [pltpu.VMEM(a.shape, a.dtype) for a in args]
    x1, x2, surface, pick, chosen, targets, handed, raw = call(
        functools.partial(load_kernel, groups),
        "load",
        [shape((fields - 1, half, width), F32)] * 2
        + [line, shape((count, margins), BF16), shape((MEMBERS * count, 2 * margins), BF16)]
        + like((targets, coupling, weights)),
        far((state, sources, targets, coupling, weights)),
        room((state, sources)) + [pltpu.SemaphoreType.DMA((5,))],
        [HBM] * 5,
    )
    wide, *sent = call(
        remap_kernel,
        "remap",
        [shape((margins * band, block), F32)] + payloads,
        (handed, raw, pick, chosen),
        [blocks],
    )
    wide, pick, mask, codes, wet, coef, table, col0 = call(
        functools.partial(sort_kernel, groups),
        "sort",
        [shape((band, margins, block), F32), shape((margins, count), BF16)]
        + like((land_mask, codes))
        + [
            line,
            shape((3, fields, 1), F32),
            shape((branches * fields, 3 * fields), BF16),
            shape((branches, fields, 1), F32),
        ],
        (targets, wide, pick, *far((land_mask, codes, mixing, courant, matrices))),
        room((mixing, courant, matrices)) + [pltpu.SemaphoreType.DMA((5,))],
        [VMEM] * 3 + [HBM] * 5,
    )
    for interval in range(INTERVALS):
        y1 = lax.ppermute(x1, "tile", inner_pairs(tiles))
        y2 = lax.ppermute(x2, "tile", outer_pairs(tiles))
        recs = [
            lax.ppermute(value, ("comp", "tile"), partner_pairs(groups, tiles, member))
            for member, value in enumerate(sent)
        ]
        late, last = interval > 0, interval == INTERVALS - 1
        if late:
            base1, base2, squashed = call(
                evolve_kernel,
                "evolve",
                halves + [shape((2 * rows, width), F32)],
                (part1, part2, gain1, gain2, ns, e2, e1, coef),
            )
        else:
            base1, base2, gain1, gain2, gain0 = call(
                start_kernel, "start", halves * 2 + [line], (x1, x2, coef, col0, codes, wet)
            )
        kept = (coef, table, codes, wet)
        parts = [halves[0] if late else shape((fields + 1, half, width), F32), pair, line]
        run_fields = functools.partial(fields_half, late, parts, kept)
        ns, flux, *edges = call(
            functools.partial(surface_kernel, groups),
            "surface",
            [line] * 2 + ([pair] * 2 if last else []),
            (*(recs[1:] + recs[:1] if last else recs), surface, mask, pick),
            [blocks],
        )
        d1, d2 = edges if last else (ns, ns)
        e1 = lax.ppermute(d1, "tile", inner_pairs(tiles))
        e2 = lax.ppermute(d2, "tile", outer_pairs(tiles))
        if late:
            part2, part02, own = run_fields(False, base2, y2, ns, col0, squashed)
            part1, part01 = run_fields(True, base1, y1, part02, col0, squashed)
        else:
            part2, part02, own = run_fields(False, base2, y2, ns)
            part1, part01 = run_fields(True, base1, y1, part02)
        x1, x2 = part1, part2
        common = (own, e2, e1, coef, wet, part01, part02, gain0, flux)
        if not last:
            surface, *sent = call(
                functools.partial(hand_kernel, groups),
                "hand",
                [line] + payloads,
                (*common, wide, pick),
                [blocks],
                flops=20_000_000_000,
            )
        else:
            new_state, new_coupling = call(
                functools.partial(close_kernel, groups),
                "close",
                [shape(state.shape, F32), shape(coupling.shape, F32)],
                (*common, gain1, gain2, part1, part2),
                [pltpu.VMEM((rows, width), F32)] * 2
                + [
                    pltpu.VMEM(state.shape, F32),
                    pltpu.VMEM(coupling.shape, F32),
                    pltpu.SemaphoreType.DMA((1 + fields // SUBLANES,)),
                ],
                out_specs=[HBM] * 2,
            )
    return new_state, new_coupling


def solution(mesh):
    placed = (
        P("comp", None, "tile", None),
        P("comp", "tile", None),
        P("comp", "tile", None),
        P("comp", "tile", None),
        P("comp", None),
        P("comp", None),
        P("comp", None, None, None),
        P("comp", "tile", None, None),
        P("comp", "tile"),
        P("comp", "tile"),
    )
    return jax.shard_map(
        on_device,
        mesh=mesh,
        in_specs=placed,
        out_specs=(P("comp", None, "tile", None), P("comp", "tile", None)),
        check_vma=False,
    )
```

```python
import functools

import jax
import jax.numpy as jnp
from jax import lax
from jax.experimental import pallas as pl
from jax.experimental.pallas import tpu as pltpu
from jax.sharding import PartitionSpec as P

SUBSTEPS = 2
INTERVALS = 2
EXCHANGE = 0.5
OCEAN_SHARE = 0.3

F32 = jnp.float32
BF16 = jnp.bfloat16
VMEM = pl.BlockSpec(memory_space=pltpu.VMEM)
HBM = pl.BlockSpec(memory_space=pltpu.HBM)
PARAMS = pltpu.CompilerParams(vmem_limit_bytes=40 * 1024 * 1024)


MEMBERS = 3
SUBLANES = 8
BAND = 8


def partner_pairs(groups, tiles, member):
    air_count = MEMBERS * groups // 4
    pairs = []
    for group in range(groups):
        ocean = group >= air_count
        if ocean:
            partner = MEMBERS * (group - air_count) + member
        else:
            partner = air_count + group // MEMBERS if group % MEMBERS == member else group
        for tile in range(tiles):
            other = tile ^ 1 if partner == group else tile
            pairs.append((group * tiles + tile, partner * tiles + other))
    return pairs


def inner_pairs(count):
    return [(tile, tile ^ 1) for tile in range(count)]


def outer_pairs(count):
    return [(tile, (tile + 1) % count if tile % 2 else (tile - 1) % count) for tile in range(count)]


def split_high_low(value):
    high = value.astype(BF16)
    low = (value - high.astype(F32)).astype(BF16)
    return high, low


def products(handed, picked_by, weight, blk_ref):
    rows, width = handed.shape
    block = blk_ref.shape[1]
    per_row = width // block
    for c in range(per_row):
        blk_ref[pl.ds(c, rows, stride=per_row), :] = handed[:, c * block : (c + 1) * block]
    blocks = blk_ref[: rows * per_row, :].astype(BF16)
    even = blocks.astype(F32)
    turned = [blocks] + [pltpu.roll(even, block - j, 1).astype(BF16) for j in range(1, BAND)]
    picked = picked_by(jnp.concatenate(turned, axis=1))
    total = weight(0) * picked[:, :block]
    for j in range(1, BAND):
        total = total + weight(j) * picked[:, j * block : (j + 1) * block]
    return total


def column(row):
    n = row.shape[1]
    diagonal = lax.broadcasted_iota(jnp.int32, (n, n), 0) == lax.broadcasted_iota(jnp.int32, (n, n), 1)
    return jnp.sum(jnp.where(diagonal, row, 0.0), axis=1, keepdims=True)


def is_odd():
    return lax.rem(lax.axis_index("tile"), 2) == 1


def is_sea(groups):
    return lax.axis_index("comp") >= MEMBERS * groups // 4


def halves_of(rows):
    half = len(rows) // 2
    head, tail = rows[:half], rows[half:]
    inner = [jnp.where(is_odd(), h, t) for h, t in zip(head, tail)]
    outer = [jnp.where(is_odd(), t, h) for h, t in zip(head, tail)]
    return inner, outer


def rows_of(inner, outer):
    head = [jnp.where(is_odd(), i, o) for i, o in zip(inner, outer)]
    tail = [jnp.where(is_odd(), o, i) for i, o in zip(inner, outer)]
    return head + tail


def lines_of(lines):
    return [lines[r : r + 1] for r in range(lines.shape[0])]


def copy_all(pairs, sems):
    copies = [pltpu.make_async_copy(src, dst, sems.at[n]) for n, (src, dst) in enumerate(pairs)]
    for copy in copies:
        copy.start()
    return copies


def load_kernel(groups, state, sources, targets, coupling, weights, *refs):
    x1, x2, surface, pick, chosen, targets_v, coupling_v, weights_v, state_v, sources_v, sems = refs
    copies = copy_all(
        (
            (sources, sources_v),
            (targets, targets_v),
            (state, state_v),
            (coupling, coupling_v),
            (weights, weights_v),
        ),
        sems,
    )
    copies[0].wait()
    copies[1].wait()
    count, margins = pick.shape
    slot = lax.broadcasted_iota(jnp.int32, (count, margins), 0)
    pick[...] = (slot == sources_v[...]).astype(F32).astype(BF16)
    me = lax.axis_index("comp")
    air_count = MEMBERS * groups // 4
    for n in range(MEMBERS):
        ocean = jnp.where(lax.rem(me, MEMBERS) == n, air_count + lax.div(me, MEMBERS), me)
        partner = jnp.where(me < air_count, ocean, MEMBERS * (me - air_count) + n)
        hit = (targets_v[...] == slot + partner * count).astype(F32).astype(BF16)
        chosen[n * count : (n + 1) * count] = jnp.concatenate([hit, hit], axis=1)
    copies[2].wait()
    for ref, half in zip((x1, x2), halves_of([state_v[0, 1:, r, :] for r in range(state_v.shape[2])])):
        for i, value in enumerate(half):
            ref[:, i, :] = value
    surface[...] = state_v[0, 0]
    for copy in copies[3:]:
        copy.wait()


def all_fields(x, i):
    width = x.shape[2]
    if x.shape[0] % SUBLANES:
        cut = SUBLANES - 1
        top = jnp.concatenate([jnp.zeros((1, width), F32), x[:cut, i, :]], axis=0)
        return jnp.concatenate([top, x[cut:, i, :]], axis=0)
    return x[:, i, :]


def remap_kernel(coupling, weights, pick, chosen, wide, *refs):
    outs, blk = refs[:-1], refs[-1]
    count, margins = pick.shape
    wide[...] = weights[0].reshape(wide.shape).astype(F32)
    contrib = products(
        coupling[0],
        lambda blocks: lax.dot_general(
            pick[...], blocks, (((0,), (0,)), ((), ())), preferred_element_type=F32
        ),
        lambda j: wide[pl.ds(j, margins, stride=BAND), :],
        blk,
    )
    both = jnp.concatenate(split_high_low(contrib), axis=0)
    blocks = jnp.dot(chosen[...], both, preferred_element_type=F32)
    for n, out in enumerate(outs):
        out[...] = blocks[n * count : (n + 1) * count]


def sort_kernel(groups, targets, wide, pick, *refs):
    args, refs = refs[:5], refs[5:]
    wide_out, pick_out, mask, codes, wet, coef, table, col0, mixing, courant, matrices, sems = refs
    copies = copy_all(tuple(zip(args, (mask, codes, mixing, courant, matrices))), sems)
    count, margins = pick.shape
    me = lax.axis_index("comp")
    air_count = MEMBERS * groups // 4
    first = jnp.where(is_sea(groups), MEMBERS * (me - air_count), air_count + lax.div(me, MEMBERS))
    place = targets[...] - first * count
    here = lax.broadcasted_iota(jnp.int32, (margins, margins), 0)
    there = lax.broadcasted_iota(jnp.int32, (margins, margins), 1)
    level = place.astype(F32)
    same = jnp.logical_and(column(level) == level, here < there)
    rank = jnp.sum(jnp.where(same, 1.0, 0.0), axis=0, keepdims=True).astype(jnp.int32)
    place = place + jnp.where(is_sea(groups), 0, rank * count)
    order = (here == place).astype(F32).astype(BF16)
    pick_out[...] = lax.dot_general(
        order, pick[...], (((1,), (1,)), ((), ())), preferred_element_type=F32
    ).astype(BF16)
    for j in range(BAND):
        band = wide[pl.ds(j, margins, stride=BAND), :].astype(BF16)
        wide_out[j] = jnp.dot(order, band, preferred_element_type=F32)
    for copy in copies:
        copy.wait()
    wet[...] = jnp.where(is_sea(groups), mask[0].astype(F32), 1.0)
    m, c = column(mixing[...]), column(courant[...])
    coef[0], coef[1], coef[2] = 1.0 - 4.0 * m - c, m + c, m
    branches, fields = matrices.shape[1:3]
    flat = matrices[0].reshape(branches * fields, fields)
    col0[...] = flat[:, :1].reshape(branches, fields, 1)
    flat = jnp.where(lax.broadcasted_iota(jnp.int32, flat.shape, 1) == 0, 0.0, flat)
    high, low = split_high_low(flat)
    table[...] = jnp.concatenate([high, high, low], axis=1)


def surface_kernel(groups, *refs):
    recs, refs = refs[:MEMBERS], refs[MEMBERS:]
    surface_ref, mask_ref, _, ns_ref, flux_ref, *ends, blk = refs
    rows, width = ns_ref.shape
    block = blk.shape[-1]
    per_row = width // block
    total = recs[0][...]
    for rec in recs[1:]:
        total = total + rec[...]
    blk[: total.shape[0], :] = total
    received = jnp.concatenate(
        [blk[pl.ds(c, rows, stride=per_row), :] for c in range(per_row)], axis=1
    )
    surface = surface_ref[...]
    flux = mask_ref[0].astype(F32) * EXCHANGE * (received - surface)
    new = surface + jnp.where(is_sea(groups), -OCEAN_SHARE * received, flux)
    ns_ref[...] = new
    flux_ref[...] = flux
    for ref, half in zip(ends, halves_of([new[: rows // 2], new[rows // 2 :]])):
        ref[...] = half[0]


def substep(f, up, down, c0, cu, m):
    width = f.shape[1]
    sides = pltpu.roll(f, 1, 1) + pltpu.roll(f, width - 1, 1)
    return c0 * f + cu * up + m * (down + sides)


def sides(f):
    return pltpu.roll(f, 1, 1) + pltpu.roll(f, f.shape[1] - 1, 1)


def own_rows(f0, f1, f2, f3, coef, base1, base2):
    c0, cu, m = coef[0], coef[1], coef[2]
    g0 = c0 * f0 + m * (f1 + sides(f0))
    g1 = substep(f1, f0, f2, c0, cu, m)
    g2 = substep(f2, f1, f3, c0, cu, m)
    g3 = c0 * f3 + cu * f2 + m * sides(f3)
    rows = [
        c0 * g0 + m * (g1 + sides(g0)) + (cu * m) * f0,
        substep(g1, g0, g2, c0, cu, m),
        substep(g2, g1, g3, c0, cu, m),
        c0 * g3 + cu * g2 + m * sides(g3) + (cu * m) * f3,
    ]
    for ref, half in zip((base1, base2), halves_of(rows)):
        for i, value in enumerate(half):
            ref[i] = value


def start_kernel(x1, x2, coef, col0, codes, wet, base1, base2, gain1, gain2, gain0):
    inner, outer = ([all_fields(x, i) for i in range(x.shape[1])] for x in (x1, x2))
    own_rows(*rows_of(inner, outer), coef, base1, base2)
    shape = gain1.shape[1:]
    rows = [
        branch_factor(col0, code, shape) * line
        for code, line in zip(lines_of(codes[0]), lines_of(wet[...]))
    ]
    for ref, half in zip((gain1, gain2), halves_of(rows)):
        for i, value in enumerate(half):
            ref[i] = value
    for r, value in enumerate(rows):
        gain0[r : r + 1, :] = value[:1]


def evolve_kernel(part1, part2, gain1, gain2, ns, e2, e1, coef, base1, base2, squashed):
    squashed[...] = jnp.tanh(field0_rows(ns, e2[...], e1[...], coef))
    half, fields, _ = gain1.shape
    line1, line2 = halves_of([squashed[r : r + 1, :] for r in range(half, 3 * half)])
    inner = [part1[:fields, i, :] + gain1[i] * line1[i] for i in range(half)]
    outer = [part2[:fields, i, :] + gain2[i] * line2[i] for i in range(half)]
    own_rows(*rows_of(inner, outer), coef, base1, base2)


def branch_factor(col0, code, shape):
    factor = jnp.broadcast_to(col0[0], shape)
    for b in range(1, col0.shape[0]):
        factor = jnp.where(code == b, col0[b], factor)
    return factor


def fields_kernel(inner, late, base, y, after, coef, table, codes, wet, *refs):
    part, part0 = refs[-2:] if inner else refs[-3:-1]
    if not inner:
        none = jnp.zeros((SUBSTEPS, base.shape[2]), F32)
        refs[-1][...] = field0_rows(after, none, none, coef)
    col0, squashed = refs[:2] if late else (None, None)
    half, fields, width = base.shape
    at_top = is_odd() if inner else jnp.logical_not(is_odd())
    c0, cu, m = coef[0], coef[1], coef[2]
    q = jnp.where(at_top, cu, m)
    branches = table.shape[0] // fields

    def halo_row(top, bottom):
        if not late:
            return jnp.where(at_top, all_fields(y, top), all_fields(y, bottom))
        value = jnp.where(at_top, y[:fields, top, :], y[:fields, bottom, :])
        code = jnp.where(at_top, y[fields:, top, :], y[fields:, bottom, :]).astype(jnp.int32)
        line = jnp.where(
            at_top, squashed[top : top + 1, :], squashed[3 * half + bottom : 3 * half + bottom + 1, :]
        )
        return value + branch_factor(col0, code, (fields, width)) * (value[:1] * line)

    near, far = halo_row(1, 0), halo_row(0, 1)
    edge = (2.0 * q * c0) * near + (2.0 * q * m) * sides(near) + (q * q) * far
    next_to_edge = (q * q) * near
    halos = jnp.where(at_top, edge, next_to_edge), jnp.where(at_top, next_to_edge, edge)
    code_lines = halves_of([codes[0, r : r + 1, :] for r in range(2 * half)])[0 if inner else 1]
    wet_lines = halves_of([wet[r : r + 1, :] for r in range(2 * half)])[0 if inner else 1]
    top_field = lax.broadcasted_iota(jnp.int32, (fields, width), 0) == 0
    for i in range(half):
        f = base[i] + halos[i]
        high, low = split_high_low(jnp.tanh(f))
        terms = jnp.dot(
            table[...], jnp.concatenate([high, low, high], axis=0), preferred_element_type=F32
        )
        tendency = terms[:fields]
        for b in range(1, branches):
            chosen = code_lines[i] == b
            tendency = jnp.where(chosen, terms[b * fields : (b + 1) * fields], tendency)
        part0[i : i + 1, :] = tendency[:1] * wet_lines[i]
        if late:
            part[i] = (f + tendency) * wet_lines[i]
        else:
            part[:fields, i, :] = jnp.where(top_field, 1.0, f + tendency) * wet_lines[i]
            part[fields:, i, :] = code_lines[i].astype(F32)


def field0_rows(ns, e2, e1, coef):
    c0, cu, m = coef[0, :1], coef[1, :1], coef[2, :1]
    odd = is_odd()
    f = jnp.concatenate([jnp.where(odd, e1, e2), ns[...], jnp.where(odd, e2, e1)], axis=0)
    rows = f.shape[0]
    for _ in range(SUBSTEPS):
        f = substep(f, pltpu.roll(f, 1, 0), pltpu.roll(f, rows - 1, 0), c0, cu, m)
    return f[SUBSTEPS : rows - SUBSTEPS]


def field0(own, e2, e1, coef, wet, part01, part02, gain0):
    odd = is_odd()
    rows = own.shape[0]
    end = e1.shape[0]
    pick = lambda even, other, at: jnp.where(odd, other[at : at + 1, :], even[at : at + 1, :])
    near = jnp.concatenate([pick(e2, e1, end - 1), pick(e1, e2, 0)], axis=0)
    far = jnp.concatenate([pick(e2, e1, end - 2), pick(e1, e2, 1)], axis=0)
    c0, cu, m = coef[0, :1], coef[1, :1], coef[2, :1]
    q = jnp.concatenate([cu, m], axis=0)
    edge = (2.0 * q * c0) * near + (2.0 * q * m) * sides(near) + (q * q) * far
    inside = (q * q) * near
    f = own[...] + jnp.concatenate([edge[:1], inside, edge[1:]], axis=0)
    squashed = jnp.tanh(f)
    part = jnp.concatenate(rows_of([part01[...]], [part02[...]]), axis=0)
    return part + gain0[...] * squashed + f * wet[...], squashed


def hand_kernel(
    groups, own, e2, e1, coef, wet, part01, part02, gain0, flux, wide, pick, *refs
):
    surf, *outs, blk = refs
    surf[...], _ = field0(own, e2, e1, coef, wet, part01, part02, gain0)
    sea = is_sea(groups)
    contrib = products(
        jnp.where(sea, surf[...], flux[...]),
        lambda blocks: jnp.dot(pick[...], blocks, preferred_element_type=F32),
        lambda j: wide[j],
        blk,
    )
    count = outs[0].shape[0]
    thirds = [contrib[n * count : (n + 1) * count] for n in range(MEMBERS)]
    member = lax.rem(lax.axis_index("comp"), MEMBERS)
    for n, (out, third) in enumerate(zip(outs, thirds)):
        out[...] = jnp.where(sea, third, jnp.where(member == n, sum(thirds), 0.0))


def close_kernel(
    groups, own, e2, e1, coef, wet, part01, part02, gain0, flux, gain1, gain2, part1, part2, *refs
):
    new_state, new_coupling, surf, squashed, stage, handed, sems = refs
    surf[...], squashed[...] = field0(own, e2, e1, coef, wet, part01, part02, gain0)
    handed[0] = jnp.where(is_sea(groups), surf[...], flux[...])
    copies = [pltpu.make_async_copy(handed, new_coupling, sems.at[0])]
    copies[0].start()
    half, fields, width = gain1.shape
    top_field = lax.broadcasted_iota(jnp.int32, (SUBLANES, width), 0) == 0
    line1, line2 = halves_of([squashed[r : r + 1, :] for r in range(2 * half)])
    for h in range(0, fields, SUBLANES):
        some = slice(h, h + SUBLANES)
        for i in range(half):
            inner = part1[i, some] + gain1[i, some] * line1[i]
            outer = part2[i, some] + gain2[i, some] * line2[i]
            for r, done in zip((i, half + i), rows_of([inner], [outer])):
                if h == 0:
                    done = jnp.where(top_field, surf[r : r + 1, :], done)
                stage[0, some, r, :] = done
        window = pl.ds(h, SUBLANES)
        copies.append(
            pltpu.make_async_copy(
                stage.at[:, window], new_state.at[:, window], sems.at[len(copies)]
            )
        )
        copies[-1].start()
    for copy in copies:
        copy.wait()


def call(kernel, name, outs, args, scratch=(), in_specs=None, out_specs=None, flops=0):
    moved = sum(a.size * a.dtype.itemsize for a in list(args) + list(outs))
    return pl.pallas_call(
        kernel,
        name=name,
        out_shape=outs,
        in_specs=in_specs or [VMEM] * len(args),
        out_specs=out_specs or [VMEM] * len(outs),
        scratch_shapes=list(scratch),
        compiler_params=PARAMS,
        cost_estimate=pl.CostEstimate(flops=flops, bytes_accessed=moved, transcendentals=0),
    )(*args)


def fields_half(late, parts, kept, inner, base, y, after, *rest):
    return call(
        functools.partial(fields_kernel, inner, late),
        "inner" if inner else "outer",
        parts[:2] if inner else parts,
        (base, y, after, *kept, *rest),
        flops=0 if inner else 4_000_000_000,
    )


def on_device(
    state, coupling, land_mask, codes, mixing, courant, matrices, weights, sources, targets
):
    groups = lax.axis_size("comp")
    tiles = lax.axis_size("tile")
    _, fields, rows, width = state.shape
    _, margins, band, block = weights.shape
    count = rows * width // block
    half = rows // 2
    branches = matrices.shape[1]
    shape = jax.ShapeDtypeStruct

    halves = [shape((half, fields, width), F32)] * 2
    payloads = [shape((count, block), F32)] * MEMBERS
    blocks = pltpu.VMEM((max(SUBLANES // rows, 1) * count, block), F32)
    line, pair = shape((rows, width), F32), shape((half, width), F32)
    far = lambda args: [pltpu.with_memory_space_constraint(a, pltpu.HBM) for a in args]
    like = lambda args: [shape(a.shape, a.dtype) for a in args]
    room = lambda args: [pltpu.VMEM(a.shape, a.dtype) for a in args]
    x1, x2, surface, pick, chosen, targets, handed, raw = call(
        functools.partial(load_kernel, groups),
        "load",
        [shape((fields - 1, half, width), F32)] * 2
        + [line, shape((count, margins), BF16), shape((MEMBERS * count, 2 * margins), BF16)]
        + like((targets, coupling, weights)),
        far((state, sources, targets, coupling, weights)),
        room((state, sources)) + [pltpu.SemaphoreType.DMA((5,))],
        [HBM] * 5,
    )
    wide, *sent = call(
        remap_kernel,
        "remap",
        [shape((margins * band, block), F32)] + payloads,
        (handed, raw, pick, chosen),
        [blocks],
    )
    wide, pick, mask, codes, wet, coef, table, col0 = call(
        functools.partial(sort_kernel, groups),
        "sort",
        [shape((band, margins, block), F32), shape((margins, count), BF16)]
        + like((land_mask, codes))
        + [
            line,
            shape((3, fields, 1), F32),
            shape((branches * fields, 3 * fields), BF16),
            shape((branches, fields, 1), F32),
        ],
        (targets, wide, pick, *far((land_mask, codes, mixing, courant, matrices))),
        room((mixing, courant, matrices)) + [pltpu.SemaphoreType.DMA((5,))],
        [VMEM] * 3 + [HBM] * 5,
    )
    for interval in range(INTERVALS):
        y1 = lax.ppermute(x1, "tile", inner_pairs(tiles))
        y2 = lax.ppermute(x2, "tile", outer_pairs(tiles))
        recs = [
            lax.ppermute(value, ("comp", "tile"), partner_pairs(groups, tiles, member))
            for member, value in enumerate(sent)
        ]
        late, last = interval > 0, interval == INTERVALS - 1
        if late:
            base1, base2, squashed = call(
                evolve_kernel,
                "evolve",
                halves + [shape((2 * rows, width), F32)],
                (part1, part2, gain1, gain2, ns, e2, e1, coef),
            )
        else:
            base1, base2, gain1, gain2, gain0 = call(
                start_kernel, "start", halves * 2 + [line], (x1, x2, coef, col0, codes, wet)
            )
        kept = (coef, table, codes, wet)
        parts = [halves[0] if late else shape((fields + 1, half, width), F32), pair, line]
        run_fields = functools.partial(fields_half, late, parts, kept)
        ns, flux, *edges = call(
            functools.partial(surface_kernel, groups),
            "surface",
            [line] * 2 + ([pair] * 2 if last else []),
            (*(recs[1:] + recs[:1] if last else recs), surface, mask, pick),
            [blocks],
        )
        d1, d2 = edges if last else (ns, ns)
        e1 = lax.ppermute(d1, "tile", inner_pairs(tiles))
        e2 = lax.ppermute(d2, "tile", outer_pairs(tiles))
        if late:
            part2, part02, own = run_fields(False, base2, y2, ns, col0, squashed)
            part1, part01 = run_fields(True, base1, y1, part02, col0, squashed)
        else:
            part2, part02, own = run_fields(False, base2, y2, ns)
            part1, part01 = run_fields(True, base1, y1, part02)
        x1, x2 = part1, part2
        common = (own, e2, e1, coef, wet, part01, part02, gain0, flux)
        if not last:
            surface, *sent = call(
                functools.partial(hand_kernel, groups),
                "hand",
                [line] + payloads,
                (*common, wide, pick),
                [blocks],
                flops=20_000_000_000,
            )
        else:
            new_state, new_coupling = call(
                functools.partial(close_kernel, groups),
                "close",
                [shape(state.shape, F32), shape(coupling.shape, F32)],
                (*common, gain1, gain2, part1, part2),
                [pltpu.VMEM((rows, width), F32)] * 2
                + [
                    pltpu.VMEM(state.shape, F32),
                    pltpu.VMEM(coupling.shape, F32),
                    pltpu.SemaphoreType.DMA((1 + fields // SUBLANES,)),
                ],
                out_specs=[HBM] * 2,
            )
    return new_state, new_coupling


def solution(mesh):
    placed = (
        P("comp", None, "tile", None),
        P("comp", "tile", None),
        P("comp", "tile", None),
        P("comp", "tile", None),
        P("comp", None),
        P("comp", None),
        P("comp", None, None, None),
        P("comp", "tile", None, None),
        P("comp", "tile"),
        P("comp", "tile"),
    )
    return jax.shard_map(
        on_device,
        mesh=mesh,
        in_specs=placed,
        out_specs=(P("comp", None, "tile", None), P("comp", "tile", None)),
        check_vma=False,
    )
```
